256 devices in a mesh: gx: 16 (over x, y), gy: 16 (over z, core).
Axes of the slice: x: 4, y: 4, z: 8, core: 2. Of those that a mesh axis runs over, the one named last changes fastest.
Arguments:
- right_side: float32 [256, 512, 128], P('gx', 'gy'), may hold values from -8 to 8
- kappa: float32 [256, 512, 128], P('gx', 'gy'), may hold values from 0.5 to 5
- owners: int32 [16, 16], replicated, may hold values from 240 to 255, as said below
Outputs:
- solution_field: float32 [256, 512, 128], P('gx', 'gy')
- residual: float32 [256, 512, 128], P('gx', 'gy')
The draws below stay inside these ranges and needn't reach their ends.
Inputs may be any that keep to these rules, and one draw needn't show every extreme that they name: Each agglomerate holds all tiles of 1 to 4 neighbouring tile columns (tiles sharing their second index), with widths drawn from the seed; owners[i, j] is the largest flat index i' * 16 + j' of a tile (i', j') in the agglomerate of tile (i, j).
All inputs are finite; a program needn't handle non-finite values.
Results may differ from the reference program's by a relative error of at most 0.0003.
Values sent between devices are 32-bit elements; how exact they have to be, the bound alone decides.
No kernel may reach another device: no remote copies, remote signals or barrier semaphores. Data moves between devices by JAX's collectives and lax.ppermute only.
A program may use at most 128 MiB of HBM per device.

```python
import math
import jax
import jax.numpy as jnp

CX = 16
CY = 32
CZ = 128
SWEEPS = 3
COARSE_STEPS = 24
AGGLOM = 4
NX = 256
NY = 512
TILES_X = 16
TILES_Y = 16


def draw_owners(key, part):
    key = jax.random.fold_in(key, 11)
    widths = jax.random.randint(key, (TILES_Y,), 1, AGGLOM + 1).astype(jnp.int32)
    ends = jnp.cumsum(widths).astype(jnp.int32) - 1
    columns = jnp.arange(TILES_Y, dtype=jnp.int32)
    large_value = jnp.int32(TILES_Y + AGGLOM + 8)
    candidate = jnp.where(ends[None, :] >= columns[:, None], ends[None, :], large_value)
    last_column = jnp.minimum(jnp.min(candidate, axis=1), TILES_Y - 1).astype(jnp.int32)
    rows = jnp.zeros((TILES_X, 1), jnp.int32)
    return (rows + (TILES_X - 1) * TILES_Y + last_column[None, :]).astype(jnp.int32)


def draw_right_side(key, part):
    key = jax.random.fold_in(key, 23)
    phases = jax.random.uniform(jax.random.fold_in(key, 1), (2,), jnp.float32, 0.0, 2.0 * math.pi)
    waves = jax.random.randint(jax.random.fold_in(key, 2), (2,), 1, 3).astype(jnp.float32)
    pos_x = (jnp.arange(NX, dtype=jnp.float32) + 0.5) / NX
    pos_y = (jnp.arange(NY, dtype=jnp.float32) + 0.5) / NY
    wave_x = jnp.cos(2.0 * math.pi * waves[0] * pos_x + phases[0])
    wave_y = jnp.cos(2.0 * math.pi * waves[1] * pos_y + phases[1])
    shape_xy = wave_x[:, None] * wave_y[None, :]
    rough_key = jax.random.fold_in(key, 3)
    smooth = 1.2 + 0.8 * shape_xy
    rough = jnp.clip(jax.random.normal(rough_key, (NX, NY, CZ), jnp.float32), -5.0, 5.0)
    return (rough + smooth[:, :, None]).astype(jnp.float32)


def block_scale(rng, dims, shards, least, high):
    factor_of = 1.0
    for axis_at, blocks in shards:
        heights = jax.random.uniform(jax.random.fold_in(jax.random.fold_in(rng, 6), axis_at), (blocks,), jnp.float32, least / len(shards), high / len(shards))
        factor_of = factor_of * jnp.repeat(jnp.exp(heights), dims[axis_at] // blocks).reshape((-1,) + (1,) * (len(dims) - 1 - axis_at))
    return factor_of


def setup_inputs(seed: int = 0) -> dict:
    seeds = jax.random.split(jax.random.key(seed), 4)
    return {
        "right_side": draw_right_side(jax.random.fold_in(seeds[3], 71), 0),
        "kappa": jnp.clip(jnp.exp(math.log(5.0) - 2.3025851 * jax.random.uniform(seeds[1], (NX, NY, CZ), jnp.float32) ** block_scale(seeds[1], (NX, NY, CZ), ((0, 16), (1, 16)), -0.2, 0.2)), 0.5, 5.0),
        "owners": draw_owners(jax.random.fold_in(seeds[3], 71), 0),
    }


SIGMA = 0.02
HIGH_BOUND = 2.0
LOW_SMOOTH = 0.3
LOW_COARSE = 0.05


def neighbours(padded):
    return (padded[:-2, 1:-1, 1:-1], padded[2:, 1:-1, 1:-1],
            padded[1:-1, :-2, 1:-1], padded[1:-1, 2:, 1:-1],
            padded[1:-1, 1:-1, :-2], padded[1:-1, 1:-1, 2:])


def build_level(coeff, scale):
    near = neighbours(jnp.pad(coeff, 1))
    faces = tuple(scale * 0.5 * (coeff + other) for other in near)
    diagonal = faces[0] + faces[1] + faces[2] + faces[3] + faces[4] + faces[5] + SIGMA * scale
    return faces, diagonal


def apply_op(field, faces, diagonal):
    near = neighbours(jnp.pad(field, 1))
    total = faces[0] * near[0] + faces[1] * near[1]
    total = total + faces[2] * near[2] + faces[3] * near[3]
    total = total + faces[4] * near[4] + faces[5] * near[5]
    return diagonal * field - total


def coarsen(field):
    sizex, sizey, sizez = field.shape
    blocks = field.reshape(sizex // 2, 2, sizey // 2, 2, sizez // 2, 2)
    return jnp.sum(blocks, axis=(1, 3, 5)) * 0.125


def refine(field):
    return jnp.repeat(jnp.repeat(jnp.repeat(field, 2, 0), 2, 1), 2, 2)


def mask_faces(faces, owners, factor_x, factor_y):
    owned = jnp.repeat(jnp.repeat(owners, factor_x, 0), factor_y, 1)
    edged = jnp.pad(owned, 1, constant_values=-1)
    left = (owned == edged[:-2, 1:-1]).astype(jnp.float32)[:, :, None]
    right = (owned == edged[2:, 1:-1]).astype(jnp.float32)[:, :, None]
    below = (owned == edged[1:-1, :-2]).astype(jnp.float32)[:, :, None]
    above = (owned == edged[1:-1, 2:]).astype(jnp.float32)[:, :, None]
    return (faces[0] * left, faces[1] * right, faces[2] * below, faces[3] * above, faces[4], faces[5])


def chebyshev(field, source, faces, diagonal, degree, lower):
    centre = 0.5 * (HIGH_BOUND + lower)
    half_width = 0.5 * (HIGH_BOUND - lower)
    sharp = centre / half_width
    if field is None:
        remain = source
    else:
        remain = source - apply_op(field, faces, diagonal)
    update = (remain / diagonal) * (1.0 / centre)
    field = update if field is None else field + update
    ratio = 1.0 / sharp
    for sweep in range(degree - 1):
        remain = source - apply_op(field, faces, diagonal)
        ratio_next = 1.0 / (2.0 * sharp - ratio)
        update = (ratio_next * ratio) * update + (2.0 * ratio_next / half_width) * (remain / diagonal)
        field = field + update
        ratio = ratio_next
    return field


def vcycle(level, source, levels):
    faces, diagonal = levels[level]
    if level == 4:
        return chebyshev(None, source, faces, diagonal, COARSE_STEPS, LOW_COARSE)
    field = chebyshev(None, source, faces, diagonal, SWEEPS, LOW_SMOOTH)
    remain = source - apply_op(field, faces, diagonal)
    correction = vcycle(level + 1, coarsen(remain), levels)
    field = field + refine(correction)
    return chebyshev(field, source, faces, diagonal, SWEEPS, LOW_SMOOTH)


def reference(right_side, kappa, owners):
    levels = []
    coeff = kappa
    for level in range(5):
        faces, diagonal = build_level(coeff, 0.25 ** level)
        if level == 4:
            faces = mask_faces(faces, owners, CX // 16, CY // 16)
        levels.append((faces, diagonal))
        if level < 4:
            coeff = coarsen(coeff)
    field = vcycle(0, right_side, levels)
    remain = right_side - apply_op(field, levels[0][0], levels[0][1])
    field = field + vcycle(0, remain, levels)
    remain = right_side - apply_op(field, levels[0][0], levels[0][1])
    return field, remain
```

```python
import functools

import jax
import jax.numpy as jnp
import numpy as np
from jax import lax
from jax.experimental import pallas as pl
from jax.experimental.pallas import tpu as pltpu
from jax.sharding import PartitionSpec as P

SIGMA = 0.02
F32 = jnp.float32
BF16 = jnp.bfloat16
TX, TY = 16, 32
HX = 10
HY = 12
PX, RY = TX + 2 * HX, TY + 2 * HY
UX, UR = TX + 10, TY + 16
VMEM_BYTES = 56 * 1024 * 1024


def cheb_steps(degree, lower):
    centre = 0.5 * (2.0 + lower)
    half = 0.5 * (2.0 - lower)
    sharp = centre / half
    ratio = 1.0 / sharp
    steps = []
    for _ in range(degree - 1):
        nxt = 1.0 / (2.0 * sharp - ratio)
        steps.append((nxt * ratio, 2.0 * nxt / half))
        ratio = nxt
    return 1.0 / centre, steps


SMOOTH = cheb_steps(3, 0.3)
COARSE = cheb_steps(24, 0.05)


def lane_map(z):
    groups = 128 // z
    out = np.zeros((4, 128, 128), np.float32)
    for q in range(4):
        for lane in range(128):
            cell = (lane // z + groups * q) // 2
            out[q, lane, cell * (z // 2) + (lane % z) // 2] = 1.0
    return out


def restrict_map(z):
    return jnp.asarray(lane_map(z).reshape(512, 128), BF16)


def prolong_map(z):
    return jnp.asarray(np.concatenate([m.T for m in lane_map(z)], axis=1), BF16)


def pair_dot(value, matrix):
    high = value.astype(BF16)
    rest = value - high.astype(F32)
    mid = rest.astype(BF16)
    low = (rest - mid.astype(F32)).astype(BF16)
    dot = functools.partial(jnp.dot, preferred_element_type=F32)
    return dot(high, matrix) + (dot(mid, matrix) + dot(low, matrix))


def lanes(shape):
    return lax.broadcasted_iota(jnp.int32, shape, len(shape) - 1)


def turn(value, shift, axis):
    return pltpu.roll(value, shift % value.shape[axis], axis)


def next_x(v, z):
    if z == 128:
        return jnp.concatenate([v[1:], v[:1]], axis=0)
    a = turn(v, -z, 2)
    b = jnp.concatenate([a[1:], a[:1]], axis=0)
    return jnp.where(lanes(v.shape) < 128 - z, a, b)


def prev_x(v, z):
    if z == 128:
        return jnp.concatenate([v[-1:], v[:-1]], axis=0)
    a = turn(v, z, 2)
    b = jnp.concatenate([a[-1:], a[:-1]], axis=0)
    return jnp.where(lanes(v.shape) >= z, a, b)


def faces_of(k, step, scale, low, high):
    own = (0.5 * scale) * k
    both = own + (0.5 * scale) * step
    if low is None:
        return both, None
    edge = jnp.where(low | high, own, 0.0)
    return jnp.where(high, 0.0, both), edge


def build(k, scale, z, inside=None, edge_x=(None, None), edge_y=(None, None)):
    shape = k.shape
    cell = lanes(shape) & (z - 1)
    wx, ex = faces_of(k, next_x(k, z), scale, *edge_x)
    wy, ey = faces_of(k, turn(k, -1, 1), scale, *edge_y)
    wz, ez = faces_of(k, turn(k, -1, 2), scale, cell == 0, cell == z - 1)
    s = ez + SIGMA * scale
    if ex is not None:
        s = s + ex
    if ey is not None:
        s = s + ey
    diagonal = s + wx + prev_x(wx, z) + wy + turn(wy, 1, 1) + wz + turn(wz, 1, 2)
    rd = 1.0 / diagonal
    if inside is not None:
        rd = jnp.where(inside, rd, 0.0)
    return wx, wy, wz, s, rd


def remain(v, b, level, z):
    wx, wy, wz, s, _ = level
    fx = wx * (next_x(v, z) - v)
    fy = wy * (turn(v, -1, 1) - v)
    fz = wz * (turn(v, -1, 2) - v)
    total = (fx - prev_x(fx, z)) + (fy - turn(fy, 1, 1)) + (fz - turn(fz, 1, 2))
    return (b - s * v) + total


def smooth(x, b, level, z):
    first, steps = SMOOTH
    rd = level[4]
    if x is None:
        d = (b * rd) * first
        x = d
    else:
        d = (remain(x, b, level, z) * rd) * first
        x = x + d
    for keep, gain in steps:
        d = keep * d + gain * (remain(x, b, level, z) * rd)
        x = x + d
    return x


def within(shape, first_x, first_y, z, size_x, size_y):
    plane = lax.broadcasted_iota(jnp.int32, shape, 0)
    cx = first_x + plane * (128 // z) + lanes(shape) // z
    cy = first_y + lax.broadcasted_iota(jnp.int32, shape, 1)
    return (cx >= 0) & (cx < size_x) & (cy >= 0) & (cy < size_y)


def pair_rows(ref, plane, start, count):
    return ref[plane, pl.ds(start, count, stride=2), :] + ref[plane, pl.ds(start + 1, count, stride=2), :]


def spread_rows(ref, plane, start, value):
    count = value.shape[0]
    ref[plane, pl.ds(start, count, stride=2), :] = value
    ref[plane, pl.ds(start + 1, count, stride=2), :] = value


def build_top(k_ref, wx, wy, wz, s, rd, planes, inside_at, body):
    rows = k_ref.shape[1]
    shape = (rows, 128)
    lane = lanes(shape)

    def step(p, carry):
        k, wxp = carry
        kn = k_ref[jnp.minimum(p + 1, planes - 1)]
        own = 0.5 * k
        fx = 0.5 * kn + own
        fy = turn(own, -1, 0) + own
        fz = jnp.where(lane == 127, 0.0, turn(own, -1, 1) + own)
        sv = SIGMA + jnp.where((lane == 0) | (lane == 127), own, 0.0)
        diagonal = sv + (fx + wxp) + (fy + turn(fy, 1, 0)) + (fz + turn(fz, 1, 1))
        rdv = jnp.where(inside_at(p), 1.0 / diagonal, 0.0)
        wx[p], wy[p], wz[p], s[p], rd[p] = fx, fy, fz, sv, rdv
        body(p, rdv)
        return kn, fx

    lax.fori_loop(0, planes, step, (k_ref[0], jnp.zeros(shape, F32)))


def sweep_top(x, wx, wy, wz, s, low, high, body):
    v0 = x[low]
    fx0 = wx[low - 1] * (v0 - x[low - 1])

    def step(p, carry):
        v, fxp = carry
        vn = x[p + 1]
        fx = wx[p] * (vn - v)
        fy = wy[p] * (turn(v, -1, 0) - v)
        fz = wz[p] * (turn(v, -1, 1) - v)
        total = (fx - fxp) + (fy - turn(fy, 1, 0)) + (fz - turn(fz, 1, 1))
        body(p, v, s[p] * v - total)
        return vn, fx

    lax.fori_loop(low, high, step, (v0, fx0))


def fill_top(dst, tile, left, right, below, above):
    dst[:, 0:2, :] = jnp.zeros((PX, 2, 128), F32)
    dst[:, RY - 2 : RY, :] = jnp.zeros((PX, 2, 128), F32)
    dst[0:HX, HY : HY + TY, :] = left
    dst[HX : HX + TX, HY : HY + TY, :] = tile
    dst[HX + TX :, HY : HY + TY, :] = right
    dst[:, 2:HY, :] = below
    dst[:, HY + TY : RY - 2, :] = above


def down_kernel(first, pos, tile, left, right, below, above, *refs):
    if first:
        ktile, r0, r1, xup, bup, kup, kx, one, two = refs[:9]
        scratch = refs[9:]
    else:
        kx, r0, r1, xup, bup, one, two = refs[:7]
        scratch = refs[7:]
    bx, wx, wy, wz, s, rd, d, x, rs, b1s, x1s, k1s = scratch
    gx, gy = pos[0], pos[1]
    row = lax.broadcasted_iota(jnp.int32, (RY, 128), 0) + (gy * TY - HY)
    row_in = (row >= 0) & (row < 512)

    def inside_at(p):
        at = gx * TX - HX + p
        return row_in & ((at >= 0) & (at < 256))

    fill_top(bx, tile[...], left[0], right[0], below[0], above[0])
    if first:
        fill_top(kx, ktile[...], left[1], right[1], below[1], above[1])

        def clear(p, _):
            kx[p] = jnp.where(inside_at(p), kx[p], 0.0)
            return 0

        lax.fori_loop(0, PX, clear, 0)

    start, steps = SMOOTH

    def begin(p, rdv):
        v = (bx[p] * rdv) * start
        d[p] = v
        x[p] = v

    build_top(kx, wx, wy, wz, s, rd, PX, inside_at, begin)
    for number, (keep, gain) in enumerate(steps):

        def advance(p, v, av):
            dv = keep * d[p] + gain * ((bx[p] - av) * rd[p])
            d[p] = dv
            x[p] = v + dv

        sweep_top(x, wx, wy, wz, s, 2 + number, PX - 2 - number, advance)

    def residual(p, v, av):
        d[p] = bx[p] - av

    sweep_top(x, wx, wy, wz, s, 4, PX - 4, residual)
    xup[...] = x[5 : 5 + UX, 4 : 4 + UR, :]
    bup[...] = bx[5 : 5 + UX, 4 : 4 + UR, :]
    if first:
        kup[...] = kx[5 : 5 + UX, 4 : 4 + UR, :]

    def coarse(src):
        for c in range(16):
            rs[c] = src[2 + 2 * c] + src[3 + 2 * c]
        flat = [
            jnp.concatenate([pair_rows(rs, 2 * c, 4, 24), pair_rows(rs, 2 * c + 1, 4, 24)], axis=1)
            for c in range(8)
        ]
        return (0.125 * pair_dot(jnp.concatenate(flat, axis=0), r0[...])).reshape(8, 24, 128)

    d[2] = jnp.zeros((RY, 128), F32)
    d[3] = jnp.zeros((RY, 128), F32)
    d[PX - 4] = jnp.zeros((RY, 128), F32)
    d[PX - 3] = jnp.zeros((RY, 128), F32)
    b1 = coarse(d)
    k1 = coarse(kx)
    level = build(k1, 0.25, 64, within(k1.shape, gx * 8 - 4, gy * 16 - 4, 64, 128, 256))
    x1 = smooth(None, b1, level, 64)
    res = remain(x1, b1, level, 64)
    b1s[...] = b1
    x1s[...] = x1
    k1s[...] = k1
    one[0] = b1s[2:6, 4:20, :]
    one[1] = x1s[2:6, 4:20, :]
    if first:
        one[2] = k1s[2:6, 4:20, :]
    b1s[...] = res

    def coarse_tile(src):
        return jnp.concatenate([pair_rows(src, 2 + q, 4, 8) for q in range(4)], axis=1)

    flat = [coarse_tile(b1s)]
    if first:
        flat.append(coarse_tile(k1s))
    out = 0.125 * pair_dot(jnp.concatenate(flat, axis=0), r1[...])
    two[...] = out.reshape(len(flat), 8, 128)


def call(kernel, outs, scratch, *args, flops=1e7):
    specs = [pl.BlockSpec(memory_space=pltpu.SMEM)]
    specs += [pl.BlockSpec(memory_space=pltpu.VMEM)] * (len(args) - 1)
    return pl.pallas_call(
        kernel,
        out_shape=[jax.ShapeDtypeStruct(o, F32) for o in outs],
        in_specs=specs,
        out_specs=[pl.BlockSpec(memory_space=pltpu.VMEM)] * len(outs),
        scratch_shapes=[pltpu.VMEM(o, F32) for o in scratch],
        compiler_params=pltpu.CompilerParams(vmem_limit_bytes=VMEM_BYTES),
        cost_estimate=pl.CostEstimate(flops=int(flops), bytes_accessed=8 << 20, transcendentals=0),
    )(*args)


def go_down(first, pos, tile, left, right, below, above, kappa, r0, r1):
    top, up = (PX, RY, 128), (UX, UR, 128)
    outs = [up, up] + ([up, top] if first else []) + [(3 if first else 2, 4, 16, 128), (2 if first else 1, 8, 128)]
    scratch = [top] * 8 + [(16, RY, 128)] + [(8, 24, 128)] * 3
    kernel = functools.partial(down_kernel, first)
    return call(kernel, outs, scratch, pos, tile, left, right, below, above, kappa, r0, r1)


def mid_kernel(first, pos, mid, below, above, *refs):
    if first:
        r2, near, three, k2 = refs[:4]
        scratch = refs[4:]
    else:
        k2, r2, near, three = refs[:4]
        scratch = refs[4:]
    hold, rs, cs = scratch
    gx, gy = pos[0], pos[1]
    skip = below.shape[0] - mid.shape[0]
    shape = (16, 24, 128)
    inside = within(shape, 0, gy * 8 - 8, 32, 64, 128)

    def rows(dst, at):
        dst[:, 0:8, :] = below[skip + at : skip + at + 16]
        dst[:, 8:16, :] = mid[at : at + 16]
        dst[:, 16:24, :] = above[skip + at : skip + at + 16]

    rows(rs, 0)
    b = rs[...]
    if first:
        rows(k2, 16)
        k2[...] = jnp.where(inside, k2[...], 0.0)
    k = k2[...]
    plane = lax.broadcasted_iota(jnp.int32, shape, 0)
    lane = lanes(shape)
    edge_x = ((plane == 0) & (lane < 32), (plane == 15) & (lane >= 96))
    level = build(k, 0.25**2, 32, inside, edge_x)
    x = smooth(None, b, level, 32)
    rs[...] = remain(x, b, level, 32)
    for number, value in enumerate((b, x) + level):
        hold[number] = value
    for i in range(5):
        at = gx - 2 + i
        ok = (at >= 0) & (at < 16)
        from_plane = jnp.clip(at, 0, 15)
        for number in range(7):
            near[number, i] = jnp.where(ok, hold[number, from_plane], 0.0)

    def coarse(src, out):
        flat = [
            jnp.concatenate([pair_rows(src, 4 * c + q, 4, 8) for q in range(4)], axis=1) for c in range(4)
        ]
        cs[...] = (0.125 * pair_dot(jnp.concatenate(flat, axis=0), r2[...])).reshape(4, 8, 128)
        for c in range(4):
            three[out + c // 2, 4 * (c % 2) : 4 * (c % 2) + 4, :] = cs[c, 2:6, :]

    coarse(rs, 0)
    if first:
        coarse(k2, 2)


def go_mid(first, pos, mid, below, above, k2, r2):
    outs = [(7, 5, 24, 128), (4 if first else 2, 8, 128)] + ([(16, 24, 128)] if first else [])
    scratch = [(7, 16, 24, 128), (16, 24, 128), (4, 8, 128)]
    args = (mid, below, above) + (() if first else (k2,)) + (r2,)
    return call(functools.partial(mid_kernel, first), outs, scratch, pos, *args)


def solve_last(b, k, owned):
    shape = k.shape
    scale = 0.25**4
    lane = lanes(shape)
    row = lax.broadcasted_iota(jnp.int32, shape, 0)
    moves = (
        (8, 1, lane < 8, True),
        (-8, 1, lane >= 120, True),
        (1, 0, row == 0, True),
        (-1, 0, row == 31, True),
        (1, 1, (lane & 7) == 0, False),
        (-1, 1, (lane & 7) == 7, False),
    )
    diagonal = jnp.full(shape, SIGMA * scale, F32)
    pulls = []
    for shift, axis, edge, masked in moves:
        weight = (0.5 * scale) * (k + jnp.where(edge, 0.0, turn(k, shift, axis)))
        diagonal = diagonal + weight
        keep = jnp.where(edge, 0.0, weight)
        if masked:
            keep = jnp.where(owned == turn(owned, shift, axis), keep, 0.0)
        pulls.append(keep)
    rd = 1.0 / diagonal
    pulls = [keep * rd for keep in pulls]
    g = b * rd
    first, steps = COARSE
    d = g * first
    x = d
    for keep, gain in steps:
        total = [pull * turn(x, move[0], move[1]) for pull, move in zip(pulls, moves)]
        near = (total[0] + total[1]) + (total[2] + total[3]) + (total[4] + total[5])
        d = keep * d + gain * ((g - x) + near)
        x = x + d
    return x


def up_kernel(first, pos, owned, b3g, k3g, near, one, left, right, below, above, x0, b0, k0, *refs):
    if first:
        r3, t3, t2, t1, t0, xout, rout, k1 = refs[:8]
        scratch = refs[8:]
    else:
        k1, xbefore, borig, r3, t3, t2, t1, t0, xout, rout = refs[:10]
        scratch = refs[10:]
    b3, k3, s3, e2, s2, b1s, s1, e0, wx, wy, wz, s, rd, d, x = scratch
    gx, gy = pos[0], pos[1]

    for g in range(16):
        for c in range(4):
            part = slice(4 * (c % 2), 4 * (c % 2) + 4)
            b3[c, 4 * g : 4 * g + 4, :] = b3g[g, c // 2, part, :]
            k3[c, 4 * g : 4 * g + 4, :] = k3g[g, c // 2, part, :]
    shape = (4, 64, 128)
    plane = lax.broadcasted_iota(jnp.int32, shape, 0)
    rown = lax.broadcasted_iota(jnp.int32, shape, 1)
    lane = lanes(shape)
    level = build(
        k3[...],
        0.25**3,
        16,
        None,
        ((plane == 0) & (lane < 16), (plane == 3) & (lane >= 112)),
        (rown == 0, rown == 63),
    )
    b = b3[...]
    x3 = smooth(None, b, level, 16)
    s3[...] = remain(x3, b, level, 16)

    flat = [
        jnp.concatenate([pair_rows(src, q, 0, 32) for q in range(4)], axis=1) for src in (s3, k3)
    ]
    fine = 0.125 * pair_dot(jnp.concatenate(flat, axis=0), r3[...])
    x4 = solve_last(fine[:32], fine[32:], owned[...])

    back = pair_dot(x4, t3[...])
    for q in range(4):
        spread_rows(s3, q, 0, back[:, 128 * q : 128 * q + 128])
    s3[...] = smooth(x3 + s3[...], b, level, 16)

    for i in range(5):
        at = jnp.clip(gx - 2 + i, 0, 15)
        back = pair_dot(s3[at // 4], t2[at % 4])
        spread_rows(e2, i, 8, back)
    e = e2[:, pl.ds(pl.multiple_of(gy * 8, 8), 24), :]
    level = tuple(near[number] for number in range(2, 7))
    x2 = near[1] + jnp.where(level[4] > 0.0, e, 0.0)
    s2[...] = smooth(x2, near[0], level, 32)

    shape = (12, 32, 128)
    inside = within(shape, gx * 8 - 8, gy * 16 - 8, 64, 128, 256)

    def fill(dst, number):
        dst[0:4, 8:24, :] = left[number]
        dst[4:8, 8:24, :] = one[number]
        dst[8:12, 8:24, :] = right[number]
        dst[:, 0:8, :] = below[12 * number : 12 * number + 12]
        dst[:, 24:32, :] = above[12 * number : 12 * number + 12]

    fill(b1s, 0)
    fill(s1, 1)
    x1 = jnp.where(inside, s1[...], 0.0)
    if first:
        fill(k1, 2)
        k1[...] = jnp.where(inside, k1[...], 0.0)
    flat = jnp.concatenate([s2[i, 4:20, :] for i in range(1, 4)], axis=0)
    back = pair_dot(flat, t1[...])
    for i in range(3):
        for q in range(4):
            spread_rows(s1, 4 * i + q, 0, back[16 * i : 16 * i + 16, 128 * q : 128 * q + 128])
    level = build(k1[...], 0.25, 64, inside)
    x1 = x1 + jnp.where(inside, s1[...], 0.0)
    s1[...] = smooth(x1, b1s[...], level, 64)

    flat = jnp.concatenate([s1[i, 4:28, :] for i in range(3, 9)], axis=0)
    back = pair_dot(flat, t0[...])
    for i in range(6):
        for q in range(2):
            spread_rows(e0, 2 * i + q, 0, back[24 * i : 24 * i + 24, 128 * q : 128 * q + 128])
    row = lax.broadcasted_iota(jnp.int32, (UR, 128), 0) + (gy * TY - 8)
    row_in = (row >= 0) & (row < 512)

    def inside_at(p):
        at = gx * TX - 5 + p
        return row_in & ((at >= 0) & (at < 256))

    def begin(p, rdv):
        correction = e0[jnp.clip((p - 1) // 2, 0, 11)]
        x[p] = x0[p] + jnp.where(rdv > 0.0, correction, 0.0)

    build_top(k0, wx, wy, wz, s, rd, UX, inside_at, begin)
    start, steps = SMOOTH

    def open_up(p, v, av):
        dv = ((b0[p] - av) * rd[p]) * start
        d[p] = dv
        x[p] = v + dv

    sweep_top(x, wx, wy, wz, s, 2, UX - 2, open_up)
    for number, (keep, gain) in enumerate(steps):

        def advance(p, v, av):
            dv = keep * d[p] + gain * ((b0[p] - av) * rd[p])
            d[p] = dv
            x[p] = v + dv

        sweep_top(x, wx, wy, wz, s, 3 + number, UX - 3 - number, advance)

    if first:
        xout[...] = x[4 : UX - 4]

        def residual(p, v, av):
            rout[p - 5] = b0[p, 8 : 8 + TY, :] - av[8 : 8 + TY]
    else:

        def add(p, _):
            x[p] = x[p] + xbefore[p - 4]
            return 0

        lax.fori_loop(4, UX - 4, add, 0)

        def residual(p, v, av):
            xout[p - 5] = v[8 : 8 + TY]
            rout[p - 5] = borig[p - 5] - av[8 : 8 + TY]

    sweep_top(x, wx, wy, wz, s, 5, UX - 5, residual)


def go_up(first, *args):
    tile = (TX, TY, 128)
    outs = [(TX + 2, UR, 128), tile, (12, 32, 128)] if first else [tile, tile]
    up = (UX, UR, 128)
    scratch = [(4, 64, 128)] * 3 + [(5, 144, 128), (5, 24, 128), (12, 32, 128), (12, 32, 128), (12, UR, 128)]
    return call(functools.partial(up_kernel, first), outs, scratch + [up] * 7, *args)


def shift(value, axis, step):
    count = lax.axis_size(axis)
    return lax.ppermute(value, axis, [(i, (i + step) % count) for i in range(count)])


def gather(value, axis):
    count = lax.axis_size(axis)
    return lax.all_to_all(jnp.broadcast_to(value[None], (count,) + value.shape), axis, 0, 0, tiled=True)


def local(right_side, kappa, owners):
    pos = jnp.stack([lax.axis_index("gx"), lax.axis_index("gy")]).astype(jnp.int32)
    owned = jnp.repeat(jnp.repeat(owners.T, 2, 0), 8, 1).astype(F32)
    r0 = restrict_map(128)[128:384]
    r1, r2, r3 = restrict_map(64), restrict_map(32), restrict_map(16)
    t0 = prolong_map(128)[:, 128:384]
    t1, t3 = prolong_map(64), prolong_map(16)
    t2 = jnp.asarray(np.transpose(lane_map(32), (0, 2, 1)), BF16)

    source = right_side
    keep = {}
    for first in (True, False):
        mid = jnp.stack([source, kappa]) if first else source[None]
        left = shift(mid[:, TX - HX :], "gx", 1)
        right = shift(mid[:, :HX], "gx", -1)
        wide = jnp.concatenate([left, mid, right], axis=1)
        below = shift(wide[:, :, TY - HX :], "gy", 1)
        above = shift(wide[:, :, :HX], "gy", -1)
        out = go_down(first, pos, source, left, right, below, above, kappa if first else keep["kx"], r0, r1)
        if first:
            xup, bup, keep["kup"], keep["kx"], one, two = out
        else:
            xup, bup, one, two = out
        left = shift(one, "gx", 1)
        right = shift(one, "gx", -1)
        rows = jnp.swapaxes(gather(two, "gx"), 0, 1).reshape(-1, 8, 128)
        wide = jnp.concatenate([left, one, right], axis=1)
        low = wide[:, :, :8].reshape(-1, 8, 128)
        high = wide[:, :, 8:].reshape(-1, 8, 128)
        below = shift(jnp.concatenate([high, rows]), "gy", 1)
        above = shift(jnp.concatenate([low, rows]), "gy", -1)
        out = go_mid(first, pos, rows, below, above, keep.get("k2"), r2)
        if first:
            near, three, keep["k2"] = out
        else:
            near, three = out
        spread = gather(three, "gy")
        if first:
            keep["k3"] = spread[:, 2:]
            spread = spread[:, :2]
        args = (pos, owned, spread, keep["k3"], near, one, left, right, below, above, xup, bup, keep["kup"])
        if first:
            keep["x"], source, keep["k1"] = go_up(True, *args, r3, t3, t2, t1, t0)
        else:
            field, residual = go_up(False, *args, keep["k1"], keep["x"], right_side, r3, t3, t2, t1, t0)
    return field, residual


def solution(mesh):
    spec = P("gx", "gy", None)
    return jax.shard_map(
        local, mesh=mesh, in_specs=(spec, spec, P()), out_specs=(spec, spec), check_vma=False
    )
```

```python
import functools

import jax
import jax.numpy as jnp
import numpy as np
from jax import lax
from jax.experimental import pallas as pl
from jax.experimental.pallas import tpu as pltpu
from jax.sharding import PartitionSpec as P

SIGMA = 0.02
F32 = jnp.float32
BF16 = jnp.bfloat16
TX, TY = 16, 32
HX = 10
HY = 12
PX, RY = TX + 2 * HX, TY + 2 * HY
UX, UR = TX + 12, TY + 16
CHUNK = 4
VMEM_BYTES = 56 * 1024 * 1024


def cheb_steps(degree, lower):
    centre = 0.5 * (2.0 + lower)
    half = 0.5 * (2.0 - lower)
    sharp = centre / half
    ratio = 1.0 / sharp
    steps = []
    for _ in range(degree - 1):
        nxt = 1.0 / (2.0 * sharp - ratio)
        steps.append((nxt * ratio, 2.0 * nxt / half))
        ratio = nxt
    return 1.0 / centre, steps


SMOOTH = cheb_steps(3, 0.3)
COARSE = cheb_steps(24, 0.05)


def lane_map(z):
    groups = 128 // z
    out = np.zeros((4, 128, 128), np.float32)
    for q in range(4):
        for lane in range(128):
            cell = (lane // z + groups * q) // 2
            out[q, lane, cell * (z // 2) + (lane % z) // 2] = 1.0
    return out


def restrict_map(z):
    return jnp.asarray(lane_map(z).reshape(512, 128), BF16)


def prolong_map(z):
    return jnp.asarray(np.concatenate([m.T for m in lane_map(z)], axis=1), BF16)


def pair_dot(value, matrix):
    high = value.astype(BF16)
    rest = value - high.astype(F32)
    mid = rest.astype(BF16)
    low = (rest - mid.astype(F32)).astype(BF16)
    dot = functools.partial(jnp.dot, preferred_element_type=F32)
    return dot(high, matrix) + (dot(mid, matrix) + dot(low, matrix))


def lanes(shape):
    return lax.broadcasted_iota(jnp.int32, shape, len(shape) - 1)


def turn(value, shift, axis):
    return pltpu.roll(value, shift % value.shape[axis], axis)


def next_x(v, z):
    if z == 128:
        return jnp.concatenate([v[1:], v[:1]], axis=0)
    a = turn(v, -z, 2)
    b = jnp.concatenate([a[1:], a[:1]], axis=0)
    return jnp.where(lanes(v.shape) < 128 - z, a, b)


def prev_x(v, z):
    if z == 128:
        return jnp.concatenate([v[-1:], v[:-1]], axis=0)
    a = turn(v, z, 2)
    b = jnp.concatenate([a[-1:], a[:-1]], axis=0)
    return jnp.where(lanes(v.shape) >= z, a, b)


def faces_of(k, step, scale, low, high):
    own = (0.5 * scale) * k
    both = own + (0.5 * scale) * step
    if low is None:
        return both, None
    edge = jnp.where(low | high, own, 0.0)
    return jnp.where(high, 0.0, both), edge


def build(k, scale, z, inside=None, edge_x=(None, None), edge_y=(None, None)):
    shape = k.shape
    cell = lanes(shape) & (z - 1)
    wx, ex = faces_of(k, next_x(k, z), scale, *edge_x)
    wy, ey = faces_of(k, turn(k, -1, 1), scale, *edge_y)
    wz, ez = faces_of(k, turn(k, -1, 2), scale, cell == 0, cell == z - 1)
    s = ez + SIGMA * scale
    if ex is not None:
        s = s + ex
    if ey is not None:
        s = s + ey
    diagonal = s + wx + prev_x(wx, z) + wy + turn(wy, 1, 1) + wz + turn(wz, 1, 2)
    rd = 1.0 / diagonal
    if inside is not None:
        rd = jnp.where(inside, rd, 0.0)
    return wx, wy, wz, s, rd


def remain(v, b, level, z):
    wx, wy, wz, s, _ = level
    fx = wx * (next_x(v, z) - v)
    fy = wy * (turn(v, -1, 1) - v)
    fz = wz * (turn(v, -1, 2) - v)
    total = (fx - prev_x(fx, z)) + (fy - turn(fy, 1, 1)) + (fz - turn(fz, 1, 2))
    return (b - s * v) + total


def smooth(x, b, level, z):
    first, steps = SMOOTH
    rd = level[4]
    if x is None:
        d = (b * rd) * first
        x = d
    else:
        d = (remain(x, b, level, z) * rd) * first
        x = x + d
    for keep, gain in steps:
        d = keep * d + gain * (remain(x, b, level, z) * rd)
        x = x + d
    return x


def within(shape, first_x, first_y, z, size_x, size_y):
    plane = lax.broadcasted_iota(jnp.int32, shape, 0)
    cx = first_x + plane * (128 // z) + lanes(shape) // z
    cy = first_y + lax.broadcasted_iota(jnp.int32, shape, 1)
    return (cx >= 0) & (cx < size_x) & (cy >= 0) & (cy < size_y)


def pair_rows(ref, plane, start, count):
    return ref[plane, pl.ds(start, count, stride=2), :] + ref[plane, pl.ds(start + 1, count, stride=2), :]


def spread_rows(ref, plane, start, value):
    count = value.shape[0]
    ref[plane, pl.ds(start, count, stride=2), :] = value
    ref[plane, pl.ds(start + 1, count, stride=2), :] = value


def insider(rows, first_x, first_y):
    row = lax.broadcasted_iota(jnp.int32, (CHUNK, rows, 128), 1) + first_y
    row_in = (row >= 0) & (row < 512)
    plane = lax.broadcasted_iota(jnp.int32, (CHUNK, rows, 128), 0) + first_x
    return lambda p: row_in & (plane >= -p) & (plane < 256 - p)


def build_top(k_ref, wx, wy, wz, s, rd, planes, inside_at, body):
    rows = k_ref.shape[1]
    shape = (CHUNK, rows, 128)
    lane = lanes(shape)

    def step(i, wxp):
        p = i * CHUNK
        k = k_ref[pl.ds(p, CHUNK)]
        kn = jnp.concatenate([k[1:], k_ref[pl.ds(jnp.minimum(p + CHUNK, planes - 1), 1)]], axis=0)
        own = 0.5 * k
        fx = 0.5 * kn + own
        fy = turn(own, -1, 1) + own
        fz = jnp.where(lane == 127, 0.0, turn(own, -1, 2) + own)
        sv = SIGMA + jnp.where((lane == 0) | (lane == 127), own, 0.0)
        fxp = jnp.concatenate([wxp, fx[:-1]], axis=0)
        diagonal = sv + (fx + fxp) + (fy + turn(fy, 1, 1)) + (fz + turn(fz, 1, 2))
        rdv = jnp.where(inside_at(p), 1.0 / diagonal, 0.0)
        at = pl.ds(p, CHUNK)
        wx[at], wy[at], wz[at], s[at], rd[at] = fx, fy, fz, sv, rdv
        body(p, rdv)
        return fx[-1:]

    lax.fori_loop(0, planes // CHUNK, step, jnp.zeros((1, rows, 128), F32))


def sweep_top(x, wx, wy, wz, s, low, high, body):
    fx0 = wx[low - 1 : low] * (x[low : low + 1] - x[low - 1 : low])

    def step(i, fxp):
        p = low + i * CHUNK
        at = pl.ds(p, CHUNK)
        v = x[at]
        vn = jnp.concatenate([v[1:], x[pl.ds(p + CHUNK, 1)]], axis=0)
        fx = wx[at] * (vn - v)
        fy = wy[at] * (turn(v, -1, 1) - v)
        fz = wz[at] * (turn(v, -1, 2) - v)
        fxp = jnp.concatenate([fxp, fx[:-1]], axis=0)
        total = (fx - fxp) + (fy - turn(fy, 1, 1)) + (fz - turn(fz, 1, 2))
        body(p, at, v, s[at] * v - total)
        return fx[-1:]

    assert (high - low) % CHUNK == 0
    lax.fori_loop(0, (high - low) // CHUNK, step, fx0)


def fill_top(dst, tile, left, right, below, above):
    dst[:, 0:2, :] = jnp.zeros((PX, 2, 128), F32)
    dst[:, RY - 2 : RY, :] = jnp.zeros((PX, 2, 128), F32)
    dst[0:HX, HY : HY + TY, :] = left
    dst[HX : HX + TX, HY : HY + TY, :] = tile
    dst[HX + TX :, HY : HY + TY, :] = right
    dst[:, 2:HY, :] = below
    dst[:, HY + TY : RY - 2, :] = above


def down_kernel(first, pos, tile, left, right, below, above, *refs):
    if first:
        ktile, r0, r1, xup, bup, kup, kx, one, two = refs[:9]
        scratch = refs[9:]
    else:
        kx, r0, r1, xup, bup, one, two = refs[:7]
        scratch = refs[7:]
    bx, wx, wy, wz, s, rd, d, x, rs, b1s, x1s, k1s = scratch
    gx, gy = pos[0], pos[1]
    inside_at = insider(RY, gx * TX - HX, gy * TY - HY)

    fill_top(bx, tile[...], left[0], right[0], below[0], above[0])
    if first:
        fill_top(kx, ktile[...], left[1], right[1], below[1], above[1])

        def clear(i, _):
            at = pl.ds(i * CHUNK, CHUNK)
            kx[at] = jnp.where(inside_at(i * CHUNK), kx[at], 0.0)
            return 0

        lax.fori_loop(0, PX // CHUNK, clear, 0)

    start, steps = SMOOTH

    def begin(p, rdv):
        at = pl.ds(p, CHUNK)
        v = (bx[at] * rdv) * start
        d[at] = v
        x[at] = v

    build_top(kx, wx, wy, wz, s, rd, PX, inside_at, begin)
    for number, (keep, gain) in enumerate(steps):

        def advance(p, at, v, av):
            dv = keep * d[at] + gain * ((bx[at] - av) * rd[at])
            d[at] = dv
            x[at] = v + dv

        sweep_top(x, wx, wy, wz, s, 2, PX - 2, advance)

    def residual(p, at, v, av):
        d[at] = bx[at] - av

    sweep_top(x, wx, wy, wz, s, 4, PX - 4, residual)
    xup[...] = x[4 : 4 + UX, 4 : 4 + UR, :]
    bup[...] = bx[4 : 4 + UX, 4 : 4 + UR, :]
    if first:
        kup[...] = kx[4 : 4 + UX, 4 : 4 + UR, :]

    def coarse(src):
        for c in range(16):
            rs[c] = src[2 + 2 * c] + src[3 + 2 * c]
        flat = [
            jnp.concatenate([pair_rows(rs, 2 * c, 4, 24), pair_rows(rs, 2 * c + 1, 4, 24)], axis=1)
            for c in range(8)
        ]
        return (0.125 * pair_dot(jnp.concatenate(flat, axis=0), r0[...])).reshape(8, 24, 128)

    d[2] = jnp.zeros((RY, 128), F32)
    d[3] = jnp.zeros((RY, 128), F32)
    d[PX - 4] = jnp.zeros((RY, 128), F32)
    d[PX - 3] = jnp.zeros((RY, 128), F32)
    b1 = coarse(d)
    k1 = coarse(kx)
    level = build(k1, 0.25, 64, within(k1.shape, gx * 8 - 4, gy * 16 - 4, 64, 128, 256))
    x1 = smooth(None, b1, level, 64)
    res = remain(x1, b1, level, 64)
    b1s[...] = b1
    x1s[...] = x1
    k1s[...] = k1
    one[0] = b1s[2:6, 4:20, :]
    one[1] = x1s[2:6, 4:20, :]
    if first:
        one[2] = k1s[2:6, 4:20, :]
    b1s[...] = res

    def coarse_tile(src):
        return jnp.concatenate([pair_rows(src, 2 + q, 4, 8) for q in range(4)], axis=1)

    flat = [coarse_tile(b1s)]
    if first:
        flat.append(coarse_tile(k1s))
    out = 0.125 * pair_dot(jnp.concatenate(flat, axis=0), r1[...])
    two[...] = out.reshape(len(flat), 8, 128)


def call(kernel, outs, scratch, *args, flops=1e7):
    specs = [pl.BlockSpec(memory_space=pltpu.SMEM)]
    specs += [pl.BlockSpec(memory_space=pltpu.VMEM)] * (len(args) - 1)
    return pl.pallas_call(
        kernel,
        out_shape=[jax.ShapeDtypeStruct(o, F32) for o in outs],
        in_specs=specs,
        out_specs=[pl.BlockSpec(memory_space=pltpu.VMEM)] * len(outs),
        scratch_shapes=[pltpu.VMEM(o, F32) for o in scratch],
        compiler_params=pltpu.CompilerParams(vmem_limit_bytes=VMEM_BYTES),
        cost_estimate=pl.CostEstimate(flops=int(flops), bytes_accessed=8 << 20, transcendentals=0),
    )(*args)


def go_down(first, pos, tile, left, right, below, above, kappa, r0, r1):
    top, up = (PX, RY, 128), (UX, UR, 128)
    outs = [up, up] + ([up, top] if first else []) + [(3 if first else 2, 4, 16, 128), (2 if first else 1, 8, 128)]
    scratch = [top] * 8 + [(16, RY, 128)] + [(8, 24, 128)] * 3
    kernel = functools.partial(down_kernel, first)
    return call(kernel, outs, scratch, pos, tile, left, right, below, above, kappa, r0, r1)


def mid_kernel(first, pos, mid, below, above, *refs):
    if first:
        r2, near, three, k2 = refs[:4]
        scratch = refs[4:]
    else:
        k2, r2, near, three = refs[:4]
        scratch = refs[4:]
    hold, rs, cs = scratch
    gx, gy = pos[0], pos[1]
    skip = below.shape[0] - mid.shape[0]
    shape = (16, 24, 128)
    inside = within(shape, 0, gy * 8 - 8, 32, 64, 128)

    def rows(dst, at):
        dst[:, 0:8, :] = below[skip + at : skip + at + 16]
        dst[:, 8:16, :] = mid[at : at + 16]
        dst[:, 16:24, :] = above[skip + at : skip + at + 16]

    rows(rs, 0)
    b = rs[...]
    if first:
        rows(k2, 16)
        k2[...] = jnp.where(inside, k2[...], 0.0)
    k = k2[...]
    plane = lax.broadcasted_iota(jnp.int32, shape, 0)
    lane = lanes(shape)
    edge_x = ((plane == 0) & (lane < 32), (plane == 15) & (lane >= 96))
    level = build(k, 0.25**2, 32, inside, edge_x)
    x = smooth(None, b, level, 32)
    rs[...] = remain(x, b, level, 32)
    for number, value in enumerate((b, x) + level):
        hold[number] = value
    for i in range(5):
        at = gx - 2 + i
        ok = (at >= 0) & (at < 16)
        from_plane = jnp.clip(at, 0, 15)
        for number in range(7):
            near[number, i] = jnp.where(ok, hold[number, from_plane], 0.0)

    def coarse(src, out):
        flat = [
            jnp.concatenate([pair_rows(src, 4 * c + q, 4, 8) for q in range(4)], axis=1) for c in range(4)
        ]
        cs[...] = (0.125 * pair_dot(jnp.concatenate(flat, axis=0), r2[...])).reshape(4, 8, 128)
        for c in range(4):
            three[out + c // 2, 4 * (c % 2) : 4 * (c % 2) + 4, :] = cs[c, 2:6, :]

    coarse(rs, 0)
    if first:
        coarse(k2, 2)


def go_mid(first, pos, mid, below, above, k2, r2):
    outs = [(7, 5, 24, 128), (4 if first else 2, 8, 128)] + ([(16, 24, 128)] if first else [])
    scratch = [(7, 16, 24, 128), (16, 24, 128), (4, 8, 128)]
    args = (mid, below, above) + (() if first else (k2,)) + (r2,)
    return call(functools.partial(mid_kernel, first), outs, scratch, pos, *args)


def solve_last(b, k, owned):
    shape = k.shape
    scale = 0.25**4
    lane = lanes(shape)
    row = lax.broadcasted_iota(jnp.int32, shape, 0)
    moves = (
        (8, 1, lane < 8, True),
        (-8, 1, lane >= 120, True),
        (1, 0, row == 0, True),
        (-1, 0, row == 31, True),
        (1, 1, (lane & 7) == 0, False),
        (-1, 1, (lane & 7) == 7, False),
    )
    diagonal = jnp.full(shape, SIGMA * scale, F32)
    pulls = []
    for shift, axis, edge, masked in moves:
        weight = (0.5 * scale) * (k + jnp.where(edge, 0.0, turn(k, shift, axis)))
        diagonal = diagonal + weight
        keep = jnp.where(edge, 0.0, weight)
        if masked:
            keep = jnp.where(owned == turn(owned, shift, axis), keep, 0.0)
        pulls.append(keep)
    rd = 1.0 / diagonal
    pulls = [keep * rd for keep in pulls]
    g = b * rd
    first, steps = COARSE
    d = g * first
    x = d
    for keep, gain in steps:
        total = [pull * turn(x, move[0], move[1]) for pull, move in zip(pulls, moves)]
        near = (total[0] + total[1]) + (total[2] + total[3]) + (total[4] + total[5])
        d = keep * d + gain * ((g - x) + near)
        x = x + d
    return x


def up_kernel(first, pos, owned, b3g, k3g, near, one, left, right, below, above, x0, b0, k0, *refs):
    if first:
        r3, t3, t2, t1, t0, xout, rout, k1 = refs[:8]
        scratch = refs[8:]
    else:
        k1, xbefore, borig, r3, t3, t2, t1, t0, xout, rout = refs[:10]
        scratch = refs[10:]
    b3, k3, s3, e2, s2, b1s, s1, e0, wx, wy, wz, s, rd, d, x = scratch
    gx, gy = pos[0], pos[1]

    for g in range(16):
        for c in range(4):
            part = slice(4 * (c % 2), 4 * (c % 2) + 4)
            b3[c, 4 * g : 4 * g + 4, :] = b3g[g, c // 2, part, :]
            k3[c, 4 * g : 4 * g + 4, :] = k3g[g, c // 2, part, :]
    shape = (4, 64, 128)
    plane = lax.broadcasted_iota(jnp.int32, shape, 0)
    rown = lax.broadcasted_iota(jnp.int32, shape, 1)
    lane = lanes(shape)
    level = build(
        k3[...],
        0.25**3,
        16,
        None,
        ((plane == 0) & (lane < 16), (plane == 3) & (lane >= 112)),
        (rown == 0, rown == 63),
    )
    b = b3[...]
    x3 = smooth(None, b, level, 16)
    s3[...] = remain(x3, b, level, 16)

    flat = [
        jnp.concatenate([pair_rows(src, q, 0, 32) for q in range(4)], axis=1) for src in (s3, k3)
    ]
    fine = 0.125 * pair_dot(jnp.concatenate(flat, axis=0), r3[...])
    x4 = solve_last(fine[:32], fine[32:], owned[...])

    back = pair_dot(x4, t3[...])
    for q in range(4):
        spread_rows(s3, q, 0, back[:, 128 * q : 128 * q + 128])
    s3[...] = smooth(x3 + s3[...], b, level, 16)

    for i in range(5):
        at = jnp.clip(gx - 2 + i, 0, 15)
        back = pair_dot(s3[at // 4], t2[at % 4])
        spread_rows(e2, i, 8, back)
    e = e2[:, pl.ds(pl.multiple_of(gy * 8, 8), 24), :]
    level = tuple(near[number] for number in range(2, 7))
    x2 = near[1] + jnp.where(level[4] > 0.0, e, 0.0)
    s2[...] = smooth(x2, near[0], level, 32)

    shape = (12, 32, 128)
    inside = within(shape, gx * 8 - 8, gy * 16 - 8, 64, 128, 256)

    def fill(dst, number):
        dst[0:4, 8:24, :] = left[number]
        dst[4:8, 8:24, :] = one[number]
        dst[8:12, 8:24, :] = right[number]
        dst[:, 0:8, :] = below[12 * number : 12 * number + 12]
        dst[:, 24:32, :] = above[12 * number : 12 * number + 12]

    fill(b1s, 0)
    fill(s1, 1)
    x1 = jnp.where(inside, s1[...], 0.0)
    if first:
        fill(k1, 2)
        k1[...] = jnp.where(inside, k1[...], 0.0)
    flat = jnp.concatenate([s2[i, 4:20, :] for i in range(1, 4)], axis=0)
    back = pair_dot(flat, t1[...])
    for i in range(3):
        for q in range(4):
            spread_rows(s1, 4 * i + q, 0, back[16 * i : 16 * i + 16, 128 * q : 128 * q + 128])
    level = build(k1[...], 0.25, 64, inside)
    x1 = x1 + jnp.where(inside, s1[...], 0.0)
    s1[...] = smooth(x1, b1s[...], level, 64)

    flat = jnp.concatenate([s1[i, 4:28, :] for i in range(3, 9)], axis=0)
    back = pair_dot(flat, t0[...])
    for i in range(6):
        for q in range(2):
            spread_rows(e0, 2 * i + q, 0, back[24 * i : 24 * i + 24, 128 * q : 128 * q + 128])
    inside_at = insider(UR, gx * TX - 6, gy * TY - 8)

    def begin(p, rdv):
        at = pl.ds(p, CHUNK)
        low = jnp.maximum(p // 2 - 1, 0)
        high = jnp.minimum(p // 2, 11)
        pair = (e0[pl.ds(low, 1)], e0[pl.ds(high, 1)])
        correction = jnp.concatenate([pair[0], pair[0], pair[1], pair[1]], axis=0)
        x[at] = x0[at] + jnp.where(rdv > 0.0, correction, 0.0)

    build_top(k0, wx, wy, wz, s, rd, UX, inside_at, begin)
    start, steps = SMOOTH

    def open_up(p, at, v, av):
        dv = ((b0[at] - av) * rd[at]) * start
        d[at] = dv
        x[at] = v + dv

    sweep_top(x, wx, wy, wz, s, 2, UX - 2, open_up)
    for number, (keep, gain) in enumerate(steps):

        def advance(p, at, v, av):
            dv = keep * d[at] + gain * ((b0[at] - av) * rd[at])
            d[at] = dv
            x[at] = v + dv

        sweep_top(x, wx, wy, wz, s, 4, UX - 4, advance)

    if first:
        xout[...] = x[5 : UX - 5]

        def residual(p, at, v, av):
            rout[pl.ds(p - 6, CHUNK)] = b0[at, 8 : 8 + TY, :] - av[:, 8 : 8 + TY]
    else:
        x[5 : UX - 5] = x[5 : UX - 5] + xbefore[...]

        def residual(p, at, v, av):
            out = pl.ds(p - 6, CHUNK)
            xout[out] = v[:, 8 : 8 + TY]
            rout[out] = borig[out] - av[:, 8 : 8 + TY]

    sweep_top(x, wx, wy, wz, s, 6, UX - 6, residual)


def go_up(first, *args):
    tile = (TX, TY, 128)
    outs = [(TX + 2, UR, 128), tile, (12, 32, 128)] if first else [tile, tile]
    up = (UX, UR, 128)
    scratch = [(4, 64, 128)] * 3 + [(5, 144, 128), (5, 24, 128), (12, 32, 128), (12, 32, 128), (12, UR, 128)]
    return call(functools.partial(up_kernel, first), outs, scratch + [up] * 7, *args)


def shift(value, axis, step):
    count = lax.axis_size(axis)
    return lax.ppermute(value, axis, [(i, (i + step) % count) for i in range(count)])


def gather(value, axis):
    count = lax.axis_size(axis)
    return lax.all_to_all(jnp.broadcast_to(value[None], (count,) + value.shape), axis, 0, 0, tiled=True)


def local(right_side, kappa, owners):
    pos = jnp.stack([lax.axis_index("gx"), lax.axis_index("gy")]).astype(jnp.int32)
    owned = jnp.repeat(jnp.repeat(owners.T, 2, 0), 8, 1).astype(F32)
    r0 = restrict_map(128)[128:384]
    r1, r2, r3 = restrict_map(64), restrict_map(32), restrict_map(16)
    t0 = prolong_map(128)[:, 128:384]
    t1, t3 = prolong_map(64), prolong_map(16)
    t2 = jnp.asarray(np.transpose(lane_map(32), (0, 2, 1)), BF16)

    source = right_side
    keep = {}
    for first in (True, False):
        mid = jnp.stack([source, kappa]) if first else source[None]
        left = shift(mid[:, TX - HX :], "gx", 1)
        right = shift(mid[:, :HX], "gx", -1)
        wide = jnp.concatenate([left, mid, right], axis=1)
        below = shift(wide[:, :, TY - HX :], "gy", 1)
        above = shift(wide[:, :, :HX], "gy", -1)
        out = go_down(first, pos, source, left, right, below, above, kappa if first else keep["kx"], r0, r1)
        if first:
            xup, bup, keep["kup"], keep["kx"], one, two = out
        else:
            xup, bup, one, two = out
        left = shift(one, "gx", 1)
        right = shift(one, "gx", -1)
        rows = jnp.swapaxes(gather(two, "gx"), 0, 1).reshape(-1, 8, 128)
        wide = jnp.concatenate([left, one, right], axis=1)
        low = wide[:, :, :8].reshape(-1, 8, 128)
        high = wide[:, :, 8:].reshape(-1, 8, 128)
        below = shift(jnp.concatenate([high, rows]), "gy", 1)
        above = shift(jnp.concatenate([low, rows]), "gy", -1)
        out = go_mid(first, pos, rows, below, above, keep.get("k2"), r2)
        if first:
            near, three, keep["k2"] = out
        else:
            near, three = out
        spread = gather(three, "gy")
        if first:
            keep["k3"] = spread[:, 2:]
            spread = spread[:, :2]
        args = (pos, owned, spread, keep["k3"], near, one, left, right, below, above, xup, bup, keep["kup"])
        if first:
            keep["x"], source, keep["k1"] = go_up(True, *args, r3, t3, t2, t1, t0)
        else:
            field, residual = go_up(False, *args, keep["k1"], keep["x"], right_side, r3, t3, t2, t1, t0)
    return field, residual


def solution(mesh):
    spec = P("gx", "gy", None)
    return jax.shard_map(
        local, mesh=mesh, in_specs=(spec, spec, P()), out_specs=(spec, spec), check_vma=False
    )
```

```python
import functools

import jax
import jax.numpy as jnp
import numpy as np
from jax import lax
from jax.experimental import pallas as pl
from jax.experimental.pallas import tpu as pltpu
from jax.sharding import PartitionSpec as P

SIGMA = 0.02
F32 = jnp.float32
BF16 = jnp.bfloat16
TX, TY = 16, 32
HX = 10
HY = 12
PX, RY = TX + 2 * HX, TY + 2 * HY
UX, UR = TX + 16, TY + 16
CHUNK = 4
VMEM_BYTES = 56 * 1024 * 1024


def cheb_steps(degree, lower):
    centre = 0.5 * (2.0 + lower)
    half = 0.5 * (2.0 - lower)
    sharp = centre / half
    ratio = 1.0 / sharp
    steps = []
    for _ in range(degree - 1):
        nxt = 1.0 / (2.0 * sharp - ratio)
        steps.append((nxt * ratio, 2.0 * nxt / half))
        ratio = nxt
    return 1.0 / centre, steps


SMOOTH = cheb_steps(3, 0.3)
COARSE = cheb_steps(24, 0.05)


def lane_map(z):
    groups = 128 // z
    out = np.zeros((4, 128, 128), np.float32)
    for q in range(4):
        for lane in range(128):
            cell = (lane // z + groups * q) // 2
            out[q, lane, cell * (z // 2) + (lane % z) // 2] = 1.0
    return out


def restrict_map(z):
    return jnp.asarray(lane_map(z).reshape(512, 128), BF16)


def prolong_map(z):
    return jnp.asarray(np.concatenate([m.T for m in lane_map(z)], axis=1), BF16)


def pair_dot(value, matrix):
    high = value.astype(BF16)
    rest = value - high.astype(F32)
    mid = rest.astype(BF16)
    low = (rest - mid.astype(F32)).astype(BF16)
    dot = functools.partial(jnp.dot, preferred_element_type=F32)
    return dot(high, matrix) + (dot(mid, matrix) + dot(low, matrix))


def lanes(shape):
    return lax.broadcasted_iota(jnp.int32, shape, len(shape) - 1)


def turn(value, shift, axis):
    return pltpu.roll(value, shift % value.shape[axis], axis)


def next_x(v, z):
    if z == 128:
        return jnp.concatenate([v[1:], v[:1]], axis=0)
    a = turn(v, -z, 2)
    b = jnp.concatenate([a[1:], a[:1]], axis=0)
    return jnp.where(lanes(v.shape) < 128 - z, a, b)


def prev_x(v, z):
    if z == 128:
        return jnp.concatenate([v[-1:], v[:-1]], axis=0)
    a = turn(v, z, 2)
    b = jnp.concatenate([a[-1:], a[:-1]], axis=0)
    return jnp.where(lanes(v.shape) >= z, a, b)


def faces_of(k, step, scale, low, high):
    own = (0.5 * scale) * k
    both = own + (0.5 * scale) * step
    if low is None:
        return both, None
    edge = jnp.where(low | high, own, 0.0)
    return jnp.where(high, 0.0, both), edge


def build(k, scale, z, inside=None, edge_x=(None, None), edge_y=(None, None)):
    shape = k.shape
    cell = lanes(shape) & (z - 1)
    wx, ex = faces_of(k, next_x(k, z), scale, *edge_x)
    wy, ey = faces_of(k, turn(k, -1, 1), scale, *edge_y)
    wz, ez = faces_of(k, turn(k, -1, 2), scale, cell == 0, cell == z - 1)
    s = ez + SIGMA * scale
    if ex is not None:
        s = s + ex
    if ey is not None:
        s = s + ey
    diagonal = s + wx + prev_x(wx, z) + wy + turn(wy, 1, 1) + wz + turn(wz, 1, 2)
    rd = 1.0 / diagonal
    if inside is not None:
        rd = jnp.where(inside, rd, 0.0)
    return wx, wy, wz, s, rd


def remain(v, b, level, z):
    wx, wy, wz, s, _ = level
    fx = wx * (next_x(v, z) - v)
    fy = wy * (turn(v, -1, 1) - v)
    fz = wz * (turn(v, -1, 2) - v)
    total = (fx - prev_x(fx, z)) + (fy - turn(fy, 1, 1)) + (fz - turn(fz, 1, 2))
    return (b - s * v) + total


def smooth(x, b, level, z):
    first, steps = SMOOTH
    rd = level[4]
    if x is None:
        d = (b * rd) * first
        x = d
    else:
        d = (remain(x, b, level, z) * rd) * first
        x = x + d
    for keep, gain in steps:
        d = keep * d + gain * (remain(x, b, level, z) * rd)
        x = x + d
    return x


def within(shape, first_x, first_y, z, size_x, size_y):
    plane = lax.broadcasted_iota(jnp.int32, shape, 0)
    cx = first_x + plane * (128 // z) + lanes(shape) // z
    cy = first_y + lax.broadcasted_iota(jnp.int32, shape, 1)
    return (cx >= 0) & (cx < size_x) & (cy >= 0) & (cy < size_y)


def pair_rows(ref, plane, start, count):
    return ref[plane, pl.ds(start, count, stride=2), :] + ref[plane, pl.ds(start + 1, count, stride=2), :]


def spread_rows(ref, plane, start, value):
    count = value.shape[0]
    ref[plane, pl.ds(start, count, stride=2), :] = value
    ref[plane, pl.ds(start + 1, count, stride=2), :] = value


def insider(rows, first_x, first_y):
    row = lax.broadcasted_iota(jnp.int32, (CHUNK, rows, 128), 1) + first_y
    row_in = (row >= 0) & (row < 512)
    plane = lax.broadcasted_iota(jnp.int32, (CHUNK, rows, 128), 0) + first_x
    return lambda p: row_in & (plane >= -p) & (plane < 256 - p)


def build_top(k_ref, wx, wy, wz, s, rd, low, high, inside_at, body):
    rows = k_ref.shape[1]
    shape = (CHUNK, rows, 128)
    lane = lanes(shape)

    def step(i, wxp):
        p = low + i * CHUNK
        k = k_ref[pl.ds(p, CHUNK)]
        kn = jnp.concatenate([k[1:], k_ref[pl.ds(jnp.minimum(p + CHUNK, k_ref.shape[0] - 1), 1)]], axis=0)
        own = 0.5 * k
        fx = 0.5 * kn + own
        fy = turn(own, -1, 1) + own
        fz = jnp.where(lane == 127, 0.0, turn(own, -1, 2) + own)
        sv = SIGMA + jnp.where((lane == 0) | (lane == 127), own, 0.0)
        fxp = jnp.concatenate([wxp, fx[:-1]], axis=0)
        diagonal = sv + (fx + fxp) + (fy + turn(fy, 1, 1)) + (fz + turn(fz, 1, 2))
        rdv = jnp.where(inside_at(p), 1.0 / diagonal, 0.0)
        at = pl.ds(p, CHUNK)
        wx[at], wy[at], wz[at], s[at], rd[at] = fx, fy, fz, sv, rdv
        body(p, rdv)
        return fx[-1:]

    assert (high - low) % CHUNK == 0
    lax.fori_loop(0, (high - low) // CHUNK, step, jnp.zeros((1, rows, 128), F32))


def sweep_top(x, wx, wy, wz, s, low, high, body):
    fx0 = wx[low - 1 : low] * (x[low : low + 1] - x[low - 1 : low])

    def step(i, fxp):
        p = low + i * CHUNK
        at = pl.ds(p, CHUNK)
        v = x[at]
        vn = jnp.concatenate([v[1:], x[pl.ds(p + CHUNK, 1)]], axis=0)
        fx = wx[at] * (vn - v)
        fy = wy[at] * (turn(v, -1, 1) - v)
        fz = wz[at] * (turn(v, -1, 2) - v)
        fxp = jnp.concatenate([fxp, fx[:-1]], axis=0)
        total = (fx - fxp) + (fy - turn(fy, 1, 1)) + (fz - turn(fz, 1, 2))
        body(p, at, v, s[at] * v - total)
        return fx[-1:]

    assert (high - low) % CHUNK == 0
    lax.fori_loop(0, (high - low) // CHUNK, step, fx0)


def fill_top(dst, tile, left, right, below, above):
    dst[:, 0:2, :] = jnp.zeros((PX, 2, 128), F32)
    dst[:, RY - 2 : RY, :] = jnp.zeros((PX, 2, 128), F32)
    dst[0:HX, HY : HY + TY, :] = left
    dst[HX : HX + TX, HY : HY + TY, :] = tile
    dst[HX + TX :, HY : HY + TY, :] = right
    dst[:, 2:HY, :] = below
    dst[:, HY + TY : RY - 2, :] = above


def down_kernel(pos, tile, left, right, below, above, ktile, r0, r1, xup, bup, kup, one, two, *scratch):
    bx, kx, wx, wy, wz, s, rd, d, x, rs, b1s, x1s, k1s = scratch
    gx, gy = pos[0], pos[1]
    inside_at = insider(RY, gx * TX - HX, gy * TY - HY)
    fill_top(bx, tile[...], left[0], right[0], below[0], above[0])
    fill_top(kx, ktile[...], left[1], right[1], below[1], above[1])

    def clear(i, _):
        at = pl.ds(i * CHUNK, CHUNK)
        kx[at] = jnp.where(inside_at(i * CHUNK), kx[at], 0.0)
        return 0

    lax.fori_loop(0, PX // CHUNK, clear, 0)
    start, steps = SMOOTH

    def begin(p, rdv):
        at = pl.ds(p, CHUNK)
        v = (bx[at] * rdv) * start
        d[at] = v
        x[at] = v

    build_top(kx, wx, wy, wz, s, rd, 0, PX, inside_at, begin)
    for keep, gain in steps:
        sweep_top(x, wx, wy, wz, s, 2, PX - 2, advance_top(keep, gain, bx, 0, rd, d, x))

    def residual(p, at, v, av):
        d[at] = bx[at] - av

    sweep_top(x, wx, wy, wz, s, 4, PX - 4, residual)
    region = (slice(2, 2 + UX), slice(4, 4 + UR))
    xup[...] = x[region]
    bup[...] = bx[region]
    kup[...] = kx[region]

    def coarse(src):
        for c in range(16):
            rs[c] = src[2 + 2 * c] + src[3 + 2 * c]
        return pair_planes(rs, 8, 4, 24, r0)

    for p in (2, 3, PX - 4, PX - 3):
        d[p] = jnp.zeros((RY, 128), F32)
    b1 = coarse(d)
    k1 = coarse(kx)
    level = build(k1, 0.25, 64, within(k1.shape, gx * 8 - 4, gy * 16 - 4, 64, 128, 256))
    x1 = smooth(None, b1, level, 64)
    b1s[...] = b1
    x1s[...] = x1
    k1s[...] = k1
    for number, src in enumerate((b1s, x1s, k1s)):
        one[number] = src[2:6, 4:20, :]
    b1s[...] = remain(x1, b1, level, 64)
    send_all(two, coarse_tile((b1s, k1s), 2, 4, r1))


def pair_planes(rs, planes, start, rows, r0):
    flat = [
        jnp.concatenate([pair_rows(rs, 2 * c, start, rows), pair_rows(rs, 2 * c + 1, start, rows)], axis=1)
        for c in range(planes)
    ]
    return (0.125 * pair_dot(jnp.concatenate(flat, axis=0), r0[...])).reshape(planes, rows, 128)


def coarse_tile(sources, plane, row, r1):
    flat = [
        jnp.concatenate([pair_rows(src, plane + q, row, 8) for q in range(4)], axis=1) for src in sources
    ]
    out = 0.125 * pair_dot(jnp.concatenate(flat, axis=0), r1[...])
    return out.reshape(len(sources), 8, 128)


def send_all(out, value):
    for g in range(16):
        out[g] = value


def advance_top(keep, gain, b, shift_b, rd, d, x):
    def advance(p, at, v, av):
        dv = keep * d[at] + gain * ((b[pl.ds(p - shift_b, CHUNK)] - av) * rd[at])
        d[at] = dv
        x[at] = v + dv

    return advance


def open_top(b, shift_b, rd, d, x):
    def advance(p, at, v, av):
        dv = ((b[pl.ds(p - shift_b, CHUNK)] - av) * rd[at]) * SMOOTH[0]
        d[at] = dv
        x[at] = v + dv

    return advance


def call(kernel, outs, scratch, *args, flops=1e7):
    specs = [pl.BlockSpec(memory_space=pltpu.SMEM)]
    specs += [pl.BlockSpec(memory_space=pltpu.VMEM)] * (len(args) - 1)
    return pl.pallas_call(
        kernel,
        out_shape=[jax.ShapeDtypeStruct(o, F32) for o in outs],
        in_specs=specs,
        out_specs=[pl.BlockSpec(memory_space=pltpu.VMEM)] * len(outs),
        scratch_shapes=[pltpu.VMEM(o, F32) for o in scratch],
        compiler_params=pltpu.CompilerParams(vmem_limit_bytes=VMEM_BYTES),
        cost_estimate=pl.CostEstimate(flops=int(flops), bytes_accessed=8 << 20, transcendentals=0),
    )(*args)


def go_down(*args):
    top, up = (PX, RY, 128), (UX, UR, 128)
    outs = [up, up, up, (3, 4, 16, 128), (16, 2, 8, 128)]
    scratch = [top] * 9 + [(16, RY, 128)] + [(8, 24, 128)] * 3
    return call(down_kernel, outs, scratch, *args)


def one_kernel(pos, mid, left, right, below, above, k1, r1, bout, xout, two, res):
    gx, gy = pos[0], pos[1]
    fill_one(bout, left[:, 0:16], mid[...], right[:, 0:16], below[...], above[...])
    b = bout[...]
    inside = within(b.shape, gx * 8 - 8, gy * 16 - 8, 64, 128, 256)
    level = build(k1[...], 0.25, 64, inside)
    x = smooth(None, b, level, 64)
    xout[...] = x
    res[...] = remain(x, b, level, 64)
    send_all(two, coarse_tile((res,), 4, 8, r1))


def fill_one(dst, left, tile, right, below, above):
    dst[0:4, 8:24, :] = left
    dst[4:8, 8:24, :] = tile
    dst[8:12, 8:24, :] = right
    dst[:, 0:8, :] = below
    dst[:, 24:32, :] = above


def go_one(*args):
    wide = (12, 32, 128)
    return call(one_kernel, [wide, wide, (16, 1, 8, 128)], [wide], *args)


def mid_kernel(first, pos, mid, below, above, *refs):
    if first:
        r2, near, three, k2, x2 = refs[:5]
        scratch = refs[5:]
    else:
        k2, r2, near, three = refs[:4]
        scratch = refs[4:]
    hold, rs, cs = scratch
    gx, gy = pos[0], pos[1]
    shape = (16, 24, 128)
    inside = within(shape, 0, gy * 8 - 8, 32, 64, 128)

    def rows(dst, number):
        part = slice(16 * number, 16 * number + 16)
        dst[:, 0:8, :] = below[part]
        dst[:, 8:16, :] = mid[:, number]
        dst[:, 16:24, :] = above[part]

    rows(rs, 0)
    b = rs[...]
    if first:
        rows(k2, 1)
        k2[...] = jnp.where(inside, k2[...], 0.0)
    k = k2[...]
    plane = lax.broadcasted_iota(jnp.int32, shape, 0)
    lane = lanes(shape)
    edge_x = ((plane == 0) & (lane < 32), (plane == 15) & (lane >= 96))
    level = build(k, 0.25**2, 32, inside, edge_x)
    x = smooth(None, b, level, 32)
    rs[...] = remain(x, b, level, 32)
    for number, value in enumerate((b, x) + level):
        hold[number] = value
    for i in range(5):
        at = gx - 2 + i
        ok = (at >= 0) & (at < 16)
        from_plane = jnp.clip(at, 0, 15)
        for number in range(7):
            near[number, i] = jnp.where(ok, hold[number, from_plane], 0.0)

    if first:
        x2[...] = near[1, :, 8:16, :]

    def coarse(src, out):
        flat = [
            jnp.concatenate([pair_rows(src, 4 * c + q, 4, 8) for q in range(4)], axis=1) for c in range(4)
        ]
        cs[...] = (0.125 * pair_dot(jnp.concatenate(flat, axis=0), r2[...])).reshape(4, 8, 128)
        for c in range(4):
            part = cs[c, 2:6, :]
            for g in range(16):
                three[g, out + c // 2, 4 * (c % 2) : 4 * (c % 2) + 4, :] = part

    coarse(rs, 0)
    if first:
        coarse(k2, 2)


def go_mid(first, pos, mid, below, above, k2, r2):
    outs = [(7, 5, 24, 128), (16, 4 if first else 2, 8, 128)]
    outs += [(16, 24, 128), (5, 8, 128)] if first else []
    scratch = [(7, 16, 24, 128), (16, 24, 128), (4, 8, 128)]
    args = (mid, below, above) + (() if first else (k2,)) + (r2,)
    return call(functools.partial(mid_kernel, first), outs, scratch, pos, *args)


def solve_last(b, k, owned):
    shape = k.shape
    scale = 0.25**4
    lane = lanes(shape)
    row = lax.broadcasted_iota(jnp.int32, shape, 0)
    moves = (
        (8, 1, lane < 8, True),
        (-8, 1, lane >= 120, True),
        (1, 0, row == 0, True),
        (-1, 0, row == 31, True),
        (1, 1, (lane & 7) == 0, False),
        (-1, 1, (lane & 7) == 7, False),
    )
    diagonal = jnp.full(shape, SIGMA * scale, F32)
    pulls = []
    for shift, axis, edge, masked in moves:
        weight = (0.5 * scale) * (k + jnp.where(edge, 0.0, turn(k, shift, axis)))
        diagonal = diagonal + weight
        keep = jnp.where(edge, 0.0, weight)
        if masked:
            keep = jnp.where(owned == turn(owned, shift, axis), keep, 0.0)
        pulls.append(keep)
    rd = 1.0 / diagonal
    pulls = [keep * rd for keep in pulls]
    g = b * rd
    first, steps = COARSE
    d = g * first
    x = d
    for keep, gain in steps:
        total = [pull * turn(x, move[0], move[1]) for pull, move in zip(pulls, moves)]
        near = (total[0] + total[1]) + (total[2] + total[3]) + (total[4] + total[5])
        d = keep * d + gain * ((g - x) + near)
        x = x + d
    return x


def fill_three(dst, gathered, first):
    for g in range(16):
        for c in range(4):
            part = gathered[g, first + c // 2, 4 * (c % 2) : 4 * (c % 2) + 4, :]
            dst[c, 4 * g : 4 * g + 4, :] = part


def solve_three(b_ref, k_ref, owned, s3, r3, t3):
    shape = (4, 64, 128)
    plane = lax.broadcasted_iota(jnp.int32, shape, 0)
    row = lax.broadcasted_iota(jnp.int32, shape, 1)
    lane = lanes(shape)
    edge_x = ((plane == 0) & (lane < 16), (plane == 3) & (lane >= 112))
    level = build(k_ref[...], 0.25**3, 16, None, edge_x, (row == 0, row == 63))
    b = b_ref[...]
    x = smooth(None, b, level, 16)
    s3[...] = remain(x, b, level, 16)
    flat = [
        jnp.concatenate([pair_rows(src, q, 0, 32) for q in range(4)], axis=1) for src in (s3, k_ref)
    ]
    fine = 0.125 * pair_dot(jnp.concatenate(flat, axis=0), r3[...])
    last = solve_last(fine[:32], fine[32:], owned[...])
    back = pair_dot(last, t3[...])
    for q in range(4):
        spread_rows(s3, q, 0, back[:, 128 * q : 128 * q + 128])
    s3[...] = smooth(x + s3[...], b, level, 16)


def rise_two(gx, gy, near, x2, s3, t2, e2, s2):
    for i in range(5):
        at = jnp.clip(gx - 2 + i, 0, 15)
        spread_rows(e2, i, 8, pair_dot(s3[at // 4], t2[at % 4]))
    e = e2[:, pl.ds(pl.multiple_of(gy * 8, 8), 24), :]
    level = tuple(near[number] for number in range(2, 7))
    x = jnp.where(level[4] > 0.0, x2 + e, 0.0)
    s2[...] = smooth(x, near[0], level, 32)


def rise_one(x1, b1, k1, inside, s2, t1, s1):
    flat = jnp.concatenate([s2[i, 4:20, :] for i in range(1, 4)], axis=0)
    back = pair_dot(flat, t1[...])
    for i in range(3):
        for q in range(4):
            spread_rows(s1, 4 * i + q, 0, back[16 * i : 16 * i + 16, 128 * q : 128 * q + 128])
    level = build(k1, 0.25, 64, inside)
    s1[...] = smooth(jnp.where(inside, x1 + s1[...], 0.0), b1, level, 64)


def spread_one(s1, low, high, t0, e0):
    flat = jnp.concatenate([s1[i, 4:28, :] for i in range(low, high)], axis=0)
    back = pair_dot(flat, t0[...])
    for i in range(high - low):
        for q in range(2):
            part = back[24 * i : 24 * i + 24, 128 * q : 128 * q + 128]
            spread_rows(e0, 2 * (low - 2 + i) + q, 0, part)


def add_top(x0, e0, x):
    def begin(p, rdv):
        c = p // 2
        pair = (e0[pl.ds(c, 1)], e0[pl.ds(c + 1, 1)])
        correction = jnp.concatenate([pair[0], pair[0], pair[1], pair[1]], axis=0)
        at = pl.ds(p, CHUNK)
        x[at] = jnp.where(rdv > 0.0, x0[at] + correction, 0.0)

    return begin


def turn_kernel(
    pos, owned, three, near, x2low, x2high, one, left, right, below, above, x0, b0, k0, r0, r3, t3, t2, t1, t0,
    k3, k1, xout, rout, x0n, b1n, east, west,
    b3, s3, e2, s2, x2s, b1s, s1, e0, wx, wy, wz, s, rd, d, x, rs
):
    gx, gy = pos[0], pos[1]
    fill_three(b3, three, 0)
    fill_three(k3, three, 2)
    solve_three(b3, k3, owned, s3, r3, t3)
    x2s[:, 0:8, :] = x2low[...]
    x2s[:, 8:16, :] = near[1, :, 8:16, :]
    x2s[:, 16:24, :] = x2high[...]
    rise_two(gx, gy, near, x2s[...], s3, t2, e2, s2)

    inside = within((12, 32, 128), gx * 8 - 8, gy * 16 - 8, 64, 128, 256)
    for number, dst in enumerate((b1s, s1, k1)):
        part = slice(32 + 12 * number, 44 + 12 * number)
        fill_one(dst, left[number], one[number], right[number], below[part], above[part])
    k1[...] = jnp.where(inside, k1[...], 0.0)
    rise_one(s1[...], b1s[...], k1[...], inside, s2, t1, s1)

    spread_one(s1, 2, 10, t0, e0)
    inside_at = insider(UR, gx * TX - 8, gy * TY - 8)
    build_top(k0, wx, wy, wz, s, rd, 0, UX, inside_at, add_top(x0, e0, x))
    start, steps = SMOOTH
    sweep_top(x, wx, wy, wz, s, 2, UX - 2, open_top(b0, 0, rd, d, x))
    for (keep, gain), edge in zip(steps, (2, 4)):
        sweep_top(x, wx, wy, wz, s, edge, UX - edge, advance_top(keep, gain, b0, 0, rd, d, x))

    def residual(p, at, v, av):
        rout[pl.ds(p - 4, CHUNK)] = b0[at] - av

    sweep_top(x, wx, wy, wz, s, 4, UX - 4, residual)
    xout[...] = x[7 : UX - 7]

    def begin(i, _):
        at = pl.ds(4 + i * CHUNK, CHUNK)
        v = (rout[pl.ds(i * CHUNK, CHUNK)] * rd[at]) * start
        d[at] = v
        x[at] = v
        return 0

    lax.fori_loop(0, (UX - 8) // CHUNK, begin, 0)
    for keep, gain in steps:
        sweep_top(x, wx, wy, wz, s, 6, UX - 6, advance_top(keep, gain, rout, 4, rd, d, x))

    def again(p, at, v, av):
        d[at] = rout[pl.ds(p - 4, CHUNK)] - av

    sweep_top(x, wx, wy, wz, s, 8, UX - 8, again)
    x0n[...] = x[8:24, 8:40, :]
    for c in range(8):
        rs[c] = d[8 + 2 * c] + d[9 + 2 * c]
    b1 = pair_planes(rs, 4, 8, 16, r0)
    b1n[...] = b1
    for side, plane in ((east, 20), (west, 8)):
        side[:, 0:16, :] = b1
        side[:, 16:48, :] = x[plane : plane + 4, 8:40, :]


def go_turn(*args):
    up, wide = (UX, UR, 128), (12, 32, 128)
    outs = [(4, 64, 128), wide, (TX + 2, UR, 128), (TX + 8, UR, 128), (TX, TY, 128), (4, 16, 128)]
    outs += [(4, 48, 128)] * 2
    scratch = [(4, 64, 128)] * 2 + [(5, 144, 128), (5, 24, 128), (5, 24, 128), wide, wide, (16, UR, 128)]
    return call(turn_kernel, outs, scratch + [up] * 7 + [(8, UR, 128)], *args)


def last_kernel(
    pos, owned, three, k3, near, b1, x1, k1, x0n, left, right, below, above, r, k0, xbefore, borig,
    r3, t3, t2, t1, t0, xout, rout,
    b3, s3, e2, s2, s1, e0, wx, wy, wz, s, rd, d, x
):
    gx, gy = pos[0], pos[1]
    fill_three(b3, three, 0)
    solve_three(b3, k3, owned, s3, r3, t3)
    rise_two(gx, gy, near, near[1], s3, t2, e2, s2)
    inside = within((12, 32, 128), gx * 8 - 8, gy * 16 - 8, 64, 128, 256)
    rise_one(x1[...], b1[...], k1[...], inside, s2, t1, s1)

    spread_one(s1, 3, 9, t0, e0)
    x[4:8, 8:40, :] = left[:, 16:48, :]
    x[8:24, 8:40, :] = x0n[...]
    x[24:28, 8:40, :] = right[:, 16:48, :]
    x[4:28, 0:8, :] = below[16:40]
    x[4:28, 40:48, :] = above[16:40]
    inside_at = insider(UR, gx * TX - 8, gy * TY - 8)
    build_top(k0, wx, wy, wz, s, rd, 4, UX - 4, inside_at, add_top(x, e0, x))
    sweep_top(x, wx, wy, wz, s, 4, UX - 4, open_top(r, 4, rd, d, x))
    for keep, gain in SMOOTH[1]:
        sweep_top(x, wx, wy, wz, s, 6, UX - 6, advance_top(keep, gain, r, 4, rd, d, x))
    x[7 : UX - 7] = x[7 : UX - 7] + xbefore[...]

    def residual(p, at, v, av):
        out = pl.ds(p - 8, CHUNK)
        xout[out] = v[:, 8 : 8 + TY]
        rout[out] = borig[out] - av[:, 8 : 8 + TY]

    sweep_top(x, wx, wy, wz, s, 8, UX - 8, residual)


def go_last(*args):
    up, wide, tile = (UX, UR, 128), (12, 32, 128), (TX, TY, 128)
    scratch = [(4, 64, 128)] * 2 + [(5, 144, 128), (5, 24, 128), wide, (16, UR, 128)]
    return call(last_kernel, [tile, tile], scratch + [up] * 7, *args)


def shift(value, axis, step):
    count = lax.axis_size(axis)
    return lax.ppermute(value, axis, [(i, (i + step) % count) for i in range(count)])


def gather(copies, axis):
    return lax.all_to_all(copies, axis, 0, 0, tiled=True)


def local(right_side, kappa, owners):
    pos = jnp.stack([lax.axis_index("gx"), lax.axis_index("gy")]).astype(jnp.int32)
    owned = jnp.repeat(jnp.repeat(owners.T, 2, 0), 8, 1).astype(F32)
    r0 = restrict_map(128)[128:384]
    r1, r2, r3 = restrict_map(64), restrict_map(32), restrict_map(16)
    t0 = prolong_map(128)[:, 128:384]
    t1, t3 = prolong_map(64), prolong_map(16)
    t2 = jnp.asarray(np.transpose(lane_map(32), (0, 2, 1)), BF16)

    mid = jnp.stack([right_side, kappa])
    left = shift(mid[:, TX - HX :], "gx", 1)
    right = shift(mid[:, :HX], "gx", -1)
    wide = jnp.concatenate([left, mid, right], axis=1)
    below = shift(wide[:, :, TY - HX :], "gy", 1)
    above = shift(wide[:, :, :HX], "gy", -1)
    xup, bup, kup, one, two = go_down(pos, right_side, left, right, below, above, kappa, r0, r1)
    left = shift(one, "gx", 1)
    right = shift(one, "gx", -1)
    two = gather(two, "gx")
    rows = jnp.swapaxes(two, 0, 1).reshape(-1, 8, 128)
    wide = jnp.concatenate([left, one, right], axis=1)
    below = shift(jnp.concatenate([rows, wide[:, :, 8:].reshape(-1, 8, 128)]), "gy", 1)
    above = shift(jnp.concatenate([rows, wide[:, :, :8].reshape(-1, 8, 128)]), "gy", -1)
    near, three, k2, x2 = go_mid(True, pos, two, below, above, None, r2)
    x2low = shift(x2, "gy", 1)
    x2high = shift(x2, "gy", -1)
    three = gather(three, "gy")
    k3, k1, xbefore, source, x0n, b1n, east, west = go_turn(
        pos, owned, three, near, x2low, x2high, one, left, right, below, above, xup, bup, kup, r0, r3, t3, t2, t1, t0
    )

    left = shift(east, "gx", 1)
    right = shift(west, "gx", -1)
    wide = jnp.concatenate([left[:, :16], b1n, right[:, :16]])
    below = shift(wide[:, 8:], "gy", 1)
    above = shift(wide[:, :8], "gy", -1)
    b1, x1, two = go_one(pos, b1n, left, right, below, above, k1, r1)
    two = gather(two, "gx")
    wide = jnp.concatenate([left[:, 16:], x0n, right[:, 16:]])
    below = shift(jnp.concatenate([two[:, 0], wide[:, 24:]]), "gy", 1)
    above = shift(jnp.concatenate([two[:, 0], wide[:, :8]]), "gy", -1)
    near, three = go_mid(False, pos, two, below, above, k2, r2)
    three = gather(three, "gy")
    field, residual = go_last(
        pos, owned, three, k3, near, b1, x1, k1, x0n, left, right, below, above, source, kup, xbefore, right_side,
        r3, t3, t2, t1, t0
    )
    return field, residual


def solution(mesh):
    spec = P("gx", "gy", None)
    return jax.shard_map(
        local, mesh=mesh, in_specs=(spec, spec, P()), out_specs=(spec, spec), check_vma=False
    )
```

```python
import functools

import jax
import jax.numpy as jnp
import numpy as np
from jax import lax
from jax.experimental import pallas as pl
from jax.experimental.pallas import tpu as pltpu
from jax.sharding import PartitionSpec as P

SIGMA = 0.02
F32 = jnp.float32
BF16 = jnp.bfloat16
TX, TY = 16, 32
HX = 10
HY = 12
PX, RY = TX + 2 * HX, TY + 2 * HY
CHUNK = 4
VMEM_BYTES = 24 * 1024 * 1024


def cheb_steps(degree, lower):
    centre = 0.5 * (2.0 + lower)
    half = 0.5 * (2.0 - lower)
    sharp = centre / half
    ratio = 1.0 / sharp
    steps = []
    for _ in range(degree - 1):
        nxt = 1.0 / (2.0 * sharp - ratio)
        steps.append((nxt * ratio, 2.0 * nxt / half))
        ratio = nxt
    return 1.0 / centre, steps


SMOOTH = cheb_steps(3, 0.3)
COARSE = cheb_steps(24, 0.05)


def lane_map(z):
    groups = 128 // z
    out = np.zeros((4, 128, 128), np.float32)
    for q in range(4):
        for lane in range(128):
            cell = (lane // z + groups * q) // 2
            out[q, lane, cell * (z // 2) + (lane % z) // 2] = 1.0
    return out


def restrict_map(z):
    return jnp.asarray(lane_map(z).reshape(512, 128), BF16)


def prolong_map(z):
    return jnp.asarray(np.concatenate([m.T for m in lane_map(z)], axis=1), BF16)


def pair_dot(value, matrix):
    high = value.astype(BF16)
    rest = value - high.astype(F32)
    mid = rest.astype(BF16)
    low = (rest - mid.astype(F32)).astype(BF16)
    dot = functools.partial(jnp.dot, preferred_element_type=F32)
    return dot(high, matrix) + (dot(mid, matrix) + dot(low, matrix))


def lanes(shape):
    return lax.broadcasted_iota(jnp.int32, shape, len(shape) - 1)


def turn(value, shift, axis):
    return pltpu.roll(value, shift % value.shape[axis], axis)


def next_x(v, z):
    if z == 128:
        return jnp.concatenate([v[1:], v[:1]], axis=0)
    a = turn(v, -z, 2)
    b = jnp.concatenate([a[1:], a[:1]], axis=0)
    return jnp.where(lanes(v.shape) < 128 - z, a, b)


def prev_x(v, z):
    if z == 128:
        return jnp.concatenate([v[-1:], v[:-1]], axis=0)
    a = turn(v, z, 2)
    b = jnp.concatenate([a[-1:], a[:-1]], axis=0)
    return jnp.where(lanes(v.shape) >= z, a, b)


def faces_of(k, step, scale, low, high):
    own = (0.5 * scale) * k
    both = own + (0.5 * scale) * step
    if low is None:
        return both, None
    edge = jnp.where(low | high, own, 0.0)
    return jnp.where(high, 0.0, both), edge


def build(k, scale, z, inside=None, edge_x=(None, None), edge_y=(None, None)):
    shape = k.shape
    cell = lanes(shape) & (z - 1)
    wx, ex = faces_of(k, next_x(k, z), scale, *edge_x)
    wy, ey = faces_of(k, turn(k, -1, 1), scale, *edge_y)
    wz, ez = faces_of(k, turn(k, -1, 2), scale, cell == 0, cell == z - 1)
    s = ez + SIGMA * scale
    if ex is not None:
        s = s + ex
    if ey is not None:
        s = s + ey
    diagonal = s + wx + prev_x(wx, z) + wy + turn(wy, 1, 1) + wz + turn(wz, 1, 2)
    rd = 1.0 / diagonal
    if inside is not None:
        rd = jnp.where(inside, rd, 0.0)
    return wx, wy, wz, s, rd


def remain(v, b, level, z):
    wx, wy, wz, s, _ = level
    fx = wx * (next_x(v, z) - v)
    fy = wy * (turn(v, -1, 1) - v)
    fz = wz * (turn(v, -1, 2) - v)
    total = (fx - prev_x(fx, z)) + (fy - turn(fy, 1, 1)) + (fz - turn(fz, 1, 2))
    return (b - s * v) + total


def smooth(x, b, level, z):
    first, steps = SMOOTH
    rd = level[4]
    if x is None:
        d = (b * rd) * first
        x = d
    else:
        d = (remain(x, b, level, z) * rd) * first
        x = x + d
    for keep, gain in steps:
        d = keep * d + gain * (remain(x, b, level, z) * rd)
        x = x + d
    return x


def within(shape, first_x, first_y, z, size_x, size_y):
    plane = lax.broadcasted_iota(jnp.int32, shape, 0)
    cx = first_x + plane * (128 // z) + lanes(shape) // z
    cy = first_y + lax.broadcasted_iota(jnp.int32, shape, 1)
    return (cx >= 0) & (cx < size_x) & (cy >= 0) & (cy < size_y)


def pair_rows(ref, plane, start, count):
    return ref[plane, pl.ds(start, count, stride=2), :] + ref[plane, pl.ds(start + 1, count, stride=2), :]


def spread_rows(ref, plane, start, value):
    count = value.shape[0]
    ref[plane, pl.ds(start, count, stride=2), :] = value
    ref[plane, pl.ds(start + 1, count, stride=2), :] = value


def insider(rows, first_x, first_y):
    row = lax.broadcasted_iota(jnp.int32, (CHUNK, rows, 128), 1) + first_y
    row_in = (row >= 0) & (row < 512)
    plane = lax.broadcasted_iota(jnp.int32, (CHUNK, rows, 128), 0) + first_x
    return lambda p: row_in & (plane >= -p) & (plane < 256 - p)


def build_top(k_ref, wx, wy, wz, s, rd, low, high, inside_at, body):
    rows = k_ref.shape[1]
    shape = (CHUNK, rows, 128)
    lane = lanes(shape)

    def step(i, wxp):
        p = low + i * CHUNK
        k = k_ref[pl.ds(p, CHUNK)]
        kn = jnp.concatenate([k[1:], k_ref[pl.ds(jnp.minimum(p + CHUNK, k_ref.shape[0] - 1), 1)]], axis=0)
        own = 0.5 * k
        fx = 0.5 * kn + own
        fy = turn(own, -1, 1) + own
        fz = jnp.where(lane == 127, 0.0, turn(own, -1, 2) + own)
        sv = SIGMA + jnp.where((lane == 0) | (lane == 127), own, 0.0)
        fxp = jnp.concatenate([wxp, fx[:-1]], axis=0)
        diagonal = sv + (fx + fxp) + (fy + turn(fy, 1, 1)) + (fz + turn(fz, 1, 2))
        rdv = jnp.where(inside_at(p), 1.0 / diagonal, 0.0)
        at = pl.ds(p, CHUNK)
        wx[at], wy[at], wz[at], s[at], rd[at] = fx, fy, fz, sv, rdv
        body(p, rdv)
        return fx[-1:]

    assert (high - low) % CHUNK == 0
    lax.fori_loop(0, (high - low) // CHUNK, step, jnp.zeros((1, rows, 128), F32))


def sweep_top(x, wx, wy, wz, s, low, high, body):
    fx0 = wx[low - 1 : low] * (x[low : low + 1] - x[low - 1 : low])

    def step(i, fxp):
        p = low + i * CHUNK
        at = pl.ds(p, CHUNK)
        v = x[at]
        vn = jnp.concatenate([v[1:], x[pl.ds(p + CHUNK, 1)]], axis=0)
        fx = wx[at] * (vn - v)
        fy = wy[at] * (turn(v, -1, 1) - v)
        fz = wz[at] * (turn(v, -1, 2) - v)
        fxp = jnp.concatenate([fxp, fx[:-1]], axis=0)
        total = (fx - fxp) + (fy - turn(fy, 1, 1)) + (fz - turn(fz, 1, 2))
        body(p, at, v, s[at] * v - total)
        return fx[-1:]

    assert (high - low) % CHUNK == 0
    lax.fori_loop(0, (high - low) // CHUNK, step, fx0)


def fill_top(dst, tile, left, right, below, above):
    dst[:, 0:2, :] = jnp.zeros((PX, 2, 128), F32)
    dst[:, RY - 2 : RY, :] = jnp.zeros((PX, 2, 128), F32)
    dst[0:HX, HY : HY + TY, :] = left
    dst[HX : HX + TX, HY : HY + TY, :] = tile
    dst[HX + TX :, HY : HY + TY, :] = right
    dst[:, 2:HY, :] = below
    dst[:, HY + TY : RY - 2, :] = above


def down_kernel(pos, tile, left, right, below, above, ktile, r0, r1, bx, x, wx, wy, wz, s, rd, one, two, *scratch):
    kx, d, rs, b1s, x1s, k1s = scratch
    gx, gy = pos[0], pos[1]
    inside_at = insider(RY, gx * TX - HX, gy * TY - HY)
    fill_top(bx, tile[...], left[0], right[0], below[0], above[0])
    fill_top(kx, ktile[...], left[1], right[1], below[1], above[1])

    def clear(i, _):
        at = pl.ds(i * CHUNK, CHUNK)
        kx[at] = jnp.where(inside_at(i * CHUNK), kx[at], 0.0)
        return 0

    lax.fori_loop(0, PX // CHUNK, clear, 0)
    start, steps = SMOOTH

    def begin(p, rdv):
        at = pl.ds(p, CHUNK)
        v = (bx[at] * rdv) * start
        d[at] = v
        x[at] = v

    build_top(kx, wx, wy, wz, s, rd, 0, PX, inside_at, begin)
    for keep, gain in steps:
        sweep_top(x, wx, wy, wz, s, 2, PX - 2, advance_top(keep, gain, bx, 0, rd, d, x))

    def residual(p, at, v, av):
        d[at] = bx[at] - av

    sweep_top(x, wx, wy, wz, s, 4, PX - 4, residual)

    def coarse(src):
        for c in range(16):
            rs[c] = src[2 + 2 * c] + src[3 + 2 * c]
        return pair_planes(rs, 8, 4, 24, r0)

    for p in (2, 3, PX - 4, PX - 3):
        d[p] = jnp.zeros((RY, 128), F32)
    b1 = coarse(d)
    k1 = coarse(kx)
    level = build(k1, 0.25, 64, within(k1.shape, gx * 8 - 4, gy * 16 - 4, 64, 128, 256))
    x1 = smooth(None, b1, level, 64)
    b1s[...] = b1
    x1s[...] = x1
    k1s[...] = k1
    for number, src in enumerate((b1s, x1s, k1s)):
        one[number] = src[2:6, 4:20, :]
    b1s[...] = remain(x1, b1, level, 64)
    send_all(two, coarse_tile((b1s, k1s), 2, 4, r1))


def pair_planes(rs, planes, start, rows, r0):
    flat = [
        jnp.concatenate([pair_rows(rs, 2 * c, start, rows), pair_rows(rs, 2 * c + 1, start, rows)], axis=1)
        for c in range(planes)
    ]
    return (0.125 * pair_dot(jnp.concatenate(flat, axis=0), r0[...])).reshape(planes, rows, 128)


def coarse_tile(sources, plane, row, r1):
    flat = [
        jnp.concatenate([pair_rows(src, plane + q, row, 8) for q in range(4)], axis=1) for src in sources
    ]
    out = 0.125 * pair_dot(jnp.concatenate(flat, axis=0), r1[...])
    return out.reshape(len(sources), 8, 128)


def send_all(out, value):
    for g in range(16):
        out[g] = value


def advance_top(keep, gain, b, shift_b, rd, d, x):
    def advance(p, at, v, av):
        dv = keep * d[at] + gain * ((b[pl.ds(p - shift_b, CHUNK)] - av) * rd[at])
        d[at] = dv
        x[at] = v + dv

    return advance


def open_top(b, shift_b, rd, d, x):
    def advance(p, at, v, av):
        dv = ((b[pl.ds(p - shift_b, CHUNK)] - av) * rd[at]) * SMOOTH[0]
        d[at] = dv
        x[at] = v + dv

    return advance


def call(kernel, outs, scratch, *args, flops=1e7):
    specs = [pl.BlockSpec(memory_space=pltpu.SMEM)]
    specs += [pl.BlockSpec(memory_space=pltpu.VMEM)] * (len(args) - 1)
    return pl.pallas_call(
        kernel,
        out_shape=[jax.ShapeDtypeStruct(o, F32) for o in outs],
        in_specs=specs,
        out_specs=[pl.BlockSpec(memory_space=pltpu.VMEM)] * len(outs),
        scratch_shapes=[pltpu.VMEM(o, F32) for o in scratch],
        compiler_params=pltpu.CompilerParams(vmem_limit_bytes=VMEM_BYTES),
        cost_estimate=pl.CostEstimate(flops=int(flops), bytes_accessed=8 << 20, transcendentals=0),
    )(*args)


def go_down(*args):
    top = (PX, RY, 128)
    outs = [top] * 7 + [(3, 4, 16, 128), (16, 2, 8, 128)]
    scratch = [top] * 2 + [(16, RY, 128)] + [(8, 24, 128)] * 3
    return call(down_kernel, outs, scratch, *args)


def one_kernel(pos, mid, left, right, below, above, k1, r1, bout, xout, two, res):
    gx, gy = pos[0], pos[1]
    fill_one(bout, left[:, 0:16], mid[...], right[:, 0:16], below[...], above[...])
    b = bout[...]
    inside = within(b.shape, gx * 8 - 8, gy * 16 - 8, 64, 128, 256)
    level = build(k1[...], 0.25, 64, inside)
    x = smooth(None, b, level, 64)
    xout[...] = x
    res[...] = remain(x, b, level, 64)
    send_all(two, coarse_tile((res,), 4, 8, r1))


def fill_one(dst, left, tile, right, below, above):
    dst[0:4, 8:24, :] = left
    dst[4:8, 8:24, :] = tile
    dst[8:12, 8:24, :] = right
    dst[:, 0:8, :] = below
    dst[:, 24:32, :] = above


def go_one(*args):
    wide = (12, 32, 128)
    return call(one_kernel, [wide, wide, (16, 1, 8, 128)], [wide], *args)


def mid_kernel(first, pos, mid, below, above, *refs):
    if first:
        r2, near, three, k2, x2 = refs[:5]
        scratch = refs[5:]
    else:
        k2, r2, near, three = refs[:4]
        scratch = refs[4:]
    hold, rs, cs = scratch
    gx, gy = pos[0], pos[1]
    shape = (16, 24, 128)
    inside = within(shape, 0, gy * 8 - 8, 32, 64, 128)

    def rows(dst, number):
        part = slice(16 * number, 16 * number + 16)
        dst[:, 0:8, :] = below[part]
        dst[:, 8:16, :] = mid[:, number]
        dst[:, 16:24, :] = above[part]

    rows(rs, 0)
    b = rs[...]
    if first:
        rows(k2, 1)
        k2[...] = jnp.where(inside, k2[...], 0.0)
    k = k2[...]
    plane = lax.broadcasted_iota(jnp.int32, shape, 0)
    lane = lanes(shape)
    edge_x = ((plane == 0) & (lane < 32), (plane == 15) & (lane >= 96))
    level = build(k, 0.25**2, 32, inside, edge_x)
    x = smooth(None, b, level, 32)
    rs[...] = remain(x, b, level, 32)
    for number, value in enumerate((b, x) + level):
        hold[number] = value
    for i in range(5):
        at = gx - 2 + i
        ok = (at >= 0) & (at < 16)
        from_plane = jnp.clip(at, 0, 15)
        for number in range(7):
            near[number, i] = jnp.where(ok, hold[number, from_plane], 0.0)

    if first:
        x2[...] = near[1, :, 8:16, :]

    def coarse(src, out):
        flat = [
            jnp.concatenate([pair_rows(src, 4 * c + q, 4, 8) for q in range(4)], axis=1) for c in range(4)
        ]
        cs[...] = (0.125 * pair_dot(jnp.concatenate(flat, axis=0), r2[...])).reshape(4, 8, 128)
        for c in range(4):
            part = cs[c, 2:6, :]
            for g in range(16):
                three[g, out + c // 2, 4 * (c % 2) : 4 * (c % 2) + 4, :] = part

    coarse(rs, 0)
    if first:
        coarse(k2, 2)


def go_mid(first, pos, mid, below, above, k2, r2):
    outs = [(7, 5, 24, 128), (16, 4 if first else 2, 8, 128)]
    outs += [(16, 24, 128), (5, 8, 128)] if first else []
    scratch = [(7, 16, 24, 128), (16, 24, 128), (4, 8, 128)]
    args = (mid, below, above) + (() if first else (k2,)) + (r2,)
    return call(functools.partial(mid_kernel, first), outs, scratch, pos, *args)


def solve_last(b, k, owned):
    shape = k.shape
    scale = 0.25**4
    lane = lanes(shape)
    row = lax.broadcasted_iota(jnp.int32, shape, 0)
    moves = (
        (8, 1, lane < 8, True),
        (-8, 1, lane >= 120, True),
        (1, 0, row == 0, True),
        (-1, 0, row == 31, True),
        (1, 1, (lane & 7) == 0, False),
        (-1, 1, (lane & 7) == 7, False),
    )
    diagonal = jnp.full(shape, SIGMA * scale, F32)
    pulls = []
    for shift, axis, edge, masked in moves:
        weight = (0.5 * scale) * (k + jnp.where(edge, 0.0, turn(k, shift, axis)))
        diagonal = diagonal + weight
        keep = jnp.where(edge, 0.0, weight)
        if masked:
            keep = jnp.where(owned == turn(owned, shift, axis), keep, 0.0)
        pulls.append(keep)
    rd = 1.0 / diagonal
    pulls = [keep * rd for keep in pulls]
    g = b * rd
    first, steps = COARSE
    d = g * first
    x = d
    for keep, gain in steps:
        total = [pull * turn(x, move[0], move[1]) for pull, move in zip(pulls, moves)]
        near = (total[0] + total[1]) + (total[2] + total[3]) + (total[4] + total[5])
        d = keep * d + gain * ((g - x) + near)
        x = x + d
    return x


def fill_three(dst, gathered, first):
    for g in range(16):
        for c in range(4):
            part = gathered[g, first + c // 2, 4 * (c % 2) : 4 * (c % 2) + 4, :]
            dst[c, 4 * g : 4 * g + 4, :] = part


def solve_three(b_ref, k_ref, owned, s3, r3, t3):
    shape = (4, 64, 128)
    plane = lax.broadcasted_iota(jnp.int32, shape, 0)
    row = lax.broadcasted_iota(jnp.int32, shape, 1)
    lane = lanes(shape)
    edge_x = ((plane == 0) & (lane < 16), (plane == 3) & (lane >= 112))
    level = build(k_ref[...], 0.25**3, 16, None, edge_x, (row == 0, row == 63))
    b = b_ref[...]
    x = smooth(None, b, level, 16)
    s3[...] = remain(x, b, level, 16)
    flat = [
        jnp.concatenate([pair_rows(src, q, 0, 32) for q in range(4)], axis=1) for src in (s3, k_ref)
    ]
    fine = 0.125 * pair_dot(jnp.concatenate(flat, axis=0), r3[...])
    last = solve_last(fine[:32], fine[32:], owned[...])
    back = pair_dot(last, t3[...])
    for q in range(4):
        spread_rows(s3, q, 0, back[:, 128 * q : 128 * q + 128])
    s3[...] = smooth(x + s3[...], b, level, 16)


def rise_two(gx, gy, near, x2, s3, t2, e2, s2):
    for i in range(5):
        at = jnp.clip(gx - 2 + i, 0, 15)
        spread_rows(e2, i, 8, pair_dot(s3[at // 4], t2[at % 4]))
    e = e2[:, pl.ds(pl.multiple_of(gy * 8, 8), 24), :]
    level = tuple(near[number] for number in range(2, 7))
    x = jnp.where(level[4] > 0.0, x2 + e, 0.0)
    s2[...] = smooth(x, near[0], level, 32)


def rise_one(x1, b1, k1, inside, s2, t1, s1):
    flat = jnp.concatenate([s2[i, 4:20, :] for i in range(1, 4)], axis=0)
    back = pair_dot(flat, t1[...])
    for i in range(3):
        for q in range(4):
            spread_rows(s1, 4 * i + q, 0, back[16 * i : 16 * i + 16, 128 * q : 128 * q + 128])
    level = build(k1, 0.25, 64, inside)
    s1[...] = smooth(jnp.where(inside, x1 + s1[...], 0.0), b1, level, 64)


def spread_one(s1, low, high, t0, e0):
    flat = jnp.concatenate([s1[i, 4:28, :] for i in range(low, high)], axis=0)
    back = pair_dot(flat, t0[...])
    for i in range(high - low):
        for q in range(2):
            part = back[24 * i : 24 * i + 24, 128 * q : 128 * q + 128]
            spread_rows(e0, 2 * (low - 2 + i) + q, 4, part)
    e0[:, 0:4, :] = jnp.zeros((16, 4, 128), F32)
    e0[:, RY - 4 : RY, :] = jnp.zeros((16, 4, 128), F32)


def add_top(x0, e0, rd, x, low, high):
    def step(i, _):
        p = low + i * CHUNK
        c = (p - 2) // 2
        pair = (e0[pl.ds(c, 1)], e0[pl.ds(c + 1, 1)])
        correction = jnp.concatenate([pair[0], pair[0], pair[1], pair[1]], axis=0)
        at = pl.ds(p, CHUNK)
        x[at] = jnp.where(rd[at] > 0.0, x0[at] + correction, 0.0)
        return 0

    lax.fori_loop(0, (high - low) // CHUNK, step, 0)


def turn_kernel(
    pos, owned, three, near, x2low, x2high, one, left, right, below, above, b0, x0, wx, wy, wz, s, rd, r0, r3, t3, t2, t1, t0,
    k3, k1, xout, rout, x0n, b1n, east, west,
    b3, s3, e2, s2, x2s, b1s, s1, e0, d, x, rs
):
    gx, gy = pos[0], pos[1]
    fill_three(b3, three, 0)
    fill_three(k3, three, 2)
    solve_three(b3, k3, owned, s3, r3, t3)
    x2s[:, 0:8, :] = x2low[...]
    x2s[:, 8:16, :] = near[1, :, 8:16, :]
    x2s[:, 16:24, :] = x2high[...]
    rise_two(gx, gy, near, x2s[...], s3, t2, e2, s2)

    inside = within((12, 32, 128), gx * 8 - 8, gy * 16 - 8, 64, 128, 256)
    for number, dst in enumerate((b1s, s1, k1)):
        part = slice(32 + 12 * number, 44 + 12 * number)
        fill_one(dst, left[number], one[number], right[number], below[part], above[part])
    k1[...] = jnp.where(inside, k1[...], 0.0)
    rise_one(s1[...], b1s[...], k1[...], inside, s2, t1, s1)

    spread_one(s1, 2, 10, t0, e0)
    add_top(x0, e0, rd, x, 2, PX - 2)
    start, steps = SMOOTH
    sweep_top(x, wx, wy, wz, s, 4, PX - 4, open_top(b0, 0, rd, d, x))
    for (keep, gain), edge in zip(steps, (4, 6)):
        sweep_top(x, wx, wy, wz, s, edge, PX - edge, advance_top(keep, gain, b0, 0, rd, d, x))

    def residual(p, at, v, av):
        rout[pl.ds(p - 6, CHUNK)] = b0[at] - av

    sweep_top(x, wx, wy, wz, s, 6, PX - 6, residual)
    xout[...] = x[9 : PX - 9]

    def begin(i, _):
        at = pl.ds(6 + i * CHUNK, CHUNK)
        v = (rout[pl.ds(i * CHUNK, CHUNK)] * rd[at]) * start
        d[at] = v
        x[at] = v
        return 0

    lax.fori_loop(0, (PX - 12) // CHUNK, begin, 0)
    for keep, gain in steps:
        sweep_top(x, wx, wy, wz, s, 8, PX - 8, advance_top(keep, gain, rout, 6, rd, d, x))

    def again(p, at, v, av):
        d[at] = rout[pl.ds(p - 6, CHUNK)] - av

    sweep_top(x, wx, wy, wz, s, HX, HX + TX, again)
    x0n[...] = x[HX : HX + TX, HY : HY + TY, :]
    for c in range(8):
        rs[c] = d[HX + 2 * c] + d[HX + 1 + 2 * c]
    b1 = pair_planes(rs, 4, HY, 16, r0)
    b1n[...] = b1
    for side, plane in ((east, HX + TX - 4), (west, HX)):
        side[:, 0:16, :] = b1
        side[:, 16:48, :] = x[plane : plane + 4, HY : HY + TY, :]


def go_turn(*args):
    top, wide = (PX, RY, 128), (12, 32, 128)
    outs = [(4, 64, 128), wide, (TX + 2, RY, 128), (TX + 8, RY, 128), (TX, TY, 128), (4, 16, 128)]
    outs += [(4, 48, 128)] * 2
    scratch = [(4, 64, 128)] * 2 + [(5, 144, 128), (5, 24, 128), (5, 24, 128), wide, wide, (16, RY, 128)]
    return call(turn_kernel, outs, scratch + [top] * 2 + [(8, RY, 128)], *args)


def last_kernel(
    pos, owned, three, k3, near, b1, x1, k1, x0n, left, right, below, above, r, xbefore,
    b0, wx, wy, wz, s, rd, r3, t3, t2, t1, t0, xout, rout,
    b3, s3, e2, s2, s1, e0, d, x
):
    gx, gy = pos[0], pos[1]
    fill_three(b3, three, 0)
    solve_three(b3, k3, owned, s3, r3, t3)
    rise_two(gx, gy, near, near[1], s3, t2, e2, s2)
    inside = within((12, 32, 128), gx * 8 - 8, gy * 16 - 8, 64, 128, 256)
    rise_one(x1[...], b1[...], k1[...], inside, s2, t1, s1)

    spread_one(s1, 3, 9, t0, e0)
    low, high = HX - 4, HX + TX + 4
    x[low:HX, HY : HY + TY, :] = left[:, 16:48, :]
    x[HX : HX + TX, HY : HY + TY, :] = x0n[...]
    x[HX + TX : high, HY : HY + TY, :] = right[:, 16:48, :]
    x[low:high, HY - 8 : HY, :] = below[16:40]
    x[low:high, HY + TY : HY + TY + 8, :] = above[16:40]
    x[low:high, 0 : HY - 8, :] = jnp.zeros((high - low, HY - 8, 128), F32)
    x[low:high, RY - 4 : RY, :] = jnp.zeros((high - low, 4, 128), F32)
    add_top(x, e0, rd, x, low, high)
    sweep_top(x, wx, wy, wz, s, low, high, open_top(r, low, rd, d, x))
    for keep, gain in SMOOTH[1]:
        sweep_top(x, wx, wy, wz, s, 8, PX - 8, advance_top(keep, gain, r, low, rd, d, x))
    x[9 : PX - 9] = x[9 : PX - 9] + xbefore[...]

    def residual(p, at, v, av):
        d[at] = b0[at] - av

    sweep_top(x, wx, wy, wz, s, HX, HX + TX, residual)
    xout[...] = x[HX : HX + TX, HY : HY + TY, :]
    rout[...] = d[HX : HX + TX, HY : HY + TY, :]


def go_last(*args):
    top, wide, tile = (PX, RY, 128), (12, 32, 128), (TX, TY, 128)
    scratch = [(4, 64, 128)] * 2 + [(5, 144, 128), (5, 24, 128), wide, (16, RY, 128)]
    return call(last_kernel, [tile, tile], scratch + [top] * 2, *args)


def shift(value, axis, step):
    count = lax.axis_size(axis)
    return lax.ppermute(value, axis, [(i, (i + step) % count) for i in range(count)])


def gather(copies, axis):
    return lax.all_to_all(copies, axis, 0, 0, tiled=True)


def local(right_side, kappa, owners):
    pos = jnp.stack([lax.axis_index("gx"), lax.axis_index("gy")]).astype(jnp.int32)
    owned = jnp.repeat(jnp.repeat(owners.T, 2, 0), 8, 1).astype(F32)
    r0 = restrict_map(128)[128:384]
    r1, r2, r3 = restrict_map(64), restrict_map(32), restrict_map(16)
    t0 = prolong_map(128)[:, 128:384]
    t1, t3 = prolong_map(64), prolong_map(16)
    t2 = jnp.asarray(np.transpose(lane_map(32), (0, 2, 1)), BF16)

    mid = jnp.stack([right_side, kappa])
    left = shift(mid[:, TX - HX :], "gx", 1)
    right = shift(mid[:, :HX], "gx", -1)
    wide = jnp.concatenate([left, mid, right], axis=1)
    below = shift(wide[:, :, TY - HX :], "gy", 1)
    above = shift(wide[:, :, :HX], "gy", -1)
    b0, x0, wx, wy, wz, s, rd, one, two = go_down(pos, right_side, left, right, below, above, kappa, r0, r1)
    top = (wx, wy, wz, s, rd)
    left = shift(one, "gx", 1)
    right = shift(one, "gx", -1)
    two = gather(two, "gx")
    rows = jnp.swapaxes(two, 0, 1).reshape(-1, 8, 128)
    wide = jnp.concatenate([left, one, right], axis=1)
    below = shift(jnp.concatenate([rows, wide[:, :, 8:].reshape(-1, 8, 128)]), "gy", 1)
    above = shift(jnp.concatenate([rows, wide[:, :, :8].reshape(-1, 8, 128)]), "gy", -1)
    near, three, k2, x2 = go_mid(True, pos, two, below, above, None, r2)
    x2low = shift(x2, "gy", 1)
    x2high = shift(x2, "gy", -1)
    three = gather(three, "gy")
    k3, k1, xbefore, source, x0n, b1n, east, west = go_turn(
        pos, owned, three, near, x2low, x2high, one, left, right, below, above, b0, x0, *top,
        r0, r3, t3, t2, t1, t0
    )

    left = shift(east, "gx", 1)
    right = shift(west, "gx", -1)
    wide = jnp.concatenate([left[:, :16], b1n, right[:, :16]])
    below = shift(wide[:, 8:], "gy", 1)
    above = shift(wide[:, :8], "gy", -1)
    b1, x1, two = go_one(pos, b1n, left, right, below, above, k1, r1)
    two = gather(two, "gx")
    wide = jnp.concatenate([left[:, 16:], x0n, right[:, 16:]])
    below = shift(jnp.concatenate([two[:, 0], wide[:, 24:]]), "gy", 1)
    above = shift(jnp.concatenate([two[:, 0], wide[:, :8]]), "gy", -1)
    near, three = go_mid(False, pos, two, below, above, k2, r2)
    three = gather(three, "gy")
    field, residual = go_last(
        pos, owned, three, k3, near, b1, x1, k1, x0n, left, right, below, above, source, xbefore, b0,
        *top, r3, t3, t2, t1, t0
    )
    return field, residual


def solution(mesh):
    spec = P("gx", "gy", None)
    return jax.shard_map(
        local, mesh=mesh, in_specs=(spec, spec, P()), out_specs=(spec, spec), check_vma=False
    )
```

```python
import functools

import jax
import jax.numpy as jnp
from jax import lax
from jax.experimental import pallas as pl
from jax.experimental.pallas import tpu as pltpu
from jax.sharding import PartitionSpec as P

SIGMA = 0.02
F32 = jnp.float32
BF16 = jnp.bfloat16
TX, TY = 16, 32
HX = 10
HY = 12
PX, RY = TX + 2 * HX, TY + 2 * HY
CHUNK = 4
VMEM_BYTES = 56 * 1024 * 1024


def cheb_steps(degree, lower):
    centre = 0.5 * (2.0 + lower)
    half = 0.5 * (2.0 - lower)
    sharp = centre / half
    ratio = 1.0 / sharp
    steps = []
    for _ in range(degree - 1):
        nxt = 1.0 / (2.0 * sharp - ratio)
        steps.append((nxt * ratio, 2.0 * nxt / half))
        ratio = nxt
    return 1.0 / centre, steps


SMOOTH = cheb_steps(3, 0.3)
COARSE = cheb_steps(24, 0.05)


def lane_match(z, q, source, target):
    cell = (source // z + (128 // z) * q) // 2
    return jnp.where(cell * (z // 2) + (source % z) // 2 == target, 1.0, 0.0).astype(BF16)


def restrict_map(z, planes=(0, 4)):
    shape = ((planes[1] - planes[0]) * 128, 128)
    row = lax.broadcasted_iota(jnp.int32, shape, 0)
    return lane_match(z, planes[0] + row // 128, row % 128, lanes(shape))


def prolong_map(z, planes=(0, 4)):
    shape = (128, (planes[1] - planes[0]) * 128)
    column = lanes(shape)
    target = lax.broadcasted_iota(jnp.int32, shape, 0)
    return lane_match(z, planes[0] + column // 128, column % 128, target)


def prolong_one(z, q):
    shape = (128, 128)
    return lane_match(z, q, lanes(shape), lax.broadcasted_iota(jnp.int32, shape, 0))


def pair_dot(value, matrix):
    high = value.astype(BF16)
    rest = value - high.astype(F32)
    mid = rest.astype(BF16)
    low = (rest - mid.astype(F32)).astype(BF16)
    dot = functools.partial(jnp.dot, preferred_element_type=F32)
    return dot(high, matrix) + (dot(mid, matrix) + dot(low, matrix))


def lanes(shape):
    return lax.broadcasted_iota(jnp.int32, shape, len(shape) - 1)


def turn(value, shift, axis):
    return pltpu.roll(value, shift % value.shape[axis], axis)


def next_x(v, z):
    if z == 128:
        return jnp.concatenate([v[1:], v[:1]], axis=0)
    a = turn(v, -z, 2)
    b = jnp.concatenate([a[1:], a[:1]], axis=0)
    return jnp.where(lanes(v.shape) < 128 - z, a, b)


def prev_x(v, z):
    if z == 128:
        return jnp.concatenate([v[-1:], v[:-1]], axis=0)
    a = turn(v, z, 2)
    b = jnp.concatenate([a[-1:], a[:-1]], axis=0)
    return jnp.where(lanes(v.shape) >= z, a, b)


def faces_of(k, step, scale, low, high):
    own = (0.5 * scale) * k
    both = own + (0.5 * scale) * step
    if low is None:
        return both, None
    edge = jnp.where(low | high, own, 0.0)
    return jnp.where(high, 0.0, both), edge


def build(k, scale, z, inside=None, edge_x=(None, None), edge_y=(None, None)):
    shape = k.shape
    cell = lanes(shape) & (z - 1)
    wx, ex = faces_of(k, next_x(k, z), scale, *edge_x)
    wy, ey = faces_of(k, turn(k, -1, 1), scale, *edge_y)
    wz, ez = faces_of(k, turn(k, -1, 2), scale, cell == 0, cell == z - 1)
    s = ez + SIGMA * scale
    if ex is not None:
        s = s + ex
    if ey is not None:
        s = s + ey
    diagonal = s + wx + prev_x(wx, z) + wy + turn(wy, 1, 1) + wz + turn(wz, 1, 2)
    rd = 1.0 / diagonal
    if inside is not None:
        rd = jnp.where(inside, rd, 0.0)
    return wx, wy, wz, s, rd


def remain(v, b, level, z):
    wx, wy, wz, s, _ = level
    fx = wx * (next_x(v, z) - v)
    fy = wy * (turn(v, -1, 1) - v)
    fz = wz * (turn(v, -1, 2) - v)
    total = (fx - prev_x(fx, z)) + (fy - turn(fy, 1, 1)) + (fz - turn(fz, 1, 2))
    return (b - s * v) + total


def smooth(x, b, level, z):
    first, steps = SMOOTH
    rd = level[4]
    if x is None:
        d = (b * rd) * first
        x = d
    else:
        d = (remain(x, b, level, z) * rd) * first
        x = x + d
    for keep, gain in steps:
        d = keep * d + gain * (remain(x, b, level, z) * rd)
        x = x + d
    return x


def within(shape, first_x, first_y, z, size_x, size_y):
    plane = lax.broadcasted_iota(jnp.int32, shape, 0)
    cx = first_x + plane * (128 // z) + lanes(shape) // z
    cy = first_y + lax.broadcasted_iota(jnp.int32, shape, 1)
    return (cx >= 0) & (cx < size_x) & (cy >= 0) & (cy < size_y)


def pair_rows(ref, plane, start, count):
    return ref[plane, pl.ds(start, count, stride=2), :] + ref[plane, pl.ds(start + 1, count, stride=2), :]


def spread_rows(ref, plane, start, value):
    count = value.shape[0]
    ref[plane, pl.ds(start, count, stride=2), :] = value
    ref[plane, pl.ds(start + 1, count, stride=2), :] = value


def insider(rows, first_x, first_y):
    row = lax.broadcasted_iota(jnp.int32, (CHUNK, rows, 128), 1) + first_y
    row_in = (row >= 0) & (row < 512)
    plane = lax.broadcasted_iota(jnp.int32, (CHUNK, rows, 128), 0) + first_x
    return lambda p: row_in & (plane >= -p) & (plane < 256 - p)


def build_top(k_ref, wx, wy, wz, s, rd, low, high, inside_at, body):
    rows = k_ref.shape[1]
    shape = (CHUNK, rows, 128)
    lane = lanes(shape)

    def step(i, wxp):
        p = low + i * CHUNK
        k = k_ref[pl.ds(p, CHUNK)]
        kn = jnp.concatenate([k[1:], k_ref[pl.ds(jnp.minimum(p + CHUNK, k_ref.shape[0] - 1), 1)]], axis=0)
        own = 0.5 * k
        fx = 0.5 * kn + own
        fy = turn(own, -1, 1) + own
        fz = jnp.where(lane == 127, 0.0, turn(own, -1, 2) + own)
        sv = SIGMA + jnp.where((lane == 0) | (lane == 127), own, 0.0)
        fxp = jnp.concatenate([wxp, fx[:-1]], axis=0)
        diagonal = sv + (fx + fxp) + (fy + turn(fy, 1, 1)) + (fz + turn(fz, 1, 2))
        rdv = jnp.where(inside_at(p), 1.0 / diagonal, 0.0)
        at = pl.ds(p, CHUNK)
        wx[at], wy[at], wz[at], s[at], rd[at] = fx, fy, fz, sv, rdv
        body(p, rdv)
        return fx[-1:]

    assert (high - low) % CHUNK == 0
    lax.fori_loop(0, (high - low) // CHUNK, step, jnp.zeros((1, rows, 128), F32))


def sweep_top(x, wx, wy, wz, s, low, high, body):
    fx0 = wx[low - 1 : low] * (x[low : low + 1] - x[low - 1 : low])

    def step(i, fxp):
        p = low + i * CHUNK
        at = pl.ds(p, CHUNK)
        v = x[at]
        vn = jnp.concatenate([v[1:], x[pl.ds(p + CHUNK, 1)]], axis=0)
        fx = wx[at] * (vn - v)
        fy = wy[at] * (turn(v, -1, 1) - v)
        fz = wz[at] * (turn(v, -1, 2) - v)
        fxp = jnp.concatenate([fxp, fx[:-1]], axis=0)
        total = (fx - fxp) + (fy - turn(fy, 1, 1)) + (fz - turn(fz, 1, 2))
        body(p, at, v, s[at] * v - total)
        return fx[-1:]

    assert (high - low) % CHUNK == 0
    lax.fori_loop(0, (high - low) // CHUNK, step, fx0)


def fill_top(dst, tile, left, right, below, above):
    dst[:, 0:2, :] = jnp.zeros((PX, 2, 128), F32)
    dst[:, RY - 2 : RY, :] = jnp.zeros((PX, 2, 128), F32)
    dst[0:HX, HY : HY + TY, :] = left
    dst[HX : HX + TX, HY : HY + TY, :] = tile
    dst[HX + TX :, HY : HY + TY, :] = right
    dst[:, 2:HY, :] = below
    dst[:, HY + TY : RY - 2, :] = above


def down_kernel(pos, tile, left, right, below, above, ktile, one, two, *refs):
    given, (bx, x, wx, wy, wz, s, rd), (kx, d, rs, b1s, x1s, k1s, sems) = refs[:7], refs[7:14], refs[14:]
    gx, gy = pos[0], pos[1]
    inside_at = insider(RY, gx * TX - HX, gy * TY - HY)
    fill_top(bx, tile[...], left[0], right[0], below[0], above[0])
    fill_top(kx, ktile[...], left[1], right[1], below[1], above[1])

    def clear(i, _):
        at = pl.ds(i * CHUNK, CHUNK)
        kx[at] = jnp.where(inside_at(i * CHUNK), kx[at], 0.0)
        return 0

    lax.fori_loop(0, PX // CHUNK, clear, 0)
    start, steps = SMOOTH

    def begin(p, rdv):
        at = pl.ds(p, CHUNK)
        v = (bx[at] * rdv) * start
        d[at] = v
        x[at] = v

    build_top(kx, wx, wy, wz, s, rd, 0, PX, inside_at, begin)
    keeping = moves((bx, x, wx, wy, wz, s, rd), given, sems)
    for move in keeping[:1] + keeping[2:]:
        move.start()
    for keep, gain in steps:
        sweep_top(x, wx, wy, wz, s, 2, PX - 2, advance_top(keep, gain, bx, 0, rd, d, x))

    def residual(p, at, v, av):
        d[at] = bx[at] - av

    keeping[1].start()
    sweep_top(x, wx, wy, wz, s, 4, PX - 4, residual)

    def coarse(src):
        for c in range(16):
            rs[c] = src[2 + 2 * c] + src[3 + 2 * c]
        return pair_planes(rs, 8, 4, 24)

    for p in (2, 3, PX - 4, PX - 3):
        d[p] = jnp.zeros((RY, 128), F32)
    b1 = coarse(d)
    k1 = coarse(kx)
    level = build(k1, 0.25, 64, within(k1.shape, gx * 8 - 4, gy * 16 - 4, 64, 128, 256))
    x1 = smooth(None, b1, level, 64)
    b1s[...] = b1
    x1s[...] = x1
    k1s[...] = k1
    for number, src in enumerate((b1s, x1s, k1s)):
        one[number] = src[2:6, 4:20, :]
    b1s[...] = remain(x1, b1, level, 64)
    send_all(two, coarse_tile((b1s, k1s), 2, 4))
    for move in keeping:
        move.wait()


def moves(sources, targets, sems):
    return [pltpu.make_async_copy(a, b, sems.at[i]) for i, (a, b) in enumerate(zip(sources, targets))]


def pair_planes(rs, planes, start, rows):
    flat = [
        jnp.concatenate([pair_rows(rs, 2 * c, start, rows), pair_rows(rs, 2 * c + 1, start, rows)], axis=1)
        for c in range(planes)
    ]
    out = 0.125 * pair_dot(jnp.concatenate(flat, axis=0), restrict_map(128, (1, 3)))
    return out.reshape(planes, rows, 128)


def coarse_tile(sources, plane, row):
    flat = [
        jnp.concatenate([pair_rows(src, plane + q, row, 8) for q in range(4)], axis=1) for src in sources
    ]
    out = 0.125 * pair_dot(jnp.concatenate(flat, axis=0), restrict_map(64))
    return out.reshape(len(sources), 8, 128)


def send_all(out, value):
    for g in range(16):
        out[g] = value


def advance_top(keep, gain, b, shift_b, rd, d, x):
    def advance(p, at, v, av):
        dv = keep * d[at] + gain * ((b[pl.ds(p - shift_b, CHUNK)] - av) * rd[at])
        d[at] = dv
        x[at] = v + dv

    return advance


def open_top(b, shift_b, rd, d, x):
    def advance(p, at, v, av):
        dv = ((b[pl.ds(p - shift_b, CHUNK)] - av) * rd[at]) * SMOOTH[0]
        d[at] = dv
        x[at] = v + dv

    return advance


def call(kernel, outs, scratch, *args, far_in=0, far_out=0, copies=0):
    near, far = pl.BlockSpec(memory_space=pltpu.VMEM), pl.BlockSpec(memory_space=pl.ANY)
    specs = [pl.BlockSpec(memory_space=pltpu.SMEM)] + [near] * (len(args) - 1 - far_in) + [far] * far_in
    return pl.pallas_call(
        kernel,
        out_shape=[jax.ShapeDtypeStruct(o, F32) for o in outs],
        in_specs=specs,
        out_specs=[near] * (len(outs) - far_out) + [far] * far_out,
        scratch_shapes=[pltpu.VMEM(o, F32) for o in scratch]
        + ([pltpu.SemaphoreType.DMA((copies,))] if copies else []),
        compiler_params=pltpu.CompilerParams(vmem_limit_bytes=VMEM_BYTES),
        cost_estimate=pl.CostEstimate(flops=10**7, bytes_accessed=8 << 20, transcendentals=0),
    )(*args)


def go_down(*args):
    top = (PX, RY, 128)
    outs = [(3, 4, 16, 128), (16, 2, 8, 128)] + [top] * 7
    scratch = [top] * 9 + [(16, RY, 128)] + [(8, 24, 128)] * 3
    return call(down_kernel, outs, scratch, *args, far_out=7, copies=7)


def one_kernel(pos, mid, left, right, below, above, k1, bout, xout, two, res):
    gx, gy = pos[0], pos[1]
    fill_one(bout, left[:, 0:16], mid[...], right[:, 0:16], below[...], above[...])
    b = bout[...]
    inside = within(b.shape, gx * 8 - 8, gy * 16 - 8, 64, 128, 256)
    level = build(k1[...], 0.25, 64, inside)
    x = smooth(None, b, level, 64)
    xout[...] = x
    res[...] = remain(x, b, level, 64)
    send_all(two, coarse_tile((res,), 4, 8))


def fill_one(dst, left, tile, right, below, above):
    dst[0:4, 8:24, :] = left
    dst[4:8, 8:24, :] = tile
    dst[8:12, 8:24, :] = right
    dst[:, 0:8, :] = below
    dst[:, 24:32, :] = above


def go_one(*args):
    wide = (12, 32, 128)
    return call(one_kernel, [wide, wide, (16, 1, 8, 128)], [wide], *args)


def mid_kernel(first, pos, mid, below, above, *refs):
    if first:
        near, three, k2 = refs[:3]
        scratch = refs[3:]
    else:
        k2, near, three = refs[:3]
        scratch = refs[3:]
    hold, rs, cs, edge = scratch
    gx, gy = pos[0], pos[1]
    shape = (16, 24, 128)
    inside = within(shape, 0, gy * 8 - 8, 32, 64, 128)

    def rows(dst, number):
        part = slice(16 * number, 16 * number + 16)
        dst[:, 0:8, :] = below[part]
        dst[:, 8:16, :] = mid[:, number]
        dst[:, 16:24, :] = above[part]

    rows(rs, 0)
    b = rs[...]
    if first:
        rows(k2, 1)
        k2[...] = jnp.where(inside, k2[...], 0.0)
    k = k2[...]
    plane = lax.broadcasted_iota(jnp.int32, shape, 0)
    lane = lanes(shape)
    edge_x = ((plane == 0) & (lane < 32), (plane == 15) & (lane >= 96))
    level = build(k, 0.25**2, 32, inside, edge_x)
    x = smooth(None, b, level, 32)
    rs[...] = remain(x, b, level, 32)
    for number, value in enumerate((b, x) + level):
        hold[number] = value
    for i in range(5):
        at = gx - 2 + i
        ok = (at >= 0) & (at < 16)
        from_plane = jnp.clip(at, 0, 15)
        for number in range(7):
            near[number, i] = jnp.where(ok, hold[number, from_plane], 0.0)

    if first:
        for i in range(5):
            edge[0, i : i + 1, :] = near[1, i, 9:10, :]
            edge[1, i : i + 1, :] = near[1, i, 14:15, :]
        upper = lax.rem(gy + 1, 16)
        for g in range(16):
            three[g, 4] = jnp.where(upper == g, edge[0], edge[1])

    def coarse(src, out):
        flat = [
            jnp.concatenate([pair_rows(src, 4 * c + q, 4, 8) for q in range(4)], axis=1) for c in range(4)
        ]
        cs[...] = (0.125 * pair_dot(jnp.concatenate(flat, axis=0), restrict_map(32))).reshape(4, 8, 128)
        for c in range(4):
            part = cs[c, 2:6, :]
            for g in range(16):
                three[g, out + c // 2, 4 * (c % 2) : 4 * (c % 2) + 4, :] = part

    coarse(rs, 0)
    if first:
        coarse(k2, 2)


def go_mid(first, pos, mid, below, above, k2):
    outs = [(7, 5, 24, 128), (16, 5 if first else 2, 8, 128)]
    outs += [(16, 24, 128)] if first else []
    scratch = [(7, 16, 24, 128), (16, 24, 128), (4, 8, 128), (2, 8, 128)]
    args = (mid, below, above) + (() if first else (k2,))
    return call(functools.partial(mid_kernel, first), outs, scratch, pos, *args)


def solve_last(b, k, owned):
    shape = k.shape
    scale = 0.25**4
    lane = lanes(shape)
    row = lax.broadcasted_iota(jnp.int32, shape, 0)
    moves = (
        (8, 1, lane < 8, True),
        (-8, 1, lane >= 120, True),
        (1, 0, row == 0, True),
        (-1, 0, row == 31, True),
        (1, 1, (lane & 7) == 0, False),
        (-1, 1, (lane & 7) == 7, False),
    )
    diagonal = jnp.full(shape, SIGMA * scale, F32)
    pulls = []
    for shift, axis, edge, masked in moves:
        weight = (0.5 * scale) * (k + jnp.where(edge, 0.0, turn(k, shift, axis)))
        diagonal = diagonal + weight
        keep = jnp.where(edge, 0.0, weight)
        if masked:
            keep = jnp.where(owned == turn(owned, shift, axis), keep, 0.0)
        pulls.append(keep)
    rd = 1.0 / diagonal
    pulls = [keep * rd for keep in pulls]
    g = b * rd
    first, steps = COARSE
    d = g * first
    x = d
    for keep, gain in steps:
        total = [pull * turn(x, move[0], move[1]) for pull, move in zip(pulls, moves)]
        near = (total[0] + total[1]) + (total[2] + total[3]) + (total[4] + total[5])
        d = keep * d + gain * ((g - x) + near)
        x = x + d
    return x


def fill_three(dst, gathered, first):
    for g in range(16):
        for c in range(4):
            part = gathered[g, first + c // 2, 4 * (c % 2) : 4 * (c % 2) + 4, :]
            dst[c, 4 * g : 4 * g + 4, :] = part


def solve_three(b_ref, k_ref, owned, s3):
    shape = (4, 64, 128)
    plane = lax.broadcasted_iota(jnp.int32, shape, 0)
    row = lax.broadcasted_iota(jnp.int32, shape, 1)
    lane = lanes(shape)
    edge_x = ((plane == 0) & (lane < 16), (plane == 3) & (lane >= 112))
    level = build(k_ref[...], 0.25**3, 16, None, edge_x, (row == 0, row == 63))
    b = b_ref[...]
    x = smooth(None, b, level, 16)
    s3[...] = remain(x, b, level, 16)
    flat = [
        jnp.concatenate([pair_rows(src, q, 0, 32) for q in range(4)], axis=1) for src in (s3, k_ref)
    ]
    fine = 0.125 * pair_dot(jnp.concatenate(flat, axis=0), restrict_map(16))
    last = solve_last(fine[:32], fine[32:], owned[...])
    back = pair_dot(last, prolong_map(16))
    for q in range(4):
        spread_rows(s3, q, 0, back[:, 128 * q : 128 * q + 128])
    s3[...] = smooth(x + s3[...], b, level, 16)


def rise_two(gx, gy, near, x2, s3, e2, s2):
    for i in range(5):
        at = jnp.clip(gx - 2 + i, 0, 15)
        spread_rows(e2, i, 8, pair_dot(s3[at // 4], prolong_one(32, at % 4)))
    e = e2[:, pl.ds(pl.multiple_of(gy * 8, 8), 24), :]
    level = tuple(near[number] for number in range(2, 7))
    x = jnp.where(level[4] > 0.0, x2 + e, 0.0)
    s2[...] = smooth(x, near[0], level, 32)


def rise_one(x1, b1, k1, inside, s2, s1):
    flat = jnp.concatenate([s2[i, 4:20, :] for i in range(1, 4)], axis=0)
    back = pair_dot(flat, prolong_map(64))
    for i in range(3):
        for q in range(4):
            spread_rows(s1, 4 * i + q, 0, back[16 * i : 16 * i + 16, 128 * q : 128 * q + 128])
    level = build(k1, 0.25, 64, inside)
    s1[...] = smooth(jnp.where(inside, x1 + s1[...], 0.0), b1, level, 64)


def spread_one(s1, low, high, e0):
    flat = jnp.concatenate([s1[i, 4:28, :] for i in range(low, high)], axis=0)
    back = pair_dot(flat, prolong_map(128, (1, 3)))
    for i in range(high - low):
        for q in range(2):
            part = back[24 * i : 24 * i + 24, 128 * q : 128 * q + 128]
            spread_rows(e0, 2 * (low - 2 + i) + q, 4, part)
    e0[:, 0:4, :] = jnp.zeros((16, 4, 128), F32)
    e0[:, RY - 4 : RY, :] = jnp.zeros((16, 4, 128), F32)


def add_top(x0, e0, rd, x, low, high):
    def step(i, _):
        p = low + i * CHUNK
        c = (p - 2) // 2
        pair = (e0[pl.ds(c, 1)], e0[pl.ds(c + 1, 1)])
        correction = jnp.concatenate([pair[0], pair[0], pair[1], pair[1]], axis=0)
        at = pl.ds(p, CHUNK)
        x[at] = jnp.where(rd[at] > 0.0, x0[at] + correction, 0.0)
        return 0

    lax.fori_loop(0, (high - low) // CHUNK, step, 0)


def turn_kernel(
    pos, owned, three, near, one, left, right, below, above, *refs
):
    gx, gy = pos[0], pos[1]
    fars, (x0n, b1n, east, west, *far_outs) = refs[:7], refs[7:15]
    b3, s3, e2, s2, x2s, b1s, s1, e0, d, x, rs, xout, rout, k3, k1 = refs[15:30]
    tops, sems = refs[30:37], refs[37]
    b0, x0, wx, wy, wz, s, rd = tops
    loads = moves(fars, tops, sems)
    for move in loads:
        move.start()
    xkeep, rkeep, kkeep, k1keep = (
        pltpu.make_async_copy(a, b, sems.at[7 + i]) for i, (a, b) in enumerate(zip((xout, rout, k3, k1), far_outs))
    )
    fill_three(b3, three, 0)
    fill_three(k3, three, 2)
    kkeep.start()
    solve_three(b3, k3, owned, s3)
    x2s[...] = near[1]
    lower, upper = lax.rem(gy + 15, 16), lax.rem(gy + 1, 16)
    for i in range(5):
        x2s[i, 1:2, :] = three[lower, 4, i : i + 1, :]
        x2s[i, 22:23, :] = three[upper, 4, i : i + 1, :]
    rise_two(gx, gy, near, x2s[...], s3, e2, s2)

    inside = within((12, 32, 128), gx * 8 - 8, gy * 16 - 8, 64, 128, 256)
    for number, dst in enumerate((b1s, s1, k1)):
        part = slice(32 + 12 * number, 44 + 12 * number)
        fill_one(dst, left[number], one[number], right[number], below[part], above[part])
    k1[...] = jnp.where(inside, k1[...], 0.0)
    k1keep.start()
    rise_one(s1[...], b1s[...], k1[...], inside, s2, s1)

    spread_one(s1, 2, 10, e0)
    for move in loads:
        move.wait()
    add_top(x0, e0, rd, x, 2, PX - 2)
    start, steps = SMOOTH
    sweep_top(x, wx, wy, wz, s, 4, PX - 4, open_top(b0, 0, rd, d, x))
    for (keep, gain), edge in zip(steps, (4, 6)):
        sweep_top(x, wx, wy, wz, s, edge, PX - edge, advance_top(keep, gain, b0, 0, rd, d, x))

    def residual(p, at, v, av):
        rout[pl.ds(p - 6, CHUNK)] = b0[at] - av

    sweep_top(x, wx, wy, wz, s, 6, PX - 6, residual)
    xout[...] = x[9 : PX - 9]
    xkeep.start()
    rkeep.start()

    def begin(i, _):
        at = pl.ds(6 + i * CHUNK, CHUNK)
        v = (rout[pl.ds(i * CHUNK, CHUNK)] * rd[at]) * start
        d[at] = v
        x[at] = v
        return 0

    lax.fori_loop(0, (PX - 12) // CHUNK, begin, 0)
    for keep, gain in steps:
        sweep_top(x, wx, wy, wz, s, 8, PX - 8, advance_top(keep, gain, rout, 6, rd, d, x))

    def again(p, at, v, av):
        d[at] = rout[pl.ds(p - 6, CHUNK)] - av

    sweep_top(x, wx, wy, wz, s, HX, HX + TX, again)
    x0n[...] = x[HX : HX + TX, HY : HY + TY, :]
    for c in range(8):
        rs[c] = d[HX + 2 * c] + d[HX + 1 + 2 * c]
    b1 = pair_planes(rs, 4, HY, 16)
    b1n[...] = b1
    for side, plane in ((east, HX + TX - 4), (west, HX)):
        side[:, 0:16, :] = b1
        side[:, 16:48, :] = x[plane : plane + 4, HY : HY + TY, :]
    for move in (xkeep, rkeep, kkeep, k1keep):
        move.wait()


def go_turn(*args):
    top, wide, three = (PX, RY, 128), (12, 32, 128), (4, 64, 128)
    kept = [(TX + 2, RY, 128), (TX + 8, RY, 128), three, wide]
    outs = [(TX, TY, 128), (4, 16, 128), (4, 48, 128), (4, 48, 128)] + kept
    scratch = [three] * 2 + [(5, 144, 128), (5, 24, 128), (5, 24, 128), wide, wide, (16, RY, 128)]
    scratch += [top] * 2 + [(8, RY, 128)] + kept + [top] * 7
    return call(turn_kernel, outs, scratch, *args, far_in=7, far_out=4, copies=11)


def last_kernel(
    pos, owned, three, k3, near, b1, x1, k1, x0n, left, right, below, above, *refs
):
    gx, gy = pos[0], pos[1]
    fars, (xout, rout), (b3, s3, e2, s2, s1, e0, d, x) = refs[:8], refs[8:10], refs[10:18]
    tops, sems = refs[18:26], refs[26]
    r, xbefore, b0, wx, wy, wz, s, rd = tops
    loads = moves(fars, tops, sems)
    for move in loads:
        move.start()
    fill_three(b3, three, 0)
    solve_three(b3, k3, owned, s3)
    rise_two(gx, gy, near, near[1], s3, e2, s2)
    inside = within((12, 32, 128), gx * 8 - 8, gy * 16 - 8, 64, 128, 256)
    rise_one(x1[...], b1[...], k1[...], inside, s2, s1)

    spread_one(s1, 3, 9, e0)
    low, high = HX - 4, HX + TX + 4
    x[low:HX, HY : HY + TY, :] = left[:, 16:48, :]
    x[HX : HX + TX, HY : HY + TY, :] = x0n[...]
    x[HX + TX : high, HY : HY + TY, :] = right[:, 16:48, :]
    x[low:high, HY - 8 : HY, :] = below[16:40]
    x[low:high, HY + TY : HY + TY + 8, :] = above[16:40]
    x[low:high, 0 : HY - 8, :] = jnp.zeros((high - low, HY - 8, 128), F32)
    x[low:high, RY - 4 : RY, :] = jnp.zeros((high - low, 4, 128), F32)
    for move in loads:
        move.wait()
    add_top(x, e0, rd, x, low, high)
    sweep_top(x, wx, wy, wz, s, low, high, open_top(r, low, rd, d, x))
    for keep, gain in SMOOTH[1]:
        sweep_top(x, wx, wy, wz, s, 8, PX - 8, advance_top(keep, gain, r, low, rd, d, x))
    x[9 : PX - 9] = x[9 : PX - 9] + xbefore[...]

    def residual(p, at, v, av):
        d[at] = b0[at] - av

    sweep_top(x, wx, wy, wz, s, HX, HX + TX, residual)
    xout[...] = x[HX : HX + TX, HY : HY + TY, :]
    rout[...] = d[HX : HX + TX, HY : HY + TY, :]


def go_last(*args):
    top, wide, tile = (PX, RY, 128), (12, 32, 128), (TX, TY, 128)
    scratch = [(4, 64, 128)] * 2 + [(5, 144, 128), (5, 24, 128), wide, (16, RY, 128)] + [top] * 2
    scratch += [(TX + 8, RY, 128), (TX + 2, RY, 128)] + [top] * 6
    return call(last_kernel, [tile, tile], scratch, *args, far_in=8, copies=8)


def shift(value, axis, step):
    count = lax.axis_size(axis)
    return lax.ppermute(value, axis, [(i, (i + step) % count) for i in range(count)])


def gather(copies, axis):
    return lax.all_to_all(copies, axis, 0, 0, tiled=True)


def local(right_side, kappa, owners):
    pos = jnp.stack([lax.axis_index("gx"), lax.axis_index("gy")]).astype(jnp.int32)
    owned = jnp.repeat(jnp.repeat(owners.T, 2, 0), 8, 1).astype(F32)
    mid = jnp.stack([right_side, kappa])
    left = shift(mid[:, TX - HX :], "gx", 1)
    right = shift(mid[:, :HX], "gx", -1)
    wide = jnp.concatenate([left, mid, right], axis=1)
    below = shift(wide[:, :, TY - HX :], "gy", 1)
    above = shift(wide[:, :, :HX], "gy", -1)
    one, two, b0, x0, *top = go_down(pos, right_side, left, right, below, above, kappa)
    left = shift(one, "gx", 1)
    right = shift(one, "gx", -1)
    two = gather(two, "gx")
    rows = jnp.swapaxes(two, 0, 1).reshape(-1, 8, 128)
    wide = jnp.concatenate([left, one, right], axis=1)
    below = shift(jnp.concatenate([rows, wide[:, :, 8:].reshape(-1, 8, 128)]), "gy", 1)
    above = shift(jnp.concatenate([rows, wide[:, :, :8].reshape(-1, 8, 128)]), "gy", -1)
    near, three, k2 = go_mid(True, pos, two, below, above, None)
    three = gather(three, "gy")
    x0n, b1n, east, west, xbefore, source, k3, k1 = go_turn(
        pos, owned, three, near, one, left, right, below, above, b0, x0, *top
    )

    left = shift(east, "gx", 1)
    right = shift(west, "gx", -1)
    wide = jnp.concatenate([left[:, :16], b1n, right[:, :16]])
    below = shift(wide[:, 8:], "gy", 1)
    above = shift(wide[:, :8], "gy", -1)
    b1, x1, two = go_one(pos, b1n, left, right, below, above, k1)
    two = gather(two, "gx")
    wide = jnp.concatenate([left[:, 16:], x0n, right[:, 16:]])
    below = shift(jnp.concatenate([two[:, 0], wide[:, 24:]]), "gy", 1)
    above = shift(jnp.concatenate([two[:, 0], wide[:, :8]]), "gy", -1)
    near, three = go_mid(False, pos, two, below, above, k2)
    three = gather(three, "gy")
    field, residual = go_last(
        pos, owned, three, k3, near, b1, x1, k1, x0n, left, right, below, above, source, xbefore, b0, *top
    )
    return field, residual


def solution(mesh):
    spec = P("gx", "gy", None)
    return jax.shard_map(
        local, mesh=mesh, in_specs=(spec, spec, P()), out_specs=(spec, spec), check_vma=False
    )
```

```python
import functools

import jax
import jax.numpy as jnp
from jax import lax
from jax.experimental import pallas as pl
from jax.experimental.pallas import tpu as pltpu
from jax.sharding import PartitionSpec as P

SIGMA = 0.02
F32 = jnp.float32
BF16 = jnp.bfloat16
TX, TY = 16, 32
HX = 10
HY = 12
PX, RY = TX + 2 * HX, TY + 2 * HY
CHUNK = 4
PARTS = 2
VMEM_BYTES = 56 * 1024 * 1024


def cheb_steps(degree, lower):
    centre = 0.5 * (2.0 + lower)
    half = 0.5 * (2.0 - lower)
    sharp = centre / half
    ratio = 1.0 / sharp
    steps = []
    for _ in range(degree - 1):
        nxt = 1.0 / (2.0 * sharp - ratio)
        steps.append((nxt * ratio, 2.0 * nxt / half))
        ratio = nxt
    return 1.0 / centre, steps


SMOOTH = cheb_steps(3, 0.3)
COARSE = cheb_steps(24, 0.05)


def lane_match(z, q, source, target):
    bits = z.bit_length() - 1
    cell = (lax.shift_right_logical(source, bits) + (128 // z) * q) & -2
    inner = lax.shift_right_logical(source & (z - 1), 1)
    return jnp.where(cell * (z // 4) + inner == target, 1.0, 0.0).astype(BF16)


def restrict_map(z, planes=(0, 4)):
    shape = ((planes[1] - planes[0]) * 128, 128)
    row = lax.broadcasted_iota(jnp.int32, shape, 0)
    return lane_match(z, planes[0] + lax.shift_right_logical(row, 7), row & 127, lanes(shape))


def prolong_map(z, planes=(0, 4)):
    shape = (128, (planes[1] - planes[0]) * 128)
    column = lanes(shape)
    target = lax.broadcasted_iota(jnp.int32, shape, 0)
    return lane_match(z, planes[0] + lax.shift_right_logical(column, 7), column & 127, target)


def prolong_one(z, q):
    shape = (128, 128)
    return lane_match(z, q, lanes(shape), lax.broadcasted_iota(jnp.int32, shape, 0))


def pair_dot(value, matrix):
    rows = value.shape[0]
    high = value.astype(BF16).astype(F32)
    rest = value - high
    mid = rest.astype(BF16).astype(F32)
    parts = jnp.concatenate([high, mid, rest - mid], axis=0).astype(BF16)
    out = jnp.dot(parts, matrix, preferred_element_type=F32)
    return out[:rows] + (out[rows : 2 * rows] + out[2 * rows :])


def lanes(shape):
    return lax.broadcasted_iota(jnp.int32, shape, len(shape) - 1)


def turn(value, shift, axis):
    return pltpu.roll(value, shift % value.shape[axis], axis)


def next_x(v, z):
    if z == 128:
        return jnp.concatenate([v[1:], v[:1]], axis=0)
    a = turn(v, -z, 2)
    b = jnp.concatenate([a[1:], a[:1]], axis=0)
    return jnp.where(lanes(v.shape) < 128 - z, a, b)


def prev_x(v, z):
    if z == 128:
        return jnp.concatenate([v[-1:], v[:-1]], axis=0)
    a = turn(v, z, 2)
    b = jnp.concatenate([a[-1:], a[:-1]], axis=0)
    return jnp.where(lanes(v.shape) >= z, a, b)


def faces_of(k, step, scale, low, high):
    own = (0.5 * scale) * k
    both = own + (0.5 * scale) * step
    if low is None:
        return both, None
    edge = jnp.where(low | high, own, 0.0)
    return jnp.where(high, 0.0, both), edge


def build(k, scale, z, inside=None, edge_x=(None, None), edge_y=(None, None)):
    shape = k.shape
    cell = lanes(shape) & (z - 1)
    wx, ex = faces_of(k, next_x(k, z), scale, *edge_x)
    wy, ey = faces_of(k, turn(k, -1, 1), scale, *edge_y)
    wz, ez = faces_of(k, turn(k, -1, 2), scale, cell == 0, cell == z - 1)
    s = ez + SIGMA * scale
    if ex is not None:
        s = s + ex
    if ey is not None:
        s = s + ey
    diagonal = s + wx + prev_x(wx, z) + wy + turn(wy, 1, 1) + wz + turn(wz, 1, 2)
    rd = 1.0 / diagonal
    if inside is not None:
        rd = jnp.where(inside, rd, 0.0)
    return wx, wy, wz, s, rd


def remain(v, b, level, z):
    wx, wy, wz, s, _ = level
    fx = wx * (next_x(v, z) - v)
    fy = wy * (turn(v, -1, 1) - v)
    fz = wz * (turn(v, -1, 2) - v)
    total = (fx - prev_x(fx, z)) + (fy - turn(fy, 1, 1)) + (fz - turn(fz, 1, 2))
    return (b - s * v) + total


def smooth(x, b, level, z):
    first, steps = SMOOTH
    rd = level[4]
    if x is None:
        d = (b * rd) * first
        x = d
    else:
        d = (remain(x, b, level, z) * rd) * first
        x = x + d
    for keep, gain in steps:
        d = keep * d + gain * (remain(x, b, level, z) * rd)
        x = x + d
    return x


def within(shape, first_x, first_y, z, size_x, size_y):
    plane = lax.broadcasted_iota(jnp.int32, shape, 0)
    cx = first_x + plane * (128 // z) + lax.shift_right_logical(lanes(shape), z.bit_length() - 1)
    cy = first_y + lax.broadcasted_iota(jnp.int32, shape, 1)
    return (cx >= 0) & (cx < size_x) & (cy >= 0) & (cy < size_y)


def pair_rows(ref, plane, start, count):
    return ref[plane, pl.ds(start, count, stride=2), :] + ref[plane, pl.ds(start + 1, count, stride=2), :]


def spread_rows(ref, plane, start, value):
    count = value.shape[0]
    ref[plane, pl.ds(start, count, stride=2), :] = value
    ref[plane, pl.ds(start + 1, count, stride=2), :] = value


def insider(rows, first_x, first_y):
    row = lax.broadcasted_iota(jnp.int32, (CHUNK, rows, 128), 1) + first_y
    row_in = (row >= 0) & (row < 512)
    plane = lax.broadcasted_iota(jnp.int32, (CHUNK, rows, 128), 0) + first_x
    return lambda p: row_in & (plane >= -p) & (plane < 256 - p)


def build_top(k_ref, wx, wy, wz, s, rd, low, high, inside_at, body):
    rows = k_ref.shape[1]
    shape = (CHUNK, rows, 128)
    lane = lanes(shape)

    def step(i, wxp):
        p = low + i * CHUNK
        k = k_ref[pl.ds(p, CHUNK)]
        kn = jnp.concatenate([k[1:], k_ref[pl.ds(jnp.minimum(p + CHUNK, k_ref.shape[0] - 1), 1)]], axis=0)
        own = 0.5 * k
        fx = 0.5 * kn + own
        fy = turn(own, -1, 1) + own
        fz = jnp.where(lane == 127, 0.0, turn(own, -1, 2) + own)
        sv = SIGMA + jnp.where((lane == 0) | (lane == 127), own, 0.0)
        fxp = jnp.concatenate([wxp, fx[:-1]], axis=0)
        diagonal = sv + (fx + fxp) + (fy + turn(fy, 1, 1)) + (fz + turn(fz, 1, 2))
        rdv = jnp.where(inside_at(p), 1.0 / diagonal, 0.0)
        at = pl.ds(p, CHUNK)
        wx[at], wy[at], wz[at], s[at], rd[at] = fx, fy, fz, sv, rdv
        body(p, rdv)
        return fx[-1:]

    assert (high - low) % CHUNK == 0
    lax.fori_loop(0, (high - low) // CHUNK, step, jnp.zeros((1, rows, 128), F32))


def sweep_top(x, wx, wy, wz, s, low, high, body):
    size = (high - low) // PARTS
    fx0 = wx[low - 1 : low] * (x[low : low + 1] - x[low - 1 : low])

    def step(i, fxp):
        p = low + i * size
        at = pl.ds(p, size)
        v = x[at]
        vn = jnp.concatenate([v[1:], x[pl.ds(p + size, 1)]], axis=0)
        fx = wx[at] * (vn - v)
        fy = wy[at] * (turn(v, -1, 1) - v)
        fz = wz[at] * (turn(v, -1, 2) - v)
        fxp = jnp.concatenate([fxp, fx[:-1]], axis=0)
        total = (fx - fxp) + (fy - turn(fy, 1, 1)) + (fz - turn(fz, 1, 2))
        body(p, at, v, s[at] * v - total)
        return fx[-1:]

    assert (high - low) % PARTS == 0
    lax.fori_loop(0, PARTS, step, fx0, unroll=True)


def fill_top(dst, tile, left, right, below, above):
    dst[:, 0:2, :] = jnp.zeros((PX, 2, 128), F32)
    dst[:, RY - 2 : RY, :] = jnp.zeros((PX, 2, 128), F32)
    dst[0:HX, HY : HY + TY, :] = left
    dst[HX : HX + TX, HY : HY + TY, :] = tile
    dst[HX + TX :, HY : HY + TY, :] = right
    dst[:, 2:HY, :] = below
    dst[:, HY + TY : RY - 2, :] = above


def down_kernel(pos, tile, left, right, below, above, ktile, one, two, *refs):
    given, (bx, kx, x, wx, wy, wz, s, rd, d, rs, b1s, x1s, k1s, sems) = refs[:3], refs[3:]
    keeping = moves((bx, kx, x), given, sems)
    gx, gy = pos[0], pos[1]
    inside_at = insider(RY, gx * TX - HX, gy * TY - HY)
    fill_top(bx, tile[...], left[0], right[0], below[0], above[0])
    fill_top(kx, ktile[...], left[1], right[1], below[1], above[1])

    def clear(i, _):
        at = pl.ds(i * CHUNK, CHUNK)
        kx[at] = jnp.where(inside_at(i * CHUNK), kx[at], 0.0)
        return 0

    lax.fori_loop(0, PX // CHUNK, clear, 0)
    for move in keeping[:2]:
        move.start()
    start, steps = SMOOTH

    def begin(p, rdv):
        at = pl.ds(p, CHUNK)
        v = (bx[at] * rdv) * start
        d[at] = v
        x[at] = v

    build_top(kx, wx, wy, wz, s, rd, 0, PX, inside_at, begin)
    for keep, gain in steps:
        sweep_top(x, wx, wy, wz, s, 2, PX - 2, advance_top(keep, gain, bx, 0, rd, d, x))

    def residual(p, at, v, av):
        d[at] = bx[at] - av

    keeping[2].start()
    sweep_top(x, wx, wy, wz, s, 4, PX - 4, residual)

    def coarse(src):
        for c in range(16):
            rs[c] = src[2 + 2 * c] + src[3 + 2 * c]
        return pair_planes(rs, 8, 4, 24)

    for p in (2, 3, PX - 4, PX - 3):
        d[p] = jnp.zeros((RY, 128), F32)
    b1 = coarse(d)
    k1 = coarse(kx)
    level = build(k1, 0.25, 64, within(k1.shape, gx * 8 - 4, gy * 16 - 4, 64, 128, 256))
    x1 = smooth(None, b1, level, 64)
    b1s[...] = b1
    x1s[...] = x1
    k1s[...] = k1
    for number, src in enumerate((b1s, x1s, k1s)):
        one[number] = src[2:6, 4:20, :]
    b1s[...] = remain(x1, b1, level, 64)
    send_all(two, coarse_tile((b1s, k1s), 2, 4))
    for move in keeping:
        move.wait()


def moves(sources, targets, sems):
    return [pltpu.make_async_copy(a, b, sems.at[i]) for i, (a, b) in enumerate(zip(sources, targets))]


def pair_planes(rs, planes, start, rows):
    flat = [
        jnp.concatenate([pair_rows(rs, 2 * c, start, rows), pair_rows(rs, 2 * c + 1, start, rows)], axis=1)
        for c in range(planes)
    ]
    out = 0.125 * pair_dot(jnp.concatenate(flat, axis=0), restrict_map(128, (1, 3)))
    return out.reshape(planes, rows, 128)


def coarse_tile(sources, plane, row):
    flat = [
        jnp.concatenate([pair_rows(src, plane + q, row, 8) for q in range(4)], axis=1) for src in sources
    ]
    out = 0.125 * pair_dot(jnp.concatenate(flat, axis=0), restrict_map(64))
    return out.reshape(len(sources), 8, 128)


def send_all(out, value):
    for g in range(16):
        out[g] = value


def advance_top(keep, gain, b, shift_b, rd, d, x):
    def advance(p, at, v, av):
        dv = keep * d[at] + gain * ((b[pl.ds(p - shift_b, v.shape[0])] - av) * rd[at])
        d[at] = dv
        x[at] = v + dv

    return advance


def open_top(b, shift_b, rd, d, x):
    def advance(p, at, v, av):
        dv = ((b[pl.ds(p - shift_b, v.shape[0])] - av) * rd[at]) * SMOOTH[0]
        d[at] = dv
        x[at] = v + dv

    return advance


def call(kernel, outs, scratch, *args, far_in=0, far_out=0, copies=0):
    near, far = pl.BlockSpec(memory_space=pltpu.VMEM), pl.BlockSpec(memory_space=pl.ANY)
    specs = [pl.BlockSpec(memory_space=pltpu.SMEM)] + [near] * (len(args) - 1 - far_in) + [far] * far_in
    return pl.pallas_call(
        kernel,
        out_shape=[jax.ShapeDtypeStruct(o, F32) for o in outs],
        in_specs=specs,
        out_specs=[near] * (len(outs) - far_out) + [far] * far_out,
        scratch_shapes=[pltpu.VMEM(o, F32) for o in scratch]
        + ([pltpu.SemaphoreType.DMA((copies,))] if copies else []),
        compiler_params=pltpu.CompilerParams(vmem_limit_bytes=VMEM_BYTES),
        cost_estimate=pl.CostEstimate(flops=10**7, bytes_accessed=8 << 20, transcendentals=0),
    )(*args)


def go_down(*args):
    top = (PX, RY, 128)
    outs = [(3, 4, 16, 128), (16, 2, 8, 128)] + [top] * 3
    scratch = [top] * 9 + [(16, RY, 128)] + [(8, 24, 128)] * 3
    return call(down_kernel, outs, scratch, *args, far_out=3, copies=3)


def one_kernel(pos, mid, left, right, below, above, k1, bout, xout, two, res):
    gx, gy = pos[0], pos[1]
    fill_one(bout, left[:, 0:16], mid[...], right[:, 0:16], below[...], above[...])
    b = bout[...]
    inside = within(b.shape, gx * 8 - 8, gy * 16 - 8, 64, 128, 256)
    level = build(k1[...], 0.25, 64, inside)
    x = smooth(None, b, level, 64)
    xout[...] = x
    res[...] = remain(x, b, level, 64)
    send_all(two, coarse_tile((res,), 4, 8))


def fill_one(dst, left, tile, right, below, above):
    dst[0:4, 8:24, :] = left
    dst[4:8, 8:24, :] = tile
    dst[8:12, 8:24, :] = right
    dst[:, 0:8, :] = below
    dst[:, 24:32, :] = above


def go_one(*args):
    wide = (12, 32, 128)
    return call(one_kernel, [wide, wide, (16, 1, 8, 128)], [wide], *args)


def mid_kernel(first, pos, mid, below, above, *refs):
    if first:
        near, three, k2 = refs[:3]
        scratch = refs[3:]
    else:
        k2, near, three = refs[:3]
        scratch = refs[3:]
    hold, rs, cs, edge = scratch
    gx, gy = pos[0], pos[1]
    shape = (16, 24, 128)
    inside = within(shape, 0, gy * 8 - 8, 32, 64, 128)

    def rows(dst, number):
        part = slice(16 * number, 16 * number + 16)
        dst[:, 0:8, :] = below[part]
        dst[:, 8:16, :] = mid[:, number]
        dst[:, 16:24, :] = above[part]

    rows(rs, 0)
    b = rs[...]
    if first:
        rows(k2, 1)
        k2[...] = jnp.where(inside, k2[...], 0.0)
    k = k2[...]
    plane = lax.broadcasted_iota(jnp.int32, shape, 0)
    lane = lanes(shape)
    edge_x = ((plane == 0) & (lane < 32), (plane == 15) & (lane >= 96))
    level = build(k, 0.25**2, 32, inside, edge_x)
    x = smooth(None, b, level, 32)
    rs[...] = remain(x, b, level, 32)
    for number, value in enumerate((b, x, k)):
        hold[number] = value
    for i in range(5):
        at = gx - 2 + i
        ok = (at >= 0) & (at < 16)
        from_plane = jnp.clip(at, 0, 15)
        for number in range(3):
            near[number, i] = jnp.where(ok, hold[number, from_plane], 0.0)

    if first:
        for i in range(5):
            edge[0, i : i + 1, :] = near[1, i, 9:10, :]
            edge[1, i : i + 1, :] = near[1, i, 14:15, :]
        upper = lax.rem(gy + 1, 16)
        for g in range(16):
            three[g, 4] = jnp.where(upper == g, edge[0], edge[1])

    def coarse(src, out):
        flat = [
            jnp.concatenate([pair_rows(src, 4 * c + q, 4, 8) for q in range(4)], axis=1) for c in range(4)
        ]
        cs[...] = (0.125 * pair_dot(jnp.concatenate(flat, axis=0), restrict_map(32))).reshape(4, 8, 128)
        for c in range(4):
            part = cs[c, 2:6, :]
            for g in range(16):
                three[g, out + c // 2, 4 * (c % 2) : 4 * (c % 2) + 4, :] = part

    coarse(rs, 0)
    if first:
        coarse(k2, 2)


def go_mid(first, pos, mid, below, above, k2):
    outs = [(3, 5, 24, 128), (16, 5 if first else 2, 8, 128)]
    outs += [(16, 24, 128)] if first else []
    scratch = [(3, 16, 24, 128), (16, 24, 128), (4, 8, 128), (2, 8, 128)]
    args = (mid, below, above) + (() if first else (k2,))
    return call(functools.partial(mid_kernel, first), outs, scratch, pos, *args)


def solve_last(b, k, owned):
    shape = k.shape
    scale = 0.25**4
    lane = lanes(shape)
    row = lax.broadcasted_iota(jnp.int32, shape, 0)
    moves = (
        (8, 1, lane < 8, True),
        (-8, 1, lane >= 120, True),
        (1, 0, row == 0, True),
        (-1, 0, row == 31, True),
        (1, 1, (lane & 7) == 0, False),
        (-1, 1, (lane & 7) == 7, False),
    )
    diagonal = jnp.full(shape, SIGMA * scale, F32)
    pulls = []
    for shift, axis, edge, masked in moves:
        weight = (0.5 * scale) * (k + jnp.where(edge, 0.0, turn(k, shift, axis)))
        diagonal = diagonal + weight
        keep = jnp.where(edge, 0.0, weight)
        if masked:
            keep = jnp.where(owned == turn(owned, shift, axis), keep, 0.0)
        pulls.append(keep)
    rd = 1.0 / diagonal
    pulls = [keep * rd for keep in pulls]
    g = b * rd
    first, steps = COARSE
    d = g * first
    x = d
    for keep, gain in steps:
        total = [pull * turn(x, move[0], move[1]) for pull, move in zip(pulls, moves)]
        near = (total[0] + total[1]) + (total[2] + total[3]) + (total[4] + total[5])
        d = keep * d + gain * ((g - x) + near)
        x = x + d
    return x


def fill_three(dst, gathered, first):
    for g in range(16):
        for c in range(4):
            part = gathered[g, first + c // 2, 4 * (c % 2) : 4 * (c % 2) + 4, :]
            dst[c, 4 * g : 4 * g + 4, :] = part


def solve_three(b_ref, k_ref, owned, s3):
    shape = (4, 64, 128)
    plane = lax.broadcasted_iota(jnp.int32, shape, 0)
    row = lax.broadcasted_iota(jnp.int32, shape, 1)
    lane = lanes(shape)
    edge_x = ((plane == 0) & (lane < 16), (plane == 3) & (lane >= 112))
    level = build(k_ref[...], 0.25**3, 16, None, edge_x, (row == 0, row == 63))
    b = b_ref[...]
    x = smooth(None, b, level, 16)
    s3[:, 8:72, :] = remain(x, b, level, 16)
    flat = [
        jnp.concatenate([pair_rows(src, q, row0, 32) for q in range(4)], axis=1) for src, row0 in ((s3, 8), (k_ref, 0))
    ]
    fine = 0.125 * pair_dot(jnp.concatenate(flat, axis=0), restrict_map(16))
    last = solve_last(fine[:32], fine[32:], owned[...])
    back = pair_dot(last, prolong_map(16))
    for q in range(4):
        spread_rows(s3, q, 8, back[:, 128 * q : 128 * q + 128])
    s3[:, 8:72, :] = smooth(x + s3[:, 8:72, :], b, level, 16)


def rise_two(gx, gy, near, x2, s3, e2, s2):
    pair = lax.shift_right_logical(gy + 1, 1)
    rows = pl.ds(pl.multiple_of(pair * 8, 8), 24)
    for i in range(5):
        at = jnp.clip(gx - 2 + i, 0, 15)
        spread_rows(e2, i, 0, pair_dot(s3[at // 4, rows, :], prolong_one(32, at % 4)))
    e = e2[:, pl.ds(pl.multiple_of((gy + 1 - 2 * pair) * 8, 8), 24), :]
    shape = (5, 24, 128)
    inside = within(shape, gx * 4 - 8, gy * 8 - 8, 32, 64, 128)
    level = build(near[2], 0.25**2, 32, inside)
    s2[...] = smooth(jnp.where(inside, x2 + e, 0.0), near[0], level, 32)


def rise_one(x1, b1, k1, inside, s2, s1):
    flat = jnp.concatenate([s2[i, 4:20, :] for i in range(1, 4)], axis=0)
    back = pair_dot(flat, prolong_map(64))
    for i in range(3):
        for q in range(4):
            spread_rows(s1, 4 * i + q, 0, back[16 * i : 16 * i + 16, 128 * q : 128 * q + 128])
    level = build(k1, 0.25, 64, inside)
    s1[...] = smooth(jnp.where(inside, x1 + s1[...], 0.0), b1, level, 64)


def spread_one(s1, low, high, e0):
    flat = jnp.concatenate([s1[i, 4:28, :] for i in range(low, high)], axis=0)
    back = pair_dot(flat, prolong_map(128, (1, 3)))
    for i in range(high - low):
        for q in range(2):
            part = back[24 * i : 24 * i + 24, 128 * q : 128 * q + 128]
            spread_rows(e0, 2 * (low - 2 + i) + q, 4, part)
    e0[:, 0:4, :] = jnp.zeros((16, 4, 128), F32)
    e0[:, RY - 4 : RY, :] = jnp.zeros((16, 4, 128), F32)


def add_top(x0, e0, x):
    def begin(p, rdv):
        c = (p - 2) // 2
        pair = (e0[pl.ds(c, 1)], e0[pl.ds(c + 1, 1)])
        correction = jnp.concatenate([pair[0], pair[0], pair[1], pair[1]], axis=0)
        at = pl.ds(p, CHUNK)
        x[at] = jnp.where(rdv > 0.0, x0[at] + correction, 0.0)

    return begin


def turn_kernel(
    pos, owned, three, near, one, left, right, below, above, *refs
):
    gx, gy = pos[0], pos[1]
    fars, (x0n, b1n, east, west, *far_outs) = refs[:3], refs[3:11]
    b3, s3, e2, s2, x2s, b1s, s1, e0, d, x, rs, xout, rout, k3, k1 = refs[11:26]
    tops, sems = refs[26:29], refs[34]
    (b0, k0, x0), (wx, wy, wz, s, rd) = tops, refs[29:34]
    loads = moves(fars, tops, sems)
    for move in loads:
        move.start()
    xkeep, rkeep, kkeep, k1keep = (
        pltpu.make_async_copy(a, b, sems.at[3 + i]) for i, (a, b) in enumerate(zip((xout, rout, k3, k1), far_outs))
    )
    fill_three(b3, three, 0)
    fill_three(k3, three, 2)
    kkeep.start()
    solve_three(b3, k3, owned, s3)
    x2s[...] = near[1]
    lower, upper = lax.rem(gy + 15, 16), lax.rem(gy + 1, 16)
    for i in range(5):
        x2s[i, 1:2, :] = three[lower, 4, i : i + 1, :]
        x2s[i, 22:23, :] = three[upper, 4, i : i + 1, :]
    rise_two(gx, gy, near, x2s[...], s3, e2, s2)

    inside = within((12, 32, 128), gx * 8 - 8, gy * 16 - 8, 64, 128, 256)
    for number, dst in enumerate((b1s, s1, k1)):
        part = slice(32 + 12 * number, 44 + 12 * number)
        fill_one(dst, left[number], one[number], right[number], below[part], above[part])
    k1[...] = jnp.where(inside, k1[...], 0.0)
    k1keep.start()
    rise_one(s1[...], b1s[...], k1[...], inside, s2, s1)

    spread_one(s1, 2, 10, e0)
    for move in loads:
        move.wait()
    inside_at = insider(RY, gx * TX - HX, gy * TY - HY)
    build_top(k0, wx, wy, wz, s, rd, 2, PX - 2, inside_at, add_top(x0, e0, x))
    start, steps = SMOOTH
    sweep_top(x, wx, wy, wz, s, 4, PX - 4, open_top(b0, 0, rd, d, x))
    for (keep, gain), edge in zip(steps, (4, 6)):
        sweep_top(x, wx, wy, wz, s, edge, PX - edge, advance_top(keep, gain, b0, 0, rd, d, x))

    def residual(p, at, v, av):
        rout[pl.ds(p - 6, v.shape[0])] = b0[at] - av

    sweep_top(x, wx, wy, wz, s, 6, PX - 6, residual)
    xout[...] = x[9 : PX - 9]
    xkeep.start()
    rkeep.start()

    def begin(i, _):
        at = pl.ds(6 + i * CHUNK, CHUNK)
        v = (rout[pl.ds(i * CHUNK, CHUNK)] * rd[at]) * start
        d[at] = v
        x[at] = v
        return 0

    lax.fori_loop(0, (PX - 12) // CHUNK, begin, 0)
    for keep, gain in steps:
        sweep_top(x, wx, wy, wz, s, 8, PX - 8, advance_top(keep, gain, rout, 6, rd, d, x))

    def again(p, at, v, av):
        d[at] = rout[pl.ds(p - 6, v.shape[0])] - av

    sweep_top(x, wx, wy, wz, s, HX, HX + TX, again)
    x0n[...] = x[HX : HX + TX, HY : HY + TY, :]
    for c in range(8):
        rs[c] = d[HX + 2 * c] + d[HX + 1 + 2 * c]
    b1 = pair_planes(rs, 4, HY, 16)
    b1n[...] = b1
    for side, plane in ((east, HX + TX - 4), (west, HX)):
        side[:, 0:16, :] = b1
        side[:, 16:48, :] = x[plane : plane + 4, HY : HY + TY, :]
    for move in (xkeep, rkeep, kkeep, k1keep):
        move.wait()


def go_turn(*args):
    top, wide, three = (PX, RY, 128), (12, 32, 128), (4, 64, 128)
    kept = [(TX + 2, RY, 128), (TX + 8, RY, 128), three, wide]
    outs = [(TX, TY, 128), (4, 16, 128), (4, 48, 128), (4, 48, 128)] + kept
    scratch = [three, (4, 88, 128), (5, 48, 128), (5, 24, 128), (5, 24, 128), wide, wide, (16, RY, 128)]
    scratch += [top] * 2 + [(8, RY, 128)] + kept + [top] * 8
    return call(turn_kernel, outs, scratch, *args, far_in=3, far_out=4, copies=7)


def last_kernel(
    pos, owned, three, k3, near, b1, x1, k1, x0n, left, right, below, above, borig, *refs
):
    gx, gy = pos[0], pos[1]
    fars, (xout, rout), (b3, s3, e2, s2, s1, e0, d, x) = refs[:3], refs[3:5], refs[5:13]
    tops, sems = refs[13:16], refs[21]
    (r, xbefore, k0), (wx, wy, wz, s, rd) = tops, refs[16:21]
    loads = moves(fars, tops, sems)
    for move in loads:
        move.start()
    fill_three(b3, three, 0)
    solve_three(b3, k3, owned, s3)
    rise_two(gx, gy, near, near[1], s3, e2, s2)
    inside = within((12, 32, 128), gx * 8 - 8, gy * 16 - 8, 64, 128, 256)
    rise_one(x1[...], b1[...], k1[...], inside, s2, s1)

    spread_one(s1, 3, 9, e0)
    low, high = HX - 4, HX + TX + 4
    x[low:HX, HY : HY + TY, :] = left[:, 16:48, :]
    x[HX : HX + TX, HY : HY + TY, :] = x0n[...]
    x[HX + TX : high, HY : HY + TY, :] = right[:, 16:48, :]
    x[low:high, HY - 8 : HY, :] = below[16:40]
    x[low:high, HY + TY : HY + TY + 8, :] = above[16:40]
    x[low:high, 0 : HY - 8, :] = jnp.zeros((high - low, HY - 8, 128), F32)
    x[low:high, RY - 4 : RY, :] = jnp.zeros((high - low, 4, 128), F32)
    for move in loads:
        move.wait()
    inside_at = insider(RY, gx * TX - HX, gy * TY - HY)
    build_top(k0, wx, wy, wz, s, rd, low, high, inside_at, add_top(x, e0, x))
    sweep_top(x, wx, wy, wz, s, low, high, open_top(r, low, rd, d, x))
    for keep, gain in SMOOTH[1]:
        sweep_top(x, wx, wy, wz, s, 8, PX - 8, advance_top(keep, gain, r, low, rd, d, x))
    x[9 : PX - 9] = x[9 : PX - 9] + xbefore[...]

    def residual(p, at, v, av):
        d[at] = av

    sweep_top(x, wx, wy, wz, s, HX, HX + TX, residual)
    xout[...] = x[HX : HX + TX, HY : HY + TY, :]
    rout[...] = borig[...] - d[HX : HX + TX, HY : HY + TY, :]


def go_last(*args):
    top, wide, tile = (PX, RY, 128), (12, 32, 128), (TX, TY, 128)
    scratch = [(4, 64, 128), (4, 88, 128), (5, 48, 128), (5, 24, 128), wide, (16, RY, 128)] + [top] * 2
    scratch += [(TX + 8, RY, 128), (TX + 2, RY, 128)] + [top] * 6
    return call(last_kernel, [tile, tile], scratch, *args, far_in=3, copies=3)


def shift(value, axis, step):
    count = lax.axis_size(axis)
    return lax.ppermute(value, axis, [(i, (i + step) % count) for i in range(count)])


def gather(copies, axis):
    return lax.all_to_all(copies, axis, 0, 0, tiled=True)


def local(right_side, kappa, owners):
    pos = jnp.stack([lax.axis_index("gx"), lax.axis_index("gy")]).astype(jnp.int32)
    owned = jnp.repeat(jnp.repeat(owners.T, 2, 0), 8, 1).astype(F32)
    mid = jnp.stack([right_side, kappa])
    left = shift(mid[:, TX - HX :], "gx", 1)
    right = shift(mid[:, :HX], "gx", -1)
    wide = jnp.concatenate([left, mid, right], axis=1)
    below = shift(wide[:, :, TY - HX :], "gy", 1)
    above = shift(wide[:, :, :HX], "gy", -1)
    one, two, b0, k0, x0 = go_down(pos, right_side, left, right, below, above, kappa)
    left = shift(one, "gx", 1)
    right = shift(one, "gx", -1)
    two = gather(two, "gx")
    rows = jnp.swapaxes(two, 0, 1).reshape(-1, 8, 128)
    wide = jnp.concatenate([left, one, right], axis=1)
    below = shift(jnp.concatenate([rows, wide[:, :, 8:].reshape(-1, 8, 128)]), "gy", 1)
    above = shift(jnp.concatenate([rows, wide[:, :, :8].reshape(-1, 8, 128)]), "gy", -1)
    near, three, k2 = go_mid(True, pos, two, below, above, None)
    three = gather(three, "gy")
    x0n, b1n, east, west, xbefore, source, k3, k1 = go_turn(
        pos, owned, three, near, one, left, right, below, above, b0, k0, x0
    )

    left = shift(east, "gx", 1)
    right = shift(west, "gx", -1)
    wide = jnp.concatenate([left[:, :16], b1n, right[:, :16]])
    below = shift(wide[:, 8:], "gy", 1)
    above = shift(wide[:, :8], "gy", -1)
    b1, x1, two = go_one(pos, b1n, left, right, below, above, k1)
    two = gather(two, "gx")
    wide = jnp.concatenate([left[:, 16:], x0n, right[:, 16:]])
    below = shift(jnp.concatenate([two[:, 0], wide[:, 24:]]), "gy", 1)
    above = shift(jnp.concatenate([two[:, 0], wide[:, :8]]), "gy", -1)
    near, three = go_mid(False, pos, two, below, above, k2)
    three = gather(three, "gy")
    field, residual = go_last(
        pos, owned, three, k3, near, b1, x1, k1, x0n, left, right, below, above, right_side, source, xbefore, k0
    )
    return field, residual


def solution(mesh):
    spec = P("gx", "gy", None)
    return jax.shard_map(
        local, mesh=mesh, in_specs=(spec, spec, P()), out_specs=(spec, spec), check_vma=False
    )
```

```python
import functools

import jax
import jax.numpy as jnp
from jax import lax
from jax.experimental import pallas as pl
from jax.experimental.pallas import tpu as pltpu
from jax.sharding import PartitionSpec as P

SIGMA = 0.02
F32 = jnp.float32
BF16 = jnp.bfloat16
TX, TY = 16, 32
HX = 10
HY = 12
PX, RY = TX + 2 * HX, TY + 2 * HY
CHUNK = 4
PARTS = 2
VMEM_BYTES = 56 * 1024 * 1024


def cheb_steps(degree, lower):
    centre = 0.5 * (2.0 + lower)
    half = 0.5 * (2.0 - lower)
    sharp = centre / half
    ratio = 1.0 / sharp
    steps = []
    for _ in range(degree - 1):
        nxt = 1.0 / (2.0 * sharp - ratio)
        steps.append((nxt * ratio, 2.0 * nxt / half))
        ratio = nxt
    return 1.0 / centre, steps


SMOOTH = cheb_steps(3, 0.3)
COARSE = cheb_steps(24, 0.05)


def lane_match(z, q, source, target):
    bits = z.bit_length() - 1
    cell = (lax.shift_right_logical(source, bits) + (128 // z) * q) & -2
    inner = lax.shift_right_logical(source & (z - 1), 1)
    return jnp.where(cell * (z // 4) + inner == target, 1.0, 0.0).astype(BF16)


def restrict_map(z, planes=(0, 4)):
    shape = ((planes[1] - planes[0]) * 128, 128)
    row = lax.broadcasted_iota(jnp.int32, shape, 0)
    return lane_match(z, planes[0] + lax.shift_right_logical(row, 7), row & 127, lanes(shape))


def prolong_map(z, planes=(0, 4)):
    shape = (128, (planes[1] - planes[0]) * 128)
    column = lanes(shape)
    target = lax.broadcasted_iota(jnp.int32, shape, 0)
    return lane_match(z, planes[0] + lax.shift_right_logical(column, 7), column & 127, target)


def prolong_one(z, q):
    shape = (128, 128)
    return lane_match(z, q, lanes(shape), lax.broadcasted_iota(jnp.int32, shape, 0))


def pair_dot(value, matrix):
    rows = value.shape[0]
    high = value.astype(BF16).astype(F32)
    rest = value - high
    mid = rest.astype(BF16).astype(F32)
    parts = jnp.concatenate([high, mid, rest - mid], axis=0).astype(BF16)
    out = jnp.dot(parts, matrix, preferred_element_type=F32)
    return out[:rows] + (out[rows : 2 * rows] + out[2 * rows :])


def lanes(shape):
    return lax.broadcasted_iota(jnp.int32, shape, len(shape) - 1)


def turn(value, shift, axis):
    return pltpu.roll(value, shift % value.shape[axis], axis)


def next_x(v, z):
    if z == 128:
        return jnp.concatenate([v[1:], v[:1]], axis=0)
    a = turn(v, -z, 2)
    b = jnp.concatenate([a[1:], a[:1]], axis=0)
    return jnp.where(lanes(v.shape) < 128 - z, a, b)


def prev_x(v, z):
    if z == 128:
        return jnp.concatenate([v[-1:], v[:-1]], axis=0)
    a = turn(v, z, 2)
    b = jnp.concatenate([a[-1:], a[:-1]], axis=0)
    return jnp.where(lanes(v.shape) >= z, a, b)


def faces_of(k, step, scale, low, high):
    own = (0.5 * scale) * k
    both = own + (0.5 * scale) * step
    if low is None:
        return both, None
    edge = jnp.where(low | high, own, 0.0)
    return jnp.where(high, 0.0, both), edge


def build(k, scale, z, inside=None, edge_x=(None, None), edge_y=(None, None)):
    shape = k.shape
    cell = lanes(shape) & (z - 1)
    wx, ex = faces_of(k, next_x(k, z), scale, *edge_x)
    wy, ey = faces_of(k, turn(k, -1, 1), scale, *edge_y)
    wz, ez = faces_of(k, turn(k, -1, 2), scale, cell == 0, cell == z - 1)
    s = ez + SIGMA * scale
    if ex is not None:
        s = s + ex
    if ey is not None:
        s = s + ey
    diagonal = s + wx + prev_x(wx, z) + wy + turn(wy, 1, 1) + wz + turn(wz, 1, 2)
    rd = 1.0 / diagonal
    if inside is not None:
        rd = jnp.where(inside, rd, 0.0)
    return wx, wy, wz, s, rd


def remain(v, b, level, z):
    wx, wy, wz, s, _ = level
    fx = wx * (next_x(v, z) - v)
    fy = wy * (turn(v, -1, 1) - v)
    fz = wz * (turn(v, -1, 2) - v)
    total = (fx - prev_x(fx, z)) + (fy - turn(fy, 1, 1)) + (fz - turn(fz, 1, 2))
    return (b - s * v) + total


def smooth(x, b, level, z):
    first, steps = SMOOTH
    rd = level[4]
    if x is None:
        d = (b * rd) * first
        x = d
    else:
        d = (remain(x, b, level, z) * rd) * first
        x = x + d
    for keep, gain in steps:
        d = keep * d + gain * (remain(x, b, level, z) * rd)
        x = x + d
    return x


def within(shape, first_x, first_y, z, size_x, size_y):
    plane = lax.broadcasted_iota(jnp.int32, shape, 0)
    cx = first_x + plane * (128 // z) + lax.shift_right_logical(lanes(shape), z.bit_length() - 1)
    cy = first_y + lax.broadcasted_iota(jnp.int32, shape, 1)
    return (cx >= 0) & (cx < size_x) & (cy >= 0) & (cy < size_y)


def pair_rows(ref, plane, start, count):
    return ref[plane, pl.ds(start, count, stride=2), :] + ref[plane, pl.ds(start + 1, count, stride=2), :]


def spread_rows(ref, plane, start, value):
    count = value.shape[0]
    ref[plane, pl.ds(start, count, stride=2), :] = value
    ref[plane, pl.ds(start + 1, count, stride=2), :] = value


def insider(rows, first_x, first_y):
    row = lax.broadcasted_iota(jnp.int32, (CHUNK, rows, 128), 1) + first_y
    row_in = (row >= 0) & (row < 512)
    plane = lax.broadcasted_iota(jnp.int32, (CHUNK, rows, 128), 0) + first_x
    return lambda p: row_in & (plane >= -p) & (plane < 256 - p)


def build_top(k_ref, wx, wy, wz, s, rd, low, high, inside_at, body):
    rows = k_ref.shape[1]
    shape = (CHUNK, rows, 128)
    lane = lanes(shape)

    def step(i, wxp):
        p = low + i * CHUNK
        k = k_ref[pl.ds(p, CHUNK)]
        kn = jnp.concatenate([k[1:], k_ref[pl.ds(jnp.minimum(p + CHUNK, k_ref.shape[0] - 1), 1)]], axis=0)
        own = 0.5 * k
        fx = 0.5 * kn + own
        fy = turn(own, -1, 1) + own
        fz = jnp.where(lane == 127, 0.0, turn(own, -1, 2) + own)
        sv = SIGMA + jnp.where((lane == 0) | (lane == 127), own, 0.0)
        fxp = jnp.concatenate([wxp, fx[:-1]], axis=0)
        diagonal = sv + (fx + fxp) + (fy + turn(fy, 1, 1)) + (fz + turn(fz, 1, 2))
        rdv = jnp.where(inside_at(p), 1.0 / diagonal, 0.0)
        at = pl.ds(p, CHUNK)
        wx[at], wy[at], wz[at], s[at], rd[at] = fx, fy, fz, sv, rdv
        body(p, rdv)
        return fx[-1:]

    assert (high - low) % CHUNK == 0
    lax.fori_loop(0, (high - low) // CHUNK, step, jnp.zeros((1, rows, 128), F32))


def sweep_top(x, wx, wy, wz, s, low, high, body):
    size = (high - low) // PARTS
    fx0 = wx[low - 1 : low] * (x[low : low + 1] - x[low - 1 : low])

    def step(i, fxp):
        p = low + i * size
        at = pl.ds(p, size)
        v = x[at]
        vn = jnp.concatenate([v[1:], x[pl.ds(p + size, 1)]], axis=0)
        fx = wx[at] * (vn - v)
        fy = wy[at] * (turn(v, -1, 1) - v)
        fz = wz[at] * (turn(v, -1, 2) - v)
        fxp = jnp.concatenate([fxp, fx[:-1]], axis=0)
        total = (fx - fxp) + (fy - turn(fy, 1, 1)) + (fz - turn(fz, 1, 2))
        body(p, at, v, s[at] * v - total)
        return fx[-1:]

    assert (high - low) % PARTS == 0
    lax.fori_loop(0, PARTS, step, fx0, unroll=True)


class Pick:
    def __init__(self, take_first, first, second):
        self.take_first, self.first, self.second = take_first, first, second

    def __getitem__(self, index):
        return jnp.where(self.take_first, self.first[index], self.second[index])


def sides(at, first, second):
    odd = (at & 1) == 1
    return Pick(odd, first, second), Pick(odd, second, first)


def fill_top(dst, number, wide, below, above):
    dst[:, 0:2, :] = jnp.zeros((PX, 2, 128), F32)
    dst[:, RY - 2 : RY, :] = jnp.zeros((PX, 2, 128), F32)
    dst[:, HY : HY + TY, :] = wide[number]
    for p in range(PX):
        part = slice(HX * (PX * number + p), HX * (PX * number + p + 1))
        dst[p, 2:HY, :] = below[part]
        dst[p, HY + TY : RY - 2, :] = above[part]


def down_kernel(pos, wide, by_y, by_y2, one, two, *refs):
    given, (bx, kx, x, wx, wy, wz, s, rd, d, rs, b1s, x1s, k1s, sems) = refs[:3], refs[3:]
    keeping = moves((bx, kx, x), given, sems)
    gx, gy = pos[0], pos[1]
    inside_at = insider(RY, gx * TX - HX, gy * TY - HY)
    below, above = sides(gy, by_y, by_y2)
    fill_top(bx, 0, wide, below, above)
    fill_top(kx, 1, wide, below, above)

    def clear(i, _):
        at = pl.ds(i * CHUNK, CHUNK)
        kx[at] = jnp.where(inside_at(i * CHUNK), kx[at], 0.0)
        return 0

    lax.fori_loop(0, PX // CHUNK, clear, 0)
    for move in keeping[:2]:
        move.start()
    start, steps = SMOOTH

    def begin(p, rdv):
        at = pl.ds(p, CHUNK)
        v = (bx[at] * rdv) * start
        d[at] = v
        x[at] = v

    build_top(kx, wx, wy, wz, s, rd, 0, PX, inside_at, begin)
    for keep, gain in steps:
        sweep_top(x, wx, wy, wz, s, 2, PX - 2, advance_top(keep, gain, bx, 0, rd, d, x))

    def residual(p, at, v, av):
        d[at] = bx[at] - av

    keeping[2].start()
    sweep_top(x, wx, wy, wz, s, 4, PX - 4, residual)

    def coarse(src):
        for c in range(16):
            rs[c] = src[2 + 2 * c] + src[3 + 2 * c]
        return pair_planes(rs, 8, 4, 24)

    for p in (2, 3, PX - 4, PX - 3):
        d[p] = jnp.zeros((RY, 128), F32)
    b1 = coarse(d)
    k1 = coarse(kx)
    level = build(k1, 0.25, 64, within(k1.shape, gx * 8 - 4, gy * 16 - 4, 64, 128, 256))
    x1 = smooth(None, b1, level, 64)
    b1s[...] = b1
    x1s[...] = x1
    k1s[...] = k1
    for number, src in enumerate((b1s, x1s, k1s)):
        one[number] = src[2:6, 4:20, :]
    b1s[...] = remain(x1, b1, level, 64)
    send_all(two, coarse_tile((b1s, k1s), 2, 4))
    for move in keeping:
        move.wait()


def moves(sources, targets, sems):
    return [pltpu.make_async_copy(a, b, sems.at[i]) for i, (a, b) in enumerate(zip(sources, targets))]


def pair_planes(rs, planes, start, rows):
    flat = [
        jnp.concatenate([pair_rows(rs, 2 * c, start, rows), pair_rows(rs, 2 * c + 1, start, rows)], axis=1)
        for c in range(planes)
    ]
    out = 0.125 * pair_dot(jnp.concatenate(flat, axis=0), restrict_map(128, (1, 3)))
    return out.reshape(planes, rows, 128)


def coarse_tile(sources, plane, row):
    flat = [
        jnp.concatenate([pair_rows(src, plane + q, row, 8) for q in range(4)], axis=1) for src in sources
    ]
    out = 0.125 * pair_dot(jnp.concatenate(flat, axis=0), restrict_map(64))
    return out.reshape(len(sources), 8, 128)


def send_all(out, value):
    for g in range(16):
        out[g] = value


def advance_top(keep, gain, b, shift_b, rd, d, x):
    def advance(p, at, v, av):
        dv = keep * d[at] + gain * ((b[pl.ds(p - shift_b, v.shape[0])] - av) * rd[at])
        d[at] = dv
        x[at] = v + dv

    return advance


def open_top(b, shift_b, rd, d, x):
    def advance(p, at, v, av):
        dv = ((b[pl.ds(p - shift_b, v.shape[0])] - av) * rd[at]) * SMOOTH[0]
        d[at] = dv
        x[at] = v + dv

    return advance


def call(kernel, outs, scratch, *args, far_in=0, far_out=0, copies=0):
    near, far = pl.BlockSpec(memory_space=pltpu.VMEM), pl.BlockSpec(memory_space=pl.ANY)
    specs = [pl.BlockSpec(memory_space=pltpu.SMEM)] + [near] * (len(args) - 1 - far_in) + [far] * far_in
    return pl.pallas_call(
        kernel,
        out_shape=[jax.ShapeDtypeStruct(o, F32) for o in outs],
        in_specs=specs,
        out_specs=[near] * (len(outs) - far_out) + [far] * far_out,
        scratch_shapes=[pltpu.VMEM(o, F32) for o in scratch]
        + ([pltpu.SemaphoreType.DMA((copies,))] if copies else []),
        compiler_params=pltpu.CompilerParams(vmem_limit_bytes=VMEM_BYTES),
        cost_estimate=pl.CostEstimate(flops=10**7, bytes_accessed=8 << 20, transcendentals=0),
    )(*args)


def go_down(*args):
    top = (PX, RY, 128)
    outs = [(3, 4, 16, 128), (16, 2, 8, 128)] + [top] * 3
    scratch = [top] * 9 + [(16, RY, 128)] + [(8, 24, 128)] * 3
    return call(down_kernel, outs, scratch, *args, far_out=3, copies=3)


def one_kernel(pos, mid, by_x, by_x2, by_y, by_y2, k1, bout, xout, two, res):
    gx, gy = pos[0], pos[1]
    left, right = sides(gx, by_x, by_x2)
    below, above = sides(gy, by_y, by_y2)
    head = (slice(None), slice(0, 16))
    fill_one(bout, left[head], mid[...], right[head], below[...], above[...])
    b = bout[...]
    inside = within(b.shape, gx * 8 - 8, gy * 16 - 8, 64, 128, 256)
    level = build(k1[...], 0.25, 64, inside)
    x = smooth(None, b, level, 64)
    xout[...] = x
    res[...] = remain(x, b, level, 64)
    send_all(two, coarse_tile((res,), 4, 8))


def fill_one(dst, left, tile, right, below, above):
    dst[0:4, 8:24, :] = left
    dst[4:8, 8:24, :] = tile
    dst[8:12, 8:24, :] = right
    dst[:, 0:8, :] = below
    dst[:, 24:32, :] = above


def go_one(*args):
    wide = (12, 32, 128)
    return call(one_kernel, [wide, wide, (16, 1, 8, 128)], [wide], *args)


def mid_kernel(first, pos, mid, by_y, by_y2, *refs):
    if first:
        near, three, k2 = refs[:3]
        scratch = refs[3:]
    else:
        k2, near, three = refs[:3]
        scratch = refs[3:]
    hold, rs, cs, edge = scratch
    gx, gy = pos[0], pos[1]
    below, above = sides(gy, by_y, by_y2)
    shape = (16, 24, 128)
    inside = within(shape, 0, gy * 8 - 8, 32, 64, 128)

    def rows(dst, number):
        part = slice(16 * number, 16 * number + 16)
        dst[:, 0:8, :] = below[part]
        dst[:, 8:16, :] = mid[:, number]
        dst[:, 16:24, :] = above[part]

    rows(rs, 0)
    b = rs[...]
    if first:
        rows(k2, 1)
        k2[...] = jnp.where(inside, k2[...], 0.0)
    k = k2[...]
    plane = lax.broadcasted_iota(jnp.int32, shape, 0)
    lane = lanes(shape)
    edge_x = ((plane == 0) & (lane < 32), (plane == 15) & (lane >= 96))
    level = build(k, 0.25**2, 32, inside, edge_x)
    x = smooth(None, b, level, 32)
    rs[...] = remain(x, b, level, 32)
    for number, value in enumerate((b, x, k)):
        hold[number] = value
    for i in range(5):
        at = gx - 2 + i
        ok = (at >= 0) & (at < 16)
        from_plane = jnp.clip(at, 0, 15)
        for number in range(3):
            near[number, i] = jnp.where(ok, hold[number, from_plane], 0.0)

    if first:
        for i in range(5):
            edge[0, i : i + 1, :] = near[1, i, 9:10, :]
            edge[1, i : i + 1, :] = near[1, i, 14:15, :]
        upper = lax.rem(gy + 1, 16)
        for g in range(16):
            three[g, 4] = jnp.where(upper == g, edge[0], edge[1])

    def coarse(src, out):
        flat = [
            jnp.concatenate([pair_rows(src, 4 * c + q, 4, 8) for q in range(4)], axis=1) for c in range(4)
        ]
        cs[...] = (0.125 * pair_dot(jnp.concatenate(flat, axis=0), restrict_map(32))).reshape(4, 8, 128)
        for c in range(4):
            part = cs[c, 2:6, :]
            for g in range(16):
                three[g, out + c // 2, 4 * (c % 2) : 4 * (c % 2) + 4, :] = part

    coarse(rs, 0)
    if first:
        coarse(k2, 2)


def go_mid(first, pos, mid, below, above, k2):
    outs = [(3, 5, 24, 128), (16, 5 if first else 2, 8, 128)]
    outs += [(16, 24, 128)] if first else []
    scratch = [(3, 16, 24, 128), (16, 24, 128), (4, 8, 128), (2, 8, 128)]
    args = (mid, below, above) + (() if first else (k2,))
    return call(functools.partial(mid_kernel, first), outs, scratch, pos, *args)


def solve_last(b, k, owned):
    shape = k.shape
    scale = 0.25**4
    lane = lanes(shape)
    row = lax.broadcasted_iota(jnp.int32, shape, 0)
    moves = (
        (8, 1, lane < 8, True),
        (-8, 1, lane >= 120, True),
        (1, 0, row == 0, True),
        (-1, 0, row == 31, True),
        (1, 1, (lane & 7) == 0, False),
        (-1, 1, (lane & 7) == 7, False),
    )
    diagonal = jnp.full(shape, SIGMA * scale, F32)
    pulls = []
    for shift, axis, edge, masked in moves:
        weight = (0.5 * scale) * (k + jnp.where(edge, 0.0, turn(k, shift, axis)))
        diagonal = diagonal + weight
        keep = jnp.where(edge, 0.0, weight)
        if masked:
            keep = jnp.where(owned == turn(owned, shift, axis), keep, 0.0)
        pulls.append(keep)
    rd = 1.0 / diagonal
    pulls = [keep * rd for keep in pulls]
    g = b * rd
    first, steps = COARSE
    d = g * first
    x = d
    for keep, gain in steps:
        total = [pull * turn(x, move[0], move[1]) for pull, move in zip(pulls, moves)]
        near = (total[0] + total[1]) + (total[2] + total[3]) + (total[4] + total[5])
        d = keep * d + gain * ((g - x) + near)
        x = x + d
    return x


def fill_three(dst, gathered, first):
    for g in range(16):
        for c in range(4):
            part = gathered[g, first + c // 2, 4 * (c % 2) : 4 * (c % 2) + 4, :]
            dst[c, 4 * g : 4 * g + 4, :] = part


def solve_three(b_ref, k_ref, owned, s3):
    shape = (4, 64, 128)
    plane = lax.broadcasted_iota(jnp.int32, shape, 0)
    row = lax.broadcasted_iota(jnp.int32, shape, 1)
    lane = lanes(shape)
    edge_x = ((plane == 0) & (lane < 16), (plane == 3) & (lane >= 112))
    level = build(k_ref[...], 0.25**3, 16, None, edge_x, (row == 0, row == 63))
    b = b_ref[...]
    x = smooth(None, b, level, 16)
    s3[:, 8:72, :] = remain(x, b, level, 16)
    flat = [
        jnp.concatenate([pair_rows(src, q, row0, 32) for q in range(4)], axis=1) for src, row0 in ((s3, 8), (k_ref, 0))
    ]
    fine = 0.125 * pair_dot(jnp.concatenate(flat, axis=0), restrict_map(16))
    last = solve_last(fine[:32], fine[32:], owned[...])
    back = pair_dot(last, prolong_map(16))
    for q in range(4):
        spread_rows(s3, q, 8, back[:, 128 * q : 128 * q + 128])
    s3[:, 8:72, :] = smooth(x + s3[:, 8:72, :], b, level, 16)


def rise_two(gx, gy, near, x2, s3, e2, s2):
    pair = lax.shift_right_logical(gy + 1, 1)
    rows = pl.ds(pl.multiple_of(pair * 8, 8), 24)
    for i in range(5):
        at = jnp.clip(gx - 2 + i, 0, 15)
        spread_rows(e2, i, 0, pair_dot(s3[at // 4, rows, :], prolong_one(32, at % 4)))
    e = e2[:, pl.ds(pl.multiple_of((gy + 1 - 2 * pair) * 8, 8), 24), :]
    shape = (5, 24, 128)
    inside = within(shape, gx * 4 - 8, gy * 8 - 8, 32, 64, 128)
    level = build(near[2], 0.25**2, 32, inside)
    s2[...] = smooth(jnp.where(inside, x2 + e, 0.0), near[0], level, 32)


def rise_one(x1, b1, k1, inside, s2, s1):
    flat = jnp.concatenate([s2[i, 4:20, :] for i in range(1, 4)], axis=0)
    back = pair_dot(flat, prolong_map(64))
    for i in range(3):
        for q in range(4):
            spread_rows(s1, 4 * i + q, 0, back[16 * i : 16 * i + 16, 128 * q : 128 * q + 128])
    level = build(k1, 0.25, 64, inside)
    s1[...] = smooth(jnp.where(inside, x1 + s1[...], 0.0), b1, level, 64)


def spread_one(s1, low, high, e0):
    flat = jnp.concatenate([s1[i, 4:28, :] for i in range(low, high)], axis=0)
    back = pair_dot(flat, prolong_map(128, (1, 3)))
    for i in range(high - low):
        for q in range(2):
            part = back[24 * i : 24 * i + 24, 128 * q : 128 * q + 128]
            spread_rows(e0, 2 * (low - 2 + i) + q, 4, part)
    e0[:, 0:4, :] = jnp.zeros((16, 4, 128), F32)
    e0[:, RY - 4 : RY, :] = jnp.zeros((16, 4, 128), F32)


def add_top(x0, e0, x):
    def begin(p, rdv):
        c = (p - 2) // 2
        pair = (e0[pl.ds(c, 1)], e0[pl.ds(c + 1, 1)])
        correction = jnp.concatenate([pair[0], pair[0], pair[1], pair[1]], axis=0)
        at = pl.ds(p, CHUNK)
        x[at] = jnp.where(rdv > 0.0, x0[at] + correction, 0.0)

    return begin


def turn_kernel(
    pos, owned, three, near, one, by_x, by_x2, by_y, by_y2, *refs
):
    gx, gy = pos[0], pos[1]
    left, right = sides(gx, by_x, by_x2)
    below, above = sides(gy, by_y, by_y2)
    fars, (x0n, b1n, send, send2, *far_outs) = refs[:3], refs[3:11]
    b3, s3, e2, s2, x2s, b1s, s1, e0, d, x, rs, xout, rout, k3, k1 = refs[11:26]
    tops, sems = refs[26:29], refs[34]
    (b0, k0, x0), (wx, wy, wz, s, rd) = tops, refs[29:34]
    loads = moves(fars, tops, sems)
    for move in loads:
        move.start()
    xkeep, rkeep, kkeep, k1keep = (
        pltpu.make_async_copy(a, b, sems.at[3 + i]) for i, (a, b) in enumerate(zip((xout, rout, k3, k1), far_outs))
    )
    fill_three(b3, three, 0)
    fill_three(k3, three, 2)
    kkeep.start()
    solve_three(b3, k3, owned, s3)
    x2s[...] = near[1]
    lower, upper = lax.rem(gy + 15, 16), lax.rem(gy + 1, 16)
    for i in range(5):
        x2s[i, 1:2, :] = three[lower, 4, i : i + 1, :]
        x2s[i, 22:23, :] = three[upper, 4, i : i + 1, :]
    rise_two(gx, gy, near, x2s[...], s3, e2, s2)

    inside = within((12, 32, 128), gx * 8 - 8, gy * 16 - 8, 64, 128, 256)
    for number, dst in enumerate((b1s, s1, k1)):
        part = slice(32 + 12 * number, 44 + 12 * number)
        fill_one(dst, left[number], one[number], right[number], below[part], above[part])
    k1[...] = jnp.where(inside, k1[...], 0.0)
    k1keep.start()
    rise_one(s1[...], b1s[...], k1[...], inside, s2, s1)

    spread_one(s1, 2, 10, e0)
    for move in loads:
        move.wait()
    inside_at = insider(RY, gx * TX - HX, gy * TY - HY)
    build_top(k0, wx, wy, wz, s, rd, 2, PX - 2, inside_at, add_top(x0, e0, x))
    start, steps = SMOOTH
    sweep_top(x, wx, wy, wz, s, 4, PX - 4, open_top(b0, 0, rd, d, x))
    for (keep, gain), edge in zip(steps, (4, 6)):
        sweep_top(x, wx, wy, wz, s, edge, PX - edge, advance_top(keep, gain, b0, 0, rd, d, x))

    def residual(p, at, v, av):
        rout[pl.ds(p - 6, v.shape[0])] = b0[at] - av

    sweep_top(x, wx, wy, wz, s, 6, PX - 6, residual)
    xout[...] = x[9 : PX - 9]
    xkeep.start()
    rkeep.start()

    def begin(i, _):
        at = pl.ds(6 + i * CHUNK, CHUNK)
        v = (rout[pl.ds(i * CHUNK, CHUNK)] * rd[at]) * start
        d[at] = v
        x[at] = v
        return 0

    lax.fori_loop(0, (PX - 12) // CHUNK, begin, 0)
    for keep, gain in steps:
        sweep_top(x, wx, wy, wz, s, 8, PX - 8, advance_top(keep, gain, rout, 6, rd, d, x))

    def again(p, at, v, av):
        d[at] = rout[pl.ds(p - 6, v.shape[0])] - av

    sweep_top(x, wx, wy, wz, s, HX, HX + TX, again)
    x0n[...] = x[HX : HX + TX, HY : HY + TY, :]
    for c in range(8):
        rs[c] = d[HX + 2 * c] + d[HX + 1 + 2 * c]
    b1 = pair_planes(rs, 4, HY, 16)
    b1n[...] = b1
    odd = (gx & 1) == 1
    for side, of_odd, of_even in ((send, HX, HX + TX - 4), (send2, HX + TX - 4, HX)):
        side[:, 0:16, :] = b1
        side[:, 16:48, :] = x[pl.ds(jnp.where(odd, of_odd, of_even), 4), HY : HY + TY, :]
    for move in (xkeep, rkeep, kkeep, k1keep):
        move.wait()


def go_turn(*args):
    top, wide, three = (PX, RY, 128), (12, 32, 128), (4, 64, 128)
    kept = [(TX + 2, RY, 128), (TX + 8, RY, 128), three, wide]
    outs = [(TX, TY, 128), (4, 16, 128), (4, 48, 128), (4, 48, 128)] + kept
    scratch = [three, (4, 88, 128), (5, 48, 128), (5, 24, 128), (5, 24, 128), wide, wide, (16, RY, 128)]
    scratch += [top] * 2 + [(8, RY, 128)] + kept + [top] * 8
    return call(turn_kernel, outs, scratch, *args, far_in=3, far_out=4, copies=7)


def last_kernel(
    pos, owned, three, k3, near, b1, x1, k1, x0n, by_x, by_x2, by_y, by_y2, borig, *refs
):
    gx, gy = pos[0], pos[1]
    left, right = sides(gx, by_x, by_x2)
    below, above = sides(gy, by_y, by_y2)
    fars, (xout, rout), (b3, s3, e2, s2, s1, e0, d, x) = refs[:3], refs[3:5], refs[5:13]
    tops, sems = refs[13:16], refs[21]
    (r, xbefore, k0), (wx, wy, wz, s, rd) = tops, refs[16:21]
    loads = moves(fars, tops, sems)
    for move in loads:
        move.start()
    fill_three(b3, three, 0)
    solve_three(b3, k3, owned, s3)
    rise_two(gx, gy, near, near[1], s3, e2, s2)
    inside = within((12, 32, 128), gx * 8 - 8, gy * 16 - 8, 64, 128, 256)
    rise_one(x1[...], b1[...], k1[...], inside, s2, s1)

    spread_one(s1, 3, 9, e0)
    low, high = HX - 4, HX + TX + 4
    x[low:HX, HY : HY + TY, :] = left[:, 16:48, :]
    x[HX : HX + TX, HY : HY + TY, :] = x0n[...]
    x[HX + TX : high, HY : HY + TY, :] = right[:, 16:48, :]
    x[low:high, HY - 8 : HY, :] = below[16:40]
    x[low:high, HY + TY : HY + TY + 8, :] = above[16:40]
    x[low:high, 0 : HY - 8, :] = jnp.zeros((high - low, HY - 8, 128), F32)
    x[low:high, RY - 4 : RY, :] = jnp.zeros((high - low, 4, 128), F32)
    for move in loads:
        move.wait()
    inside_at = insider(RY, gx * TX - HX, gy * TY - HY)
    build_top(k0, wx, wy, wz, s, rd, low, high, inside_at, add_top(x, e0, x))
    sweep_top(x, wx, wy, wz, s, low, high, open_top(r, low, rd, d, x))
    for keep, gain in SMOOTH[1]:
        sweep_top(x, wx, wy, wz, s, 8, PX - 8, advance_top(keep, gain, r, low, rd, d, x))
    x[9 : PX - 9] = x[9 : PX - 9] + xbefore[...]

    def residual(p, at, v, av):
        d[at] = av

    sweep_top(x, wx, wy, wz, s, HX, HX + TX, residual)
    xout[...] = x[HX : HX + TX, HY : HY + TY, :]
    rout[...] = borig[...] - d[HX : HX + TX, HY : HY + TY, :]


def go_last(*args):
    top, wide, tile = (PX, RY, 128), (12, 32, 128), (TX, TY, 128)
    scratch = [(4, 64, 128), (4, 88, 128), (5, 48, 128), (5, 24, 128), wide, (16, RY, 128)] + [top] * 2
    scratch += [(TX + 8, RY, 128), (TX + 2, RY, 128)] + [top] * 6
    return call(last_kernel, [tile, tile], scratch, *args, far_in=3, copies=3)


def swap(low, high, axis):
    count = lax.axis_size(axis)
    odd = lax.axis_index(axis) % 2 == 1
    first = jnp.where(odd, low, high) if low is not high else low
    second = jnp.where(odd, high, low) if low is not high else low
    return (
        lax.ppermute(first, axis, [(i, i ^ 1) for i in range(count)]),
        lax.ppermute(second, axis, [(i, (i + 1 if i % 2 else i - 1) % count) for i in range(count)]),
    )


def apart(first, second, axis):
    odd = lax.axis_index(axis) % 2 == 1
    return jnp.where(odd, first, second), jnp.where(odd, second, first)


def gather(copies, axis):
    return lax.all_to_all(copies, axis, 0, 0, tiled=True)


def local(right_side, kappa, owners):
    pos = jnp.stack([lax.axis_index("gx"), lax.axis_index("gy")]).astype(jnp.int32)
    owned = jnp.repeat(jnp.repeat(owners.T, 2, 0), 8, 1).astype(F32)
    mid = jnp.stack([right_side, kappa])
    left, right = apart(*swap(mid[:, :HX], mid[:, TX - HX :], "gx"), "gx")
    wide = jnp.concatenate([left, mid, right], axis=1)
    low, high = (part.reshape(-1, 128) for part in (wide[:, :, :HX], wide[:, :, TY - HX :]))
    one, two, b0, k0, x0 = go_down(pos, wide, *swap(low, high, "gy"))
    by_x = swap(one, one, "gx")
    two = gather(two, "gx")
    left, right = apart(*by_x, "gx")
    rows = jnp.swapaxes(two, 0, 1).reshape(-1, 8, 128)
    wide = jnp.concatenate([left, one, right], axis=1)
    low, high = (
        jnp.concatenate([rows, part.reshape(-1, 8, 128)]) for part in (wide[:, :, :8], wide[:, :, 8:])
    )
    by_y = swap(low, high, "gy")
    near, three, k2 = go_mid(True, pos, two, *by_y, None)
    three = gather(three, "gy")
    x0n, b1n, send, send2, xbefore, source, k3, k1 = go_turn(
        pos, owned, three, near, one, *by_x, *by_y, b0, k0, x0
    )

    by_x = (
        lax.ppermute(send, "gx", [(i, i ^ 1) for i in range(16)]),
        lax.ppermute(send2, "gx", [(i, (i + 1 if i % 2 else i - 1) % 16) for i in range(16)]),
    )
    left, right = apart(*by_x, "gx")
    wide = jnp.concatenate([left[:, :16], b1n, right[:, :16]])
    b1, x1, two = go_one(pos, b1n, *by_x, *swap(wide[:, :8], wide[:, 8:], "gy"), k1)
    two = gather(two, "gx")
    wide = jnp.concatenate([left[:, 16:], x0n, right[:, 16:]])
    low, high = (jnp.concatenate([two[:, 0], part]) for part in (wide[:, :8], wide[:, 24:]))
    by_y = swap(low, high, "gy")
    near, three = go_mid(False, pos, two, *by_y, k2)
    three = gather(three, "gy")
    field, residual = go_last(
        pos, owned, three, k3, near, b1, x1, k1, x0n, *by_x, *by_y, right_side, source, xbefore, k0
    )
    return field, residual


def solution(mesh):
    spec = P("gx", "gy", None)
    return jax.shard_map(
        local, mesh=mesh, in_specs=(spec, spec, P()), out_specs=(spec, spec), check_vma=False
    )
```

```python
import functools

import jax
import jax.numpy as jnp
from jax import lax
from jax.experimental import pallas as pl
from jax.experimental.pallas import tpu as pltpu
from jax.sharding import PartitionSpec as P

SIGMA = 0.02
F32 = jnp.float32
BF16 = jnp.bfloat16
TX, TY = 16, 32
HX = 10
HY = 12
PX, RY = TX + 2 * HX, TY + 2 * HY
CHUNK = 4
PARTS = 2
VMEM_BYTES = 56 * 1024 * 1024


def cheb_steps(degree, lower):
    centre = 0.5 * (2.0 + lower)
    half = 0.5 * (2.0 - lower)
    sharp = centre / half
    ratio = 1.0 / sharp
    steps = []
    for _ in range(degree - 1):
        nxt = 1.0 / (2.0 * sharp - ratio)
        steps.append((nxt * ratio, 2.0 * nxt / half))
        ratio = nxt
    return 1.0 / centre, steps


SMOOTH = cheb_steps(3, 0.3)
COARSE = cheb_steps(24, 0.05)


def lane_match(z, q, source, target):
    bits = z.bit_length() - 1
    cell = (lax.shift_right_logical(source, bits) + (128 // z) * q) & -2
    inner = lax.shift_right_logical(source & (z - 1), 1)
    return jnp.where(cell * (z // 4) + inner == target, 1.0, 0.0).astype(BF16)


def restrict_map(z, planes=(0, 4)):
    shape = ((planes[1] - planes[0]) * 128, 128)
    row = lax.broadcasted_iota(jnp.int32, shape, 0)
    return lane_match(z, planes[0] + lax.shift_right_logical(row, 7), row & 127, lanes(shape))


def prolong_map(z, planes=(0, 4)):
    shape = (128, (planes[1] - planes[0]) * 128)
    column = lanes(shape)
    target = lax.broadcasted_iota(jnp.int32, shape, 0)
    return lane_match(z, planes[0] + lax.shift_right_logical(column, 7), column & 127, target)


def prolong_one(z, q):
    shape = (128, 128)
    return lane_match(z, q, lanes(shape), lax.broadcasted_iota(jnp.int32, shape, 0))


def pair_dot(value, matrix):
    rows = value.shape[0]
    high = value.astype(BF16).astype(F32)
    rest = value - high
    mid = rest.astype(BF16).astype(F32)
    parts = jnp.concatenate([high, mid, rest - mid], axis=0).astype(BF16)
    out = jnp.dot(parts, matrix, preferred_element_type=F32)
    return out[:rows] + (out[rows : 2 * rows] + out[2 * rows :])


def lanes(shape):
    return lax.broadcasted_iota(jnp.int32, shape, len(shape) - 1)


def turn(value, shift, axis):
    return pltpu.roll(value, shift % value.shape[axis], axis)


def next_x(v, z):
    if z == 128:
        return jnp.concatenate([v[1:], v[:1]], axis=0)
    a = turn(v, -z, 2)
    b = jnp.concatenate([a[1:], a[:1]], axis=0)
    return jnp.where(lanes(v.shape) < 128 - z, a, b)


def prev_x(v, z):
    if z == 128:
        return jnp.concatenate([v[-1:], v[:-1]], axis=0)
    a = turn(v, z, 2)
    b = jnp.concatenate([a[-1:], a[:-1]], axis=0)
    return jnp.where(lanes(v.shape) >= z, a, b)


def faces_of(k, step, scale, low, high):
    own = (0.5 * scale) * k
    both = own + (0.5 * scale) * step
    if low is None:
        return both, None
    edge = jnp.where(low | high, own, 0.0)
    return jnp.where(high, 0.0, both), edge


def build(k, scale, z, inside=None, edge_x=(None, None), edge_y=(None, None)):
    shape = k.shape
    cell = lanes(shape) & (z - 1)
    wx, ex = faces_of(k, next_x(k, z), scale, *edge_x)
    wy, ey = faces_of(k, turn(k, -1, 1), scale, *edge_y)
    wz, ez = faces_of(k, turn(k, -1, 2), scale, cell == 0, cell == z - 1)
    s = ez + SIGMA * scale
    if ex is not None:
        s = s + ex
    if ey is not None:
        s = s + ey
    diagonal = s + wx + prev_x(wx, z) + wy + turn(wy, 1, 1) + wz + turn(wz, 1, 2)
    rd = 1.0 / diagonal
    if inside is not None:
        rd = jnp.where(inside, rd, 0.0)
    return wx, wy, wz, s, rd


def remain(v, b, level, z):
    wx, wy, wz, s, _ = level
    fx = wx * (next_x(v, z) - v)
    fy = wy * (turn(v, -1, 1) - v)
    fz = wz * (turn(v, -1, 2) - v)
    total = (fx - prev_x(fx, z)) + (fy - turn(fy, 1, 1)) + (fz - turn(fz, 1, 2))
    return (b - s * v) + total


def smooth(x, b, level, z):
    first, steps = SMOOTH
    rd = level[4]
    if x is None:
        d = (b * rd) * first
        x = d
    else:
        d = (remain(x, b, level, z) * rd) * first
        x = x + d
    for keep, gain in steps:
        d = keep * d + gain * (remain(x, b, level, z) * rd)
        x = x + d
    return x


def within(shape, first_x, first_y, z, size_x, size_y):
    plane = lax.broadcasted_iota(jnp.int32, shape, 0)
    cx = first_x + plane * (128 // z) + lax.shift_right_logical(lanes(shape), z.bit_length() - 1)
    cy = first_y + lax.broadcasted_iota(jnp.int32, shape, 1)
    return (cx >= 0) & (cx < size_x) & (cy >= 0) & (cy < size_y)


def pair_rows(ref, plane, start, count):
    return ref[plane, pl.ds(start, count, stride=2), :] + ref[plane, pl.ds(start + 1, count, stride=2), :]


def spread_rows(ref, plane, start, value):
    count = value.shape[0]
    ref[plane, pl.ds(start, count, stride=2), :] = value
    ref[plane, pl.ds(start + 1, count, stride=2), :] = value


def insider(rows, first_x, first_y):
    row = lax.broadcasted_iota(jnp.int32, (CHUNK, rows, 128), 1) + first_y
    row_in = (row >= 0) & (row < 512)
    plane = lax.broadcasted_iota(jnp.int32, (CHUNK, rows, 128), 0) + first_x
    return lambda p: row_in & (plane >= -p) & (plane < 256 - p)


def build_top(k_ref, wx, wy, wz, s, rd, low, high, inside_at, body):
    rows = k_ref.shape[1]
    shape = (CHUNK, rows, 128)
    lane = lanes(shape)

    def step(i, wxp):
        p = low + i * CHUNK
        k = k_ref[pl.ds(p, CHUNK)]
        kn = jnp.concatenate([k[1:], k_ref[pl.ds(jnp.minimum(p + CHUNK, k_ref.shape[0] - 1), 1)]], axis=0)
        own = 0.5 * k
        fx = 0.5 * kn + own
        fy = turn(own, -1, 1) + own
        fz = jnp.where(lane == 127, 0.0, turn(own, -1, 2) + own)
        sv = SIGMA + jnp.where((lane == 0) | (lane == 127), own, 0.0)
        fxp = jnp.concatenate([wxp, fx[:-1]], axis=0)
        diagonal = sv + (fx + fxp) + (fy + turn(fy, 1, 1)) + (fz + turn(fz, 1, 2))
        rdv = jnp.where(inside_at(p), 1.0 / diagonal, 0.0)
        at = pl.ds(p, CHUNK)
        wx[at], wy[at], wz[at], s[at], rd[at] = fx, fy, fz, sv, rdv
        body(p, rdv)
        return fx[-1:]

    assert (high - low) % CHUNK == 0
    lax.fori_loop(0, (high - low) // CHUNK, step, jnp.zeros((1, rows, 128), F32))


def sweep_top(x, wx, wy, wz, s, low, high, body):
    size = (high - low) // PARTS
    fx0 = wx[low - 1 : low] * (x[low : low + 1] - x[low - 1 : low])

    def step(i, fxp):
        p = low + i * size
        at = pl.ds(p, size)
        v = x[at]
        vn = jnp.concatenate([v[1:], x[pl.ds(p + size, 1)]], axis=0)
        fx = wx[at] * (vn - v)
        fy = wy[at] * (turn(v, -1, 1) - v)
        fz = wz[at] * (turn(v, -1, 2) - v)
        fxp = jnp.concatenate([fxp, fx[:-1]], axis=0)
        total = (fx - fxp) + (fy - turn(fy, 1, 1)) + (fz - turn(fz, 1, 2))
        body(p, at, v, s[at] * v - total)
        return fx[-1:]

    assert (high - low) % PARTS == 0
    lax.fori_loop(0, PARTS, step, fx0, unroll=True)


class Pick:
    def __init__(self, take_first, first, second):
        self.take_first, self.first, self.second = take_first, first, second

    def __getitem__(self, index):
        return jnp.where(self.take_first, self.first[index], self.second[index])


def sides(at, first, second):
    odd = (at & 1) == 1
    return Pick(odd, first, second), Pick(odd, second, first)


def fill_top(dst, number, wide, below, above):
    dst[:, 0:2, :] = jnp.zeros((PX, 2, 128), F32)
    dst[:, RY - 2 : RY, :] = jnp.zeros((PX, 2, 128), F32)
    dst[:, HY : HY + TY, :] = wide[number]
    for p in range(PX):
        part = slice(HX * (PX * number + p), HX * (PX * number + p + 1))
        dst[p, 2:HY, :] = below[part]
        dst[p, HY + TY : RY - 2, :] = above[part]


def down_kernel(pos, wide, by_y, by_y2, one, two, *refs):
    given, (bx, kx, x, wx, wy, wz, s, rd, d, rs, b1s, x1s, k1s, sems) = refs[:3], refs[3:]
    keeping = moves((bx, kx, x), given, sems)
    gx, gy = pos[0], pos[1]
    inside_at = insider(RY, gx * TX - HX, gy * TY - HY)
    below, above = sides(gy, by_y, by_y2)
    fill_top(bx, 0, wide, below, above)
    fill_top(kx, 1, wide, below, above)

    def clear(i, _):
        at = pl.ds(i * CHUNK, CHUNK)
        kx[at] = jnp.where(inside_at(i * CHUNK), kx[at], 0.0)
        return 0

    lax.fori_loop(0, PX // CHUNK, clear, 0)
    for move in keeping[:2]:
        move.start()
    start, steps = SMOOTH

    def begin(p, rdv):
        at = pl.ds(p, CHUNK)
        v = (bx[at] * rdv) * start
        d[at] = v
        x[at] = v

    build_top(kx, wx, wy, wz, s, rd, 0, PX, inside_at, begin)
    for keep, gain in steps:
        sweep_top(x, wx, wy, wz, s, 2, PX - 2, advance_top(keep, gain, bx, 0, rd, d, x))

    def residual(p, at, v, av):
        d[at] = bx[at] - av

    keeping[2].start()
    sweep_top(x, wx, wy, wz, s, 4, PX - 4, residual)

    def coarse(src):
        for c in range(16):
            rs[c] = src[2 + 2 * c] + src[3 + 2 * c]
        return pair_planes(rs, 8, 4, 24)

    for p in (2, 3, PX - 4, PX - 3):
        d[p] = jnp.zeros((RY, 128), F32)
    b1 = coarse(d)
    k1 = coarse(kx)
    level = build(k1, 0.25, 64, within(k1.shape, gx * 8 - 4, gy * 16 - 4, 64, 128, 256))
    x1 = smooth(None, b1, level, 64)
    b1s[...] = b1
    x1s[...] = x1
    k1s[...] = k1
    for number, src in enumerate((b1s, x1s, k1s)):
        one[number] = src[2:6, 4:20, :]
    b1s[...] = remain(x1, b1, level, 64)
    send_all(two, coarse_tile((b1s, k1s), 2, 4))
    for move in keeping:
        move.wait()


def moves(sources, targets, sems):
    return [pltpu.make_async_copy(a, b, sems.at[i]) for i, (a, b) in enumerate(zip(sources, targets))]


def pair_planes(rs, planes, start, rows):
    flat = [
        jnp.concatenate([pair_rows(rs, 2 * c, start, rows), pair_rows(rs, 2 * c + 1, start, rows)], axis=1)
        for c in range(planes)
    ]
    out = 0.125 * pair_dot(jnp.concatenate(flat, axis=0), restrict_map(128, (1, 3)))
    return out.reshape(planes, rows, 128)


def coarse_tile(sources, plane, row):
    flat = [
        jnp.concatenate([pair_rows(src, plane + q, row, 8) for q in range(4)], axis=1) for src in sources
    ]
    out = 0.125 * pair_dot(jnp.concatenate(flat, axis=0), restrict_map(64))
    return out.reshape(len(sources), 8, 128)


def send_all(out, value):
    for g in range(16):
        out[g] = value


def advance_top(keep, gain, b, shift_b, rd, d, x):
    def advance(p, at, v, av):
        dv = keep * d[at] + gain * ((b[pl.ds(p - shift_b, v.shape[0])] - av) * rd[at])
        d[at] = dv
        x[at] = v + dv

    return advance


def open_top(b, shift_b, rd, d, x):
    def advance(p, at, v, av):
        dv = ((b[pl.ds(p - shift_b, v.shape[0])] - av) * rd[at]) * SMOOTH[0]
        d[at] = dv
        x[at] = v + dv

    return advance


def call(kernel, outs, scratch, *args, far_in=0, far_out=0, copies=0):
    near, far = pl.BlockSpec(memory_space=pltpu.VMEM), pl.BlockSpec(memory_space=pl.ANY)
    specs = [pl.BlockSpec(memory_space=pltpu.SMEM)] + [near] * (len(args) - 1 - far_in) + [far] * far_in
    return pl.pallas_call(
        kernel,
        out_shape=[jax.ShapeDtypeStruct(o, F32) for o in outs],
        in_specs=specs,
        out_specs=[near] * (len(outs) - far_out) + [far] * far_out,
        scratch_shapes=[pltpu.VMEM(o, F32) for o in scratch]
        + ([pltpu.SemaphoreType.DMA((copies,))] if copies else []),
        compiler_params=pltpu.CompilerParams(vmem_limit_bytes=VMEM_BYTES),
        cost_estimate=pl.CostEstimate(flops=10**7, bytes_accessed=8 << 20, transcendentals=0),
    )(*args)


def go_down(*args):
    top = (PX, RY, 128)
    outs = [(3, 4, 16, 128), (16, 2, 8, 128)] + [top] * 3
    scratch = [top] * 9 + [(16, RY, 128)] + [(8, 24, 128)] * 3
    return call(down_kernel, outs, scratch, *args, far_out=3, copies=3)


def one_kernel(pos, mid, by_x, by_x2, by_y, by_y2, k1, bout, xout, two, res):
    gx, gy = pos[0], pos[1]
    left, right = sides(gx, by_x, by_x2)
    below, above = sides(gy, by_y, by_y2)
    head = (slice(None), slice(0, 16))
    fill_one(bout, left[head], mid[...], right[head], below[...], above[...])
    b = bout[...]
    inside = within(b.shape, gx * 8 - 8, gy * 16 - 8, 64, 128, 256)
    level = build(k1[...], 0.25, 64, inside)
    x = smooth(None, b, level, 64)
    xout[...] = x
    res[...] = remain(x, b, level, 64)
    send_all(two, coarse_tile((res,), 4, 8))


def fill_one(dst, left, tile, right, below, above):
    dst[0:4, 8:24, :] = left
    dst[4:8, 8:24, :] = tile
    dst[8:12, 8:24, :] = right
    dst[:, 0:8, :] = below
    dst[:, 24:32, :] = above


def go_one(*args):
    wide = (12, 32, 128)
    return call(one_kernel, [wide, wide, (16, 1, 8, 128)], [wide], *args)


def mid_kernel(first, pos, mid, by_y, by_y2, *refs):
    if first:
        near, three, k2 = refs[:3]
        scratch = refs[3:]
    else:
        k2, near, three = refs[:3]
        scratch = refs[3:]
    hold, rs, cs, edge = scratch
    gx, gy = pos[0], pos[1]
    below, above = sides(gy, by_y, by_y2)
    shape = (16, 24, 128)
    inside = within(shape, 0, gy * 8 - 8, 32, 64, 128)

    def rows(dst, number):
        part = slice(16 * number, 16 * number + 16)
        dst[:, 0:8, :] = below[part]
        dst[:, 8:16, :] = mid[:, number]
        dst[:, 16:24, :] = above[part]

    rows(rs, 0)
    b = rs[...]
    if first:
        rows(k2, 1)
        k2[...] = jnp.where(inside, k2[...], 0.0)
    k = k2[...]
    plane = lax.broadcasted_iota(jnp.int32, shape, 0)
    lane = lanes(shape)
    edge_x = ((plane == 0) & (lane < 32), (plane == 15) & (lane >= 96))
    level = build(k, 0.25**2, 32, inside, edge_x)
    x = smooth(None, b, level, 32)
    rs[...] = remain(x, b, level, 32)
    for number, value in enumerate((b, x, k)):
        hold[number] = value
    for i in range(5):
        at = gx - 2 + i
        ok = (at >= 0) & (at < 16)
        from_plane = jnp.clip(at, 0, 15)
        for number in range(3):
            near[number, i] = jnp.where(ok, hold[number, from_plane], 0.0)

    if first:
        for i in range(5):
            edge[0, i : i + 1, :] = near[1, i, 9:10, :]
            edge[1, i : i + 1, :] = near[1, i, 14:15, :]
        upper = lax.rem(gy + 1, 16)
        for g in range(16):
            three[g, 4] = jnp.where(upper == g, edge[0], edge[1])

    def coarse(src, out):
        flat = [
            jnp.concatenate([pair_rows(src, 4 * c + q, 4, 8) for q in range(4)], axis=1) for c in range(4)
        ]
        cs[...] = (0.125 * pair_dot(jnp.concatenate(flat, axis=0), restrict_map(32))).reshape(4, 8, 128)
        for c in range(4):
            part = cs[c, 2:6, :]
            for g in range(16):
                three[g, out + c // 2, 4 * (c % 2) : 4 * (c % 2) + 4, :] = part

    coarse(rs, 0)
    if first:
        coarse(k2, 2)


def go_mid(first, pos, mid, below, above, k2):
    outs = [(3, 5, 24, 128), (16, 5 if first else 2, 8, 128)]
    outs += [(16, 24, 128)] if first else []
    scratch = [(3, 16, 24, 128), (16, 24, 128), (4, 8, 128), (2, 8, 128)]
    args = (mid, below, above) + (() if first else (k2,))
    return call(functools.partial(mid_kernel, first), outs, scratch, pos, *args)


def solve_last(b, k, owned):
    shape = k.shape
    scale = 0.25**4
    lane = lanes(shape)
    row = lax.broadcasted_iota(jnp.int32, shape, 0)
    moves = (
        (8, 1, lane < 8, True),
        (-8, 1, lane >= 120, True),
        (1, 0, row == 0, True),
        (-1, 0, row == 31, True),
        (1, 1, (lane & 7) == 0, False),
        (-1, 1, (lane & 7) == 7, False),
    )
    diagonal = jnp.full(shape, SIGMA * scale, F32)
    pulls = []
    for shift, axis, edge, masked in moves:
        weight = (0.5 * scale) * (k + jnp.where(edge, 0.0, turn(k, shift, axis)))
        diagonal = diagonal + weight
        keep = jnp.where(edge, 0.0, weight)
        if masked:
            keep = jnp.where(owned == turn(owned, shift, axis), keep, 0.0)
        pulls.append(keep)
    rd = 1.0 / diagonal
    pulls = [keep * rd for keep in pulls]
    g = b * rd
    first, steps = COARSE
    d = g * first
    x = d
    for keep, gain in steps:
        total = [pull * turn(x, move[0], move[1]) for pull, move in zip(pulls, moves)]
        near = (total[0] + total[1]) + (total[2] + total[3]) + (total[4] + total[5])
        d = keep * d + gain * ((g - x) + near)
        x = x + d
    return x


def fill_three(dst, gathered, first):
    for g in range(16):
        for c in range(4):
            part = gathered[g, first + c // 2, 4 * (c % 2) : 4 * (c % 2) + 4, :]
            dst[c, 4 * g : 4 * g + 4, :] = part


def solve_three(b_ref, k_ref, owned, s3):
    shape = (4, 64, 128)
    plane = lax.broadcasted_iota(jnp.int32, shape, 0)
    row = lax.broadcasted_iota(jnp.int32, shape, 1)
    lane = lanes(shape)
    edge_x = ((plane == 0) & (lane < 16), (plane == 3) & (lane >= 112))
    level = build(k_ref[...], 0.25**3, 16, None, edge_x, (row == 0, row == 63))
    b = b_ref[...]
    x = smooth(None, b, level, 16)
    s3[:, 8:72, :] = remain(x, b, level, 16)
    flat = [
        jnp.concatenate([pair_rows(src, q, row0, 32) for q in range(4)], axis=1) for src, row0 in ((s3, 8), (k_ref, 0))
    ]
    fine = 0.125 * pair_dot(jnp.concatenate(flat, axis=0), restrict_map(16))
    last = solve_last(fine[:32], fine[32:], owned[...])
    back = pair_dot(last, prolong_map(16))
    for q in range(4):
        spread_rows(s3, q, 8, back[:, 128 * q : 128 * q + 128])
    s3[:, 8:72, :] = smooth(x + s3[:, 8:72, :], b, level, 16)


def rise_two(gx, gy, near, x2, s3, e2, s2):
    pair = lax.shift_right_logical(gy + 1, 1)
    rows = pl.ds(pl.multiple_of(pair * 8, 8), 24)
    for i in range(5):
        at = jnp.clip(gx - 2 + i, 0, 15)
        spread_rows(e2, i, 0, pair_dot(s3[at // 4, rows, :], prolong_one(32, at % 4)))
    e = e2[:, pl.ds(pl.multiple_of((gy + 1 - 2 * pair) * 8, 8), 24), :]
    shape = (5, 24, 128)
    inside = within(shape, gx * 4 - 8, gy * 8 - 8, 32, 64, 128)
    level = build(near[2], 0.25**2, 32, inside)
    s2[...] = smooth(jnp.where(inside, x2 + e, 0.0), near[0], level, 32)


def rise_one(x1, b1, k1, inside, s2, s1):
    flat = jnp.concatenate([s2[i, 4:20, :] for i in range(1, 4)], axis=0)
    back = pair_dot(flat, prolong_map(64))
    for i in range(3):
        for q in range(4):
            spread_rows(s1, 4 * i + q, 0, back[16 * i : 16 * i + 16, 128 * q : 128 * q + 128])
    level = build(k1, 0.25, 64, inside)
    s1[...] = smooth(jnp.where(inside, x1 + s1[...], 0.0), b1, level, 64)


def spread_one(s1, low, high, e0):
    flat = jnp.concatenate([s1[i, 4:28, :] for i in range(low, high)], axis=0)
    back = pair_dot(flat, prolong_map(128, (1, 3)))
    for i in range(high - low):
        for q in range(2):
            part = back[24 * i : 24 * i + 24, 128 * q : 128 * q + 128]
            spread_rows(e0, 2 * (low - 2 + i) + q, 4, part)
    e0[:, 0:4, :] = jnp.zeros((16, 4, 128), F32)
    e0[:, RY - 4 : RY, :] = jnp.zeros((16, 4, 128), F32)


def add_top(x0, e0, x):
    def begin(p, rdv):
        c = (p - 2) // 2
        pair = (e0[pl.ds(c, 1)], e0[pl.ds(c + 1, 1)])
        correction = jnp.concatenate([pair[0], pair[0], pair[1], pair[1]], axis=0)
        at = pl.ds(p, CHUNK)
        x[at] = jnp.where(rdv > 0.0, x0[at] + correction, 0.0)

    return begin


def turn_kernel(
    pos, owned, three, *refs
):
    gx, gy = pos[0], pos[1]
    fars, (b1n, send, send2, *far_outs) = refs[:9], refs[9:17]
    b3, s3, e2, s2, x2s, b1s, s1, e0, d, x, rs, xout, rout, k3, k1, x0n = refs[17:33]
    tops, (wx, wy, wz, s, rd), sems = refs[33:42], refs[42:47], refs[47]
    near, one, by_x, by_x2, by_y, by_y2, b0, k0, x0 = tops
    left, right = sides(gx, by_x, by_x2)
    below, above = sides(gy, by_y, by_y2)
    part = pl.ds(32, 36)
    loads = moves(fars[:4] + (fars[4].at[part], fars[5].at[part]) + fars[6:], tops, sems)
    for move in loads:
        move.start()
    keeps = xkeep, rkeep, kkeep, k1keep, x0keep = [
        pltpu.make_async_copy(a, b, sems.at[9 + i])
        for i, (a, b) in enumerate(zip((xout, rout, k3, k1, x0n), far_outs))
    ]
    fill_three(b3, three, 0)
    fill_three(k3, three, 2)
    kkeep.start()
    solve_three(b3, k3, owned, s3)
    loads[0].wait()
    x2s[...] = near[1]
    lower, upper = lax.rem(gy + 15, 16), lax.rem(gy + 1, 16)
    for i in range(5):
        x2s[i, 1:2, :] = three[lower, 4, i : i + 1, :]
        x2s[i, 22:23, :] = three[upper, 4, i : i + 1, :]
    rise_two(gx, gy, near, x2s[...], s3, e2, s2)

    for move in loads[1:6]:
        move.wait()
    inside = within((12, 32, 128), gx * 8 - 8, gy * 16 - 8, 64, 128, 256)
    for number, dst in enumerate((b1s, s1, k1)):
        part = slice(12 * number, 12 * number + 12)
        fill_one(dst, left[number], one[number], right[number], below[part], above[part])
    k1[...] = jnp.where(inside, k1[...], 0.0)
    k1keep.start()
    rise_one(s1[...], b1s[...], k1[...], inside, s2, s1)

    spread_one(s1, 2, 10, e0)
    for move in loads[6:]:
        move.wait()
    inside_at = insider(RY, gx * TX - HX, gy * TY - HY)
    build_top(k0, wx, wy, wz, s, rd, 2, PX - 2, inside_at, add_top(x0, e0, x))
    start, steps = SMOOTH
    sweep_top(x, wx, wy, wz, s, 4, PX - 4, open_top(b0, 0, rd, d, x))
    for (keep, gain), edge in zip(steps, (4, 6)):
        sweep_top(x, wx, wy, wz, s, edge, PX - edge, advance_top(keep, gain, b0, 0, rd, d, x))

    def residual(p, at, v, av):
        rout[pl.ds(p - 6, v.shape[0])] = b0[at] - av

    sweep_top(x, wx, wy, wz, s, 6, PX - 6, residual)
    xout[...] = x[9 : PX - 9]
    xkeep.start()
    rkeep.start()

    def begin(i, _):
        at = pl.ds(6 + i * CHUNK, CHUNK)
        v = (rout[pl.ds(i * CHUNK, CHUNK)] * rd[at]) * start
        d[at] = v
        x[at] = v
        return 0

    lax.fori_loop(0, (PX - 12) // CHUNK, begin, 0)
    for keep, gain in steps:
        sweep_top(x, wx, wy, wz, s, 8, PX - 8, advance_top(keep, gain, rout, 6, rd, d, x))

    def again(p, at, v, av):
        d[at] = rout[pl.ds(p - 6, v.shape[0])] - av

    x0n[...] = x[HX : HX + TX, HY : HY + TY, :]
    x0keep.start()
    sweep_top(x, wx, wy, wz, s, HX, HX + TX, again)
    for c in range(8):
        rs[c] = d[HX + 2 * c] + d[HX + 1 + 2 * c]
    b1 = pair_planes(rs, 4, HY, 16)
    b1n[...] = b1
    odd = (gx & 1) == 1
    for side, of_odd, of_even in ((send, HX, HX + TX - 4), (send2, HX + TX - 4, HX)):
        side[:, 0:16, :] = b1
        side[:, 16:48, :] = x[pl.ds(jnp.where(odd, of_odd, of_even), 4), HY : HY + TY, :]
    for move in keeps:
        move.wait()


def go_turn(*args):
    top, wide, three, one = (PX, RY, 128), (12, 32, 128), (4, 64, 128), (3, 4, 16, 128)
    kept = [(TX + 2, RY, 128), (TX + 8, RY, 128), three, wide, (TX, TY, 128)]
    outs = [(4, 16, 128), (4, 48, 128), (4, 48, 128)] + kept
    scratch = [three, (4, 88, 128), (5, 48, 128), (5, 24, 128), (5, 24, 128), wide, wide, (16, RY, 128)]
    scratch += [top] * 2 + [(8, RY, 128)] + kept + [(3, 5, 24, 128)] + [one] * 3 + [(36, 8, 128)] * 2 + [top] * 8
    return call(turn_kernel, outs, scratch, *args, far_in=9, far_out=5, copies=14)


def last_kernel(
    pos, owned, three, k3, *refs
):
    gx, gy = pos[0], pos[1]
    fars, far_outs, (b3, s3, e2, s2, s1, e0, d, x) = refs[:13], refs[13:15], refs[15:23]
    tops, (wx, wy, wz, s, rd, xout, rout), sems = refs[23:36], refs[36:43], refs[43]
    near, b1, x1, k1, by_x, by_x2, by_y, by_y2, x0n, k0, r, xbefore, borig = tops
    left, right = sides(gx, by_x, by_x2)
    below, above = sides(gy, by_y, by_y2)
    part = pl.ds(16, 24)
    loads = moves(fars[:6] + (fars[6].at[part], fars[7].at[part]) + fars[8:], tops, sems)
    for move in loads:
        move.start()
    keeps = [
        pltpu.make_async_copy(a, b, sems.at[13 + i]) for i, (a, b) in enumerate(zip((xout, rout), far_outs))
    ]
    fill_three(b3, three, 0)
    solve_three(b3, k3, owned, s3)
    loads[0].wait()
    rise_two(gx, gy, near, near[1], s3, e2, s2)
    for move in loads[1:4]:
        move.wait()
    inside = within((12, 32, 128), gx * 8 - 8, gy * 16 - 8, 64, 128, 256)
    rise_one(x1[...], b1[...], k1[...], inside, s2, s1)

    spread_one(s1, 3, 9, e0)
    for move in loads[4:]:
        move.wait()
    low, high = HX - 4, HX + TX + 4
    x[low:HX, HY : HY + TY, :] = left[:, 16:48, :]
    x[HX : HX + TX, HY : HY + TY, :] = x0n[...]
    x[HX + TX : high, HY : HY + TY, :] = right[:, 16:48, :]
    x[low:high, HY - 8 : HY, :] = below[...]
    x[low:high, HY + TY : HY + TY + 8, :] = above[...]
    x[low:high, 0 : HY - 8, :] = jnp.zeros((high - low, HY - 8, 128), F32)
    x[low:high, RY - 4 : RY, :] = jnp.zeros((high - low, 4, 128), F32)
    inside_at = insider(RY, gx * TX - HX, gy * TY - HY)
    build_top(k0, wx, wy, wz, s, rd, low, high, inside_at, add_top(x, e0, x))
    sweep_top(x, wx, wy, wz, s, low, high, open_top(r, low, rd, d, x))
    for keep, gain in SMOOTH[1]:
        sweep_top(x, wx, wy, wz, s, 8, PX - 8, advance_top(keep, gain, r, low, rd, d, x))
    x[9 : PX - 9] = x[9 : PX - 9] + xbefore[...]

    def residual(p, at, v, av):
        d[at] = av

    xout[...] = x[HX : HX + TX, HY : HY + TY, :]
    keeps[0].start()
    sweep_top(x, wx, wy, wz, s, HX, HX + TX, residual)
    rout[...] = borig[...] - d[HX : HX + TX, HY : HY + TY, :]
    keeps[1].start()
    for move in keeps:
        move.wait()


def go_last(*args):
    top, wide, tile = (PX, RY, 128), (12, 32, 128), (TX, TY, 128)
    scratch = [(4, 64, 128), (4, 88, 128), (5, 48, 128), (5, 24, 128), wide, (16, RY, 128)] + [top] * 2
    scratch += [(3, 5, 24, 128)] + [wide] * 3 + [(4, 48, 128)] * 2 + [(24, 8, 128)] * 2
    scratch += [tile, top, (TX + 8, RY, 128), (TX + 2, RY, 128), tile] + [top] * 5 + [tile] * 2
    return call(last_kernel, [tile, tile], scratch, *args, far_in=13, far_out=2, copies=15)


def swap(low, high, axis):
    count = lax.axis_size(axis)
    odd = lax.axis_index(axis) % 2 == 1
    first = jnp.where(odd, low, high) if low is not high else low
    second = jnp.where(odd, high, low) if low is not high else low
    return (
        lax.ppermute(first, axis, [(i, i ^ 1) for i in range(count)]),
        lax.ppermute(second, axis, [(i, (i + 1 if i % 2 else i - 1) % count) for i in range(count)]),
    )


def apart(first, second, axis):
    odd = lax.axis_index(axis) % 2 == 1
    return jnp.where(odd, first, second), jnp.where(odd, second, first)


def gather(copies, axis):
    return lax.all_to_all(copies, axis, 0, 0, tiled=True)


def local(right_side, kappa, owners):
    pos = jnp.stack([lax.axis_index("gx"), lax.axis_index("gy")]).astype(jnp.int32)
    owned = jnp.repeat(jnp.repeat(owners.T, 2, 0), 8, 1).astype(F32)
    mid = jnp.stack([right_side, kappa])
    left, right = apart(*swap(mid[:, :HX], mid[:, TX - HX :], "gx"), "gx")
    wide = jnp.concatenate([left, mid, right], axis=1)
    low, high = (part.reshape(-1, 128) for part in (wide[:, :, :HX], wide[:, :, TY - HX :]))
    one, two, b0, k0, x0 = go_down(pos, wide, *swap(low, high, "gy"))
    by_x = swap(one, one, "gx")
    two = gather(two, "gx")
    left, right = apart(*by_x, "gx")
    rows = jnp.swapaxes(two, 0, 1).reshape(-1, 8, 128)
    wide = jnp.concatenate([left, one, right], axis=1)
    low, high = (
        jnp.concatenate([rows, part.reshape(-1, 8, 128)]) for part in (wide[:, :, :8], wide[:, :, 8:])
    )
    by_y = swap(low, high, "gy")
    near, three, k2 = go_mid(True, pos, two, *by_y, None)
    three = gather(three, "gy")
    b1n, send, send2, xbefore, source, k3, k1, x0n = go_turn(
        pos, owned, three, near, one, *by_x, *by_y, b0, k0, x0
    )

    by_x = (
        lax.ppermute(send, "gx", [(i, i ^ 1) for i in range(16)]),
        lax.ppermute(send2, "gx", [(i, (i + 1 if i % 2 else i - 1) % 16) for i in range(16)]),
    )
    left, right = apart(*by_x, "gx")
    wide = jnp.concatenate([left[:, :16], b1n, right[:, :16]])
    b1, x1, two = go_one(pos, b1n, *by_x, *swap(wide[:, :8], wide[:, 8:], "gy"), k1)
    two = gather(two, "gx")
    wide = jnp.concatenate([left[:, 16:], x0n, right[:, 16:]])
    low, high = (jnp.concatenate([two[:, 0], part]) for part in (wide[:, :8], wide[:, 24:]))
    by_y = swap(low, high, "gy")
    near, three = go_mid(False, pos, two, *by_y, k2)
    three = gather(three, "gy")
    field, residual = go_last(
        pos, owned, three, k3, near, b1, x1, k1, *by_x, *by_y, x0n, k0, source, xbefore, right_side
    )
    return field, residual


def solution(mesh):
    spec = P("gx", "gy", None)
    return jax.shard_map(
        local, mesh=mesh, in_specs=(spec, spec, P()), out_specs=(spec, spec), check_vma=False
    )
```

```python
import functools

import jax
import jax.numpy as jnp
from jax import lax
from jax.experimental import pallas as pl
from jax.experimental.pallas import tpu as pltpu
from jax.sharding import PartitionSpec as P

SIGMA = 0.02
F32 = jnp.float32
BF16 = jnp.bfloat16
TX, TY = 16, 32
HX = 10
HY = 12
PX, RY = TX + 2 * HX, TY + 2 * HY
CHUNK = 4
PARTS = 2
VMEM_BYTES = 56 * 1024 * 1024


def cheb_steps(degree, lower):
    centre = 0.5 * (2.0 + lower)
    half = 0.5 * (2.0 - lower)
    sharp = centre / half
    ratio = 1.0 / sharp
    steps = []
    for _ in range(degree - 1):
        nxt = 1.0 / (2.0 * sharp - ratio)
        steps.append((nxt * ratio, 2.0 * nxt / half))
        ratio = nxt
    return 1.0 / centre, steps


SMOOTH = cheb_steps(3, 0.3)
COARSE = cheb_steps(24, 0.05)


def lane_match(z, q, source, target):
    bits = z.bit_length() - 1
    cell = (lax.shift_right_logical(source, bits) + (128 // z) * q) & -2
    inner = lax.shift_right_logical(source & (z - 1), 1)
    return jnp.where(cell * (z // 4) + inner == target, 1.0, 0.0).astype(BF16)


def restrict_map(z, planes=(0, 4)):
    shape = ((planes[1] - planes[0]) * 128, 128)
    row = lax.broadcasted_iota(jnp.int32, shape, 0)
    return lane_match(z, planes[0] + lax.shift_right_logical(row, 7), row & 127, lanes(shape))


def prolong_map(z, planes=(0, 4)):
    shape = (128, (planes[1] - planes[0]) * 128)
    column = lanes(shape)
    target = lax.broadcasted_iota(jnp.int32, shape, 0)
    return lane_match(z, planes[0] + lax.shift_right_logical(column, 7), column & 127, target)


def prolong_one(z, q):
    shape = (128, 128)
    return lane_match(z, q, lanes(shape), lax.broadcasted_iota(jnp.int32, shape, 0))


def pair_dot(value, matrix):
    rows = value.shape[0]
    high = value.astype(BF16).astype(F32)
    rest = value - high
    mid = rest.astype(BF16).astype(F32)
    parts = jnp.concatenate([high, mid, rest - mid], axis=0).astype(BF16)
    out = jnp.dot(parts, matrix, preferred_element_type=F32)
    return out[:rows] + (out[rows : 2 * rows] + out[2 * rows :])


def lanes(shape):
    return lax.broadcasted_iota(jnp.int32, shape, len(shape) - 1)


def turn(value, shift, axis):
    return pltpu.roll(value, shift % value.shape[axis], axis)


def next_x(v, z):
    if z == 128:
        return jnp.concatenate([v[1:], v[:1]], axis=0)
    a = turn(v, -z, 2)
    b = jnp.concatenate([a[1:], a[:1]], axis=0)
    return jnp.where(lanes(v.shape) < 128 - z, a, b)


def prev_x(v, z):
    if z == 128:
        return jnp.concatenate([v[-1:], v[:-1]], axis=0)
    a = turn(v, z, 2)
    b = jnp.concatenate([a[-1:], a[:-1]], axis=0)
    return jnp.where(lanes(v.shape) >= z, a, b)


def faces_of(k, step, scale, low, high):
    own = (0.5 * scale) * k
    both = own + (0.5 * scale) * step
    if low is None:
        return both, None
    edge = jnp.where(low | high, own, 0.0)
    return jnp.where(high, 0.0, both), edge


def build(k, scale, z, inside=None, edge_x=(None, None), edge_y=(None, None)):
    shape = k.shape
    cell = lanes(shape) & (z - 1)
    wx, ex = faces_of(k, next_x(k, z), scale, *edge_x)
    wy, ey = faces_of(k, turn(k, -1, 1), scale, *edge_y)
    wz, ez = faces_of(k, turn(k, -1, 2), scale, cell == 0, cell == z - 1)
    s = ez + SIGMA * scale
    if ex is not None:
        s = s + ex
    if ey is not None:
        s = s + ey
    diagonal = s + wx + prev_x(wx, z) + wy + turn(wy, 1, 1) + wz + turn(wz, 1, 2)
    rd = 1.0 / diagonal
    if inside is not None:
        rd = jnp.where(inside, rd, 0.0)
    return wx, wy, wz, s, rd


def remain(v, b, level, z):
    wx, wy, wz, s, _ = level
    fx = wx * (next_x(v, z) - v)
    fy = wy * (turn(v, -1, 1) - v)
    fz = wz * (turn(v, -1, 2) - v)
    total = (fx - prev_x(fx, z)) + (fy - turn(fy, 1, 1)) + (fz - turn(fz, 1, 2))
    return (b - s * v) + total


def smooth(x, b, level, z):
    first, steps = SMOOTH
    rd = level[4]
    if x is None:
        d = (b * rd) * first
        x = d
    else:
        d = (remain(x, b, level, z) * rd) * first
        x = x + d
    for keep, gain in steps:
        d = keep * d + gain * (remain(x, b, level, z) * rd)
        x = x + d
    return x


def within(shape, first_x, first_y, z, size_x, size_y):
    plane = lax.broadcasted_iota(jnp.int32, shape, 0)
    cx = first_x + plane * (128 // z) + lax.shift_right_logical(lanes(shape), z.bit_length() - 1)
    cy = first_y + lax.broadcasted_iota(jnp.int32, shape, 1)
    return (cx >= 0) & (cx < size_x) & (cy >= 0) & (cy < size_y)


def pair_rows(ref, plane, start, count):
    return ref[plane, pl.ds(start, count, stride=2), :] + ref[plane, pl.ds(start + 1, count, stride=2), :]


def spread_rows(ref, plane, start, value):
    count = value.shape[0]
    ref[plane, pl.ds(start, count, stride=2), :] = value
    ref[plane, pl.ds(start + 1, count, stride=2), :] = value


def insider(rows, first_x, first_y):
    row = lax.broadcasted_iota(jnp.int32, (CHUNK, rows, 128), 1) + first_y
    row_in = (row >= 0) & (row < 512)
    plane = lax.broadcasted_iota(jnp.int32, (CHUNK, rows, 128), 0) + first_x
    return lambda p: row_in & (plane >= -p) & (plane < 256 - p)


def build_top(k_ref, wx, wy, wz, s, rd, low, high, inside_at, body):
    rows = k_ref.shape[1]
    shape = (CHUNK, rows, 128)
    lane = lanes(shape)

    def step(i, wxp):
        p = low + i * CHUNK
        k = k_ref[pl.ds(p, CHUNK)]
        kn = jnp.concatenate([k[1:], k_ref[pl.ds(jnp.minimum(p + CHUNK, k_ref.shape[0] - 1), 1)]], axis=0)
        own = 0.5 * k
        fx = 0.5 * kn + own
        fy = turn(own, -1, 1) + own
        fz = jnp.where(lane == 127, 0.0, turn(own, -1, 2) + own)
        sv = SIGMA + jnp.where((lane == 0) | (lane == 127), own, 0.0)
        fxp = jnp.concatenate([wxp, fx[:-1]], axis=0)
        diagonal = sv + (fx + fxp) + (fy + turn(fy, 1, 1)) + (fz + turn(fz, 1, 2))
        rdv = jnp.where(inside_at(p), 1.0 / diagonal, 0.0)
        at = pl.ds(p, CHUNK)
        wx[at], wy[at], wz[at], s[at], rd[at] = fx, fy, fz, sv, rdv
        body(p, rdv)
        return fx[-1:]

    assert (high - low) % CHUNK == 0
    lax.fori_loop(0, (high - low) // CHUNK, step, jnp.zeros((1, rows, 128), F32), unroll=True)


def sweep_top(x, wx, wy, wz, s, low, high, body):
    size = (high - low) // PARTS
    fx0 = wx[low - 1 : low] * (x[low : low + 1] - x[low - 1 : low])

    def step(i, fxp):
        p = low + i * size
        at = pl.ds(p, size)
        v = x[at]
        vn = jnp.concatenate([v[1:], x[pl.ds(p + size, 1)]], axis=0)
        fx = wx[at] * (vn - v)
        fy = wy[at] * (turn(v, -1, 1) - v)
        fz = wz[at] * (turn(v, -1, 2) - v)
        fxp = jnp.concatenate([fxp, fx[:-1]], axis=0)
        total = (fx - fxp) + (fy - turn(fy, 1, 1)) + (fz - turn(fz, 1, 2))
        body(p, at, v, s[at] * v - total)
        return fx[-1:]

    assert (high - low) % PARTS == 0
    lax.fori_loop(0, PARTS, step, fx0, unroll=True)


class Pick:
    def __init__(self, take_first, first, second):
        self.take_first, self.first, self.second = take_first, first, second

    def __getitem__(self, index):
        return jnp.where(self.take_first, self.first[index], self.second[index])


def sides(at, first, second):
    odd = (at & 1) == 1
    return Pick(odd, first, second), Pick(odd, second, first)


def fill_top(dst, number, wide, below, above):
    dst[:, 0:2, :] = jnp.zeros((PX, 2, 128), F32)
    dst[:, RY - 2 : RY, :] = jnp.zeros((PX, 2, 128), F32)
    dst[:, HY : HY + TY, :] = wide[number]
    for p in range(PX):
        part = slice(HX * (PX * number + p), HX * (PX * number + p + 1))
        dst[p, 2:HY, :] = below[part]
        dst[p, HY + TY : RY - 2, :] = above[part]


def down_kernel(pos, wide, by_y, by_y2, one, two, *refs):
    given, (bx, kx, x, wx, wy, wz, s, rd, d, rs, b1s, x1s, k1s, sems) = refs[:3], refs[3:]
    keeping = moves((bx, kx, x), given, sems)
    gx, gy = pos[0], pos[1]
    inside_at = insider(RY, gx * TX - HX, gy * TY - HY)
    below, above = sides(gy, by_y, by_y2)
    fill_top(bx, 0, wide, below, above)
    fill_top(kx, 1, wide, below, above)

    def clear(i, _):
        at = pl.ds(i * CHUNK, CHUNK)
        kx[at] = jnp.where(inside_at(i * CHUNK), kx[at], 0.0)
        return 0

    lax.fori_loop(0, PX // CHUNK, clear, 0, unroll=True)
    for move in keeping[:2]:
        move.start()
    start, steps = SMOOTH

    def begin(p, rdv):
        at = pl.ds(p, CHUNK)
        v = (bx[at] * rdv) * start
        d[at] = v
        x[at] = v

    build_top(kx, wx, wy, wz, s, rd, 0, PX, inside_at, begin)
    for keep, gain in steps:
        sweep_top(x, wx, wy, wz, s, 2, PX - 2, advance_top(keep, gain, bx, 0, rd, d, x))

    def residual(p, at, v, av):
        d[at] = bx[at] - av

    keeping[2].start()
    sweep_top(x, wx, wy, wz, s, 4, PX - 4, residual)

    def coarse(src):
        for c in range(16):
            rs[c] = src[2 + 2 * c] + src[3 + 2 * c]
        return pair_planes(rs, 8, 4, 24)

    for p in (2, 3, PX - 4, PX - 3):
        d[p] = jnp.zeros((RY, 128), F32)
    b1 = coarse(d)
    k1 = coarse(kx)
    level = build(k1, 0.25, 64, within(k1.shape, gx * 8 - 4, gy * 16 - 4, 64, 128, 256))
    x1 = smooth(None, b1, level, 64)
    b1s[...] = b1
    x1s[...] = x1
    k1s[...] = k1
    for number, src in enumerate((b1s, x1s, k1s)):
        one[number] = src[2:6, 4:20, :]
    b1s[...] = remain(x1, b1, level, 64)
    send_all(two, coarse_tile((b1s, k1s), 2, 4))
    for move in keeping:
        move.wait()


def moves(sources, targets, sems):
    return [pltpu.make_async_copy(a, b, sems.at[i]) for i, (a, b) in enumerate(zip(sources, targets))]


def pair_planes(rs, planes, start, rows):
    flat = [
        jnp.concatenate([pair_rows(rs, 2 * c, start, rows), pair_rows(rs, 2 * c + 1, start, rows)], axis=1)
        for c in range(planes)
    ]
    out = 0.125 * pair_dot(jnp.concatenate(flat, axis=0), restrict_map(128, (1, 3)))
    return out.reshape(planes, rows, 128)


def coarse_tile(sources, plane, row):
    flat = [
        jnp.concatenate([pair_rows(src, plane + q, row, 8) for q in range(4)], axis=1) for src in sources
    ]
    out = 0.125 * pair_dot(jnp.concatenate(flat, axis=0), restrict_map(64))
    return out.reshape(len(sources), 8, 128)


def send_all(out, value):
    for g in range(16):
        out[g] = value


def advance_top(keep, gain, b, shift_b, rd, d, x):
    def advance(p, at, v, av):
        dv = keep * d[at] + gain * ((b[pl.ds(p - shift_b, v.shape[0])] - av) * rd[at])
        d[at] = dv
        x[at] = v + dv

    return advance


def open_top(b, shift_b, rd, d, x):
    def advance(p, at, v, av):
        dv = ((b[pl.ds(p - shift_b, v.shape[0])] - av) * rd[at]) * SMOOTH[0]
        d[at] = dv
        x[at] = v + dv

    return advance


def call(kernel, outs, scratch, *args, far_in=0, far_out=0, copies=0):
    near, far = pl.BlockSpec(memory_space=pltpu.VMEM), pl.BlockSpec(memory_space=pl.ANY)
    specs = [pl.BlockSpec(memory_space=pltpu.SMEM)] + [near] * (len(args) - 1 - far_in) + [far] * far_in
    return pl.pallas_call(
        kernel,
        out_shape=[jax.ShapeDtypeStruct(o, F32) for o in outs],
        in_specs=specs,
        out_specs=[near] * (len(outs) - far_out) + [far] * far_out,
        scratch_shapes=[pltpu.VMEM(o, F32) for o in scratch]
        + ([pltpu.SemaphoreType.DMA((copies,))] if copies else []),
        compiler_params=pltpu.CompilerParams(vmem_limit_bytes=VMEM_BYTES),
        cost_estimate=pl.CostEstimate(flops=10**7, bytes_accessed=8 << 20, transcendentals=0),
    )(*args)


def go_down(*args):
    top = (PX, RY, 128)
    outs = [(3, 4, 16, 128), (16, 2, 8, 128)] + [top] * 3
    scratch = [top] * 9 + [(16, RY, 128)] + [(8, 24, 128)] * 3
    return call(down_kernel, outs, scratch, *args, far_out=3, copies=3)


def one_kernel(pos, mid, by_x, by_x2, by_y, by_y2, k1, bout, xout, two, res):
    gx, gy = pos[0], pos[1]
    left, right = sides(gx, by_x, by_x2)
    below, above = sides(gy, by_y, by_y2)
    head = (slice(None), slice(0, 16))
    fill_one(bout, left[head], mid[...], right[head], below[...], above[...])
    b = bout[...]
    inside = within(b.shape, gx * 8 - 8, gy * 16 - 8, 64, 128, 256)
    level = build(k1[...], 0.25, 64, inside)
    x = smooth(None, b, level, 64)
    xout[...] = x
    res[...] = remain(x, b, level, 64)
    send_all(two, coarse_tile((res,), 4, 8))


def fill_one(dst, left, tile, right, below, above):
    dst[0:4, 8:24, :] = left
    dst[4:8, 8:24, :] = tile
    dst[8:12, 8:24, :] = right
    dst[:, 0:8, :] = below
    dst[:, 24:32, :] = above


def go_one(*args):
    wide = (12, 32, 128)
    return call(one_kernel, [wide, wide, (16, 1, 8, 128)], [wide], *args)


def mid_kernel(first, pos, mid, by_y, by_y2, *refs):
    if first:
        near, three, k2 = refs[:3]
        scratch = refs[3:]
    else:
        k2, near, three = refs[:3]
        scratch = refs[3:]
    hold, rs, cs, edge = scratch
    gx, gy = pos[0], pos[1]
    below, above = sides(gy, by_y, by_y2)
    shape = (16, 24, 128)
    inside = within(shape, 0, gy * 8 - 8, 32, 64, 128)

    def rows(dst, number):
        part = slice(16 * number, 16 * number + 16)
        dst[:, 0:8, :] = below[part]
        dst[:, 8:16, :] = mid[:, number]
        dst[:, 16:24, :] = above[part]

    rows(rs, 0)
    b = rs[...]
    if first:
        rows(k2, 1)
        k2[...] = jnp.where(inside, k2[...], 0.0)
    k = k2[...]
    plane = lax.broadcasted_iota(jnp.int32, shape, 0)
    lane = lanes(shape)
    edge_x = ((plane == 0) & (lane < 32), (plane == 15) & (lane >= 96))
    level = build(k, 0.25**2, 32, inside, edge_x)
    x = smooth(None, b, level, 32)
    rs[...] = remain(x, b, level, 32)
    for number, value in enumerate((b, x, k)):
        hold[number] = value
    for i in range(5):
        at = gx - 2 + i
        ok = (at >= 0) & (at < 16)
        from_plane = jnp.clip(at, 0, 15)
        for number in range(3):
            near[number, i] = jnp.where(ok, hold[number, from_plane], 0.0)

    if first:
        for i in range(5):
            edge[0, i : i + 1, :] = near[1, i, 9:10, :]
            edge[1, i : i + 1, :] = near[1, i, 14:15, :]
        upper = lax.rem(gy + 1, 16)
        for g in range(16):
            three[g, 4] = jnp.where(upper == g, edge[0], edge[1])

    def coarse(src, out):
        flat = [
            jnp.concatenate([pair_rows(src, 4 * c + q, 4, 8) for q in range(4)], axis=1) for c in range(4)
        ]
        cs[...] = (0.125 * pair_dot(jnp.concatenate(flat, axis=0), restrict_map(32))).reshape(4, 8, 128)
        for c in range(4):
            part = cs[c, 2:6, :]
            for g in range(16):
                three[g, out + c // 2, 4 * (c % 2) : 4 * (c % 2) + 4, :] = part

    coarse(rs, 0)
    if first:
        coarse(k2, 2)


def go_mid(first, pos, mid, below, above, k2):
    outs = [(3, 5, 24, 128), (16, 5 if first else 2, 8, 128)]
    outs += [(16, 24, 128)] if first else []
    scratch = [(3, 16, 24, 128), (16, 24, 128), (4, 8, 128), (2, 8, 128)]
    args = (mid, below, above) + (() if first else (k2,))
    return call(functools.partial(mid_kernel, first), outs, scratch, pos, *args)


def solve_last(b, k, owned):
    shape = k.shape
    scale = 0.25**4
    lane = lanes(shape)
    row = lax.broadcasted_iota(jnp.int32, shape, 0)
    moves = (
        (8, 1, lane < 8, True),
        (-8, 1, lane >= 120, True),
        (1, 0, row == 0, True),
        (-1, 0, row == 31, True),
        (1, 1, (lane & 7) == 0, False),
        (-1, 1, (lane & 7) == 7, False),
    )
    diagonal = jnp.full(shape, SIGMA * scale, F32)
    pulls = []
    for shift, axis, edge, masked in moves:
        weight = (0.5 * scale) * (k + jnp.where(edge, 0.0, turn(k, shift, axis)))
        diagonal = diagonal + weight
        keep = jnp.where(edge, 0.0, weight)
        if masked:
            keep = jnp.where(owned == turn(owned, shift, axis), keep, 0.0)
        pulls.append(keep)
    rd = 1.0 / diagonal
    pulls = [keep * rd for keep in pulls]
    g = b * rd
    first, steps = COARSE
    d = g * first
    x = d
    for keep, gain in steps:
        total = [pull * turn(x, move[0], move[1]) for pull, move in zip(pulls, moves)]
        near = (total[0] + total[1]) + (total[2] + total[3]) + (total[4] + total[5])
        d = keep * d + gain * ((g - x) + near)
        x = x + d
    return x


def fill_three(dst, gathered, first):
    for g in range(16):
        for c in range(4):
            part = gathered[g, first + c // 2, 4 * (c % 2) : 4 * (c % 2) + 4, :]
            dst[c, 4 * g : 4 * g + 4, :] = part


def solve_three(b_ref, k_ref, owned, s3):
    shape = (4, 64, 128)
    plane = lax.broadcasted_iota(jnp.int32, shape, 0)
    row = lax.broadcasted_iota(jnp.int32, shape, 1)
    lane = lanes(shape)
    edge_x = ((plane == 0) & (lane < 16), (plane == 3) & (lane >= 112))
    level = build(k_ref[...], 0.25**3, 16, None, edge_x, (row == 0, row == 63))
    b = b_ref[...]
    x = smooth(None, b, level, 16)
    s3[:, 8:72, :] = remain(x, b, level, 16)
    flat = [
        jnp.concatenate([pair_rows(src, q, row0, 32) for q in range(4)], axis=1) for src, row0 in ((s3, 8), (k_ref, 0))
    ]
    fine = 0.125 * pair_dot(jnp.concatenate(flat, axis=0), restrict_map(16))
    last = solve_last(fine[:32], fine[32:], owned[...])
    back = pair_dot(last, prolong_map(16))
    for q in range(4):
        spread_rows(s3, q, 8, back[:, 128 * q : 128 * q + 128])
    s3[:, 8:72, :] = smooth(x + s3[:, 8:72, :], b, level, 16)


def rise_two(gx, gy, near, x2, s3, e2, s2):
    pair = lax.shift_right_logical(gy + 1, 1)
    rows = pl.ds(pl.multiple_of(pair * 8, 8), 24)
    for i in range(5):
        at = jnp.clip(gx - 2 + i, 0, 15)
        spread_rows(e2, i, 0, pair_dot(s3[at // 4, rows, :], prolong_one(32, at % 4)))
    e = e2[:, pl.ds(pl.multiple_of((gy + 1 - 2 * pair) * 8, 8), 24), :]
    shape = (5, 24, 128)
    inside = within(shape, gx * 4 - 8, gy * 8 - 8, 32, 64, 128)
    level = build(near[2], 0.25**2, 32, inside)
    s2[...] = smooth(jnp.where(inside, x2 + e, 0.0), near[0], level, 32)


def rise_one(x1, b1, k1, inside, s2, s1):
    flat = jnp.concatenate([s2[i, 4:20, :] for i in range(1, 4)], axis=0)
    back = pair_dot(flat, prolong_map(64))
    for i in range(3):
        for q in range(4):
            spread_rows(s1, 4 * i + q, 0, back[16 * i : 16 * i + 16, 128 * q : 128 * q + 128])
    level = build(k1, 0.25, 64, inside)
    s1[...] = smooth(jnp.where(inside, x1 + s1[...], 0.0), b1, level, 64)


def spread_one(s1, low, high, e0):
    flat = jnp.concatenate([s1[i, 4:28, :] for i in range(low, high)], axis=0)
    back = pair_dot(flat, prolong_map(128, (1, 3)))
    for i in range(high - low):
        for q in range(2):
            part = back[24 * i : 24 * i + 24, 128 * q : 128 * q + 128]
            spread_rows(e0, 2 * (low - 2 + i) + q, 4, part)
    e0[:, 0:4, :] = jnp.zeros((16, 4, 128), F32)
    e0[:, RY - 4 : RY, :] = jnp.zeros((16, 4, 128), F32)


def add_top(x0, e0, x):
    def begin(p, rdv):
        c = (p - 2) // 2
        pair = (e0[pl.ds(c, 1)], e0[pl.ds(c + 1, 1)])
        correction = jnp.concatenate([pair[0], pair[0], pair[1], pair[1]], axis=0)
        at = pl.ds(p, CHUNK)
        x[at] = jnp.where(rdv > 0.0, x0[at] + correction, 0.0)

    return begin


def turn_kernel(
    pos, owned, three, *refs
):
    gx, gy = pos[0], pos[1]
    fars, (b1n, send, send2, *far_outs) = refs[:9], refs[9:17]
    b3, s3, e2, s2, x2s, b1s, s1, e0, d, x, rs, xout, rout, k3, k1, x0n = refs[17:33]
    tops, (wx, wy, wz, s, rd), sems = refs[33:42], refs[42:47], refs[47]
    near, one, by_x, by_x2, by_y, by_y2, b0, k0, x0 = tops
    left, right = sides(gx, by_x, by_x2)
    below, above = sides(gy, by_y, by_y2)
    part = pl.ds(32, 36)
    loads = moves(fars[:4] + (fars[4].at[part], fars[5].at[part]) + fars[6:], tops, sems)
    for move in loads:
        move.start()
    keeps = xkeep, rkeep, kkeep, k1keep, x0keep = [
        pltpu.make_async_copy(a, b, sems.at[9 + i])
        for i, (a, b) in enumerate(zip((xout, rout, k3, k1, x0n), far_outs))
    ]
    fill_three(b3, three, 0)
    fill_three(k3, three, 2)
    kkeep.start()
    solve_three(b3, k3, owned, s3)
    loads[0].wait()
    x2s[...] = near[1]
    lower, upper = lax.rem(gy + 15, 16), lax.rem(gy + 1, 16)
    for i in range(5):
        x2s[i, 1:2, :] = three[lower, 4, i : i + 1, :]
        x2s[i, 22:23, :] = three[upper, 4, i : i + 1, :]
    rise_two(gx, gy, near, x2s[...], s3, e2, s2)

    for move in loads[1:6]:
        move.wait()
    inside = within((12, 32, 128), gx * 8 - 8, gy * 16 - 8, 64, 128, 256)
    for number, dst in enumerate((b1s, s1, k1)):
        part = slice(12 * number, 12 * number + 12)
        fill_one(dst, left[number], one[number], right[number], below[part], above[part])
    k1[...] = jnp.where(inside, k1[...], 0.0)
    k1keep.start()
    rise_one(s1[...], b1s[...], k1[...], inside, s2, s1)

    spread_one(s1, 2, 10, e0)
    for move in loads[6:]:
        move.wait()
    inside_at = insider(RY, gx * TX - HX, gy * TY - HY)
    build_top(k0, wx, wy, wz, s, rd, 2, PX - 2, inside_at, add_top(x0, e0, x))
    start, steps = SMOOTH
    sweep_top(x, wx, wy, wz, s, 4, PX - 4, open_top(b0, 0, rd, d, x))
    for (keep, gain), edge in zip(steps, (4, 6)):
        sweep_top(x, wx, wy, wz, s, edge, PX - edge, advance_top(keep, gain, b0, 0, rd, d, x))

    def residual(p, at, v, av):
        rout[pl.ds(p - 6, v.shape[0])] = b0[at] - av

    sweep_top(x, wx, wy, wz, s, 6, PX - 6, residual)
    xout[...] = x[9 : PX - 9]
    xkeep.start()
    rkeep.start()

    def begin(i, _):
        at = pl.ds(6 + i * CHUNK, CHUNK)
        v = (rout[pl.ds(i * CHUNK, CHUNK)] * rd[at]) * start
        d[at] = v
        x[at] = v
        return 0

    lax.fori_loop(0, (PX - 12) // CHUNK, begin, 0, unroll=True)
    for keep, gain in steps:
        sweep_top(x, wx, wy, wz, s, 8, PX - 8, advance_top(keep, gain, rout, 6, rd, d, x))

    def again(p, at, v, av):
        d[at] = rout[pl.ds(p - 6, v.shape[0])] - av

    x0n[...] = x[HX : HX + TX, HY : HY + TY, :]
    x0keep.start()
    sweep_top(x, wx, wy, wz, s, HX, HX + TX, again)
    for c in range(8):
        rs[c] = d[HX + 2 * c] + d[HX + 1 + 2 * c]
    b1 = pair_planes(rs, 4, HY, 16)
    b1n[...] = b1
    odd = (gx & 1) == 1
    for side, of_odd, of_even in ((send, HX, HX + TX - 4), (send2, HX + TX - 4, HX)):
        side[:, 0:16, :] = b1
        side[:, 16:48, :] = x[pl.ds(jnp.where(odd, of_odd, of_even), 4), HY : HY + TY, :]
    for move in keeps:
        move.wait()


def go_turn(*args):
    top, wide, three, one = (PX, RY, 128), (12, 32, 128), (4, 64, 128), (3, 4, 16, 128)
    kept = [(TX + 2, RY, 128), (TX + 8, RY, 128), three, wide, (TX, TY, 128)]
    outs = [(4, 16, 128), (4, 48, 128), (4, 48, 128)] + kept
    scratch = [three, (4, 88, 128), (5, 48, 128), (5, 24, 128), (5, 24, 128), wide, wide, (16, RY, 128)]
    scratch += [top] * 2 + [(8, RY, 128)] + kept + [(3, 5, 24, 128)] + [one] * 3 + [(36, 8, 128)] * 2 + [top] * 8
    return call(turn_kernel, outs, scratch, *args, far_in=9, far_out=5, copies=14)


def last_kernel(
    pos, owned, three, k3, *refs
):
    gx, gy = pos[0], pos[1]
    fars, far_outs, (b3, s3, e2, s2, s1, e0, d, x) = refs[:13], refs[13:15], refs[15:23]
    tops, (wx, wy, wz, s, rd, xout, rout), sems = refs[23:36], refs[36:43], refs[43]
    near, b1, x1, k1, by_x, by_x2, by_y, by_y2, x0n, k0, r, xbefore, borig = tops
    left, right = sides(gx, by_x, by_x2)
    below, above = sides(gy, by_y, by_y2)
    part = pl.ds(16, 24)
    loads = moves(fars[:6] + (fars[6].at[part], fars[7].at[part]) + fars[8:], tops, sems)
    for move in loads:
        move.start()
    keeps = [
        pltpu.make_async_copy(a, b, sems.at[13 + i]) for i, (a, b) in enumerate(zip((xout, rout), far_outs))
    ]
    fill_three(b3, three, 0)
    solve_three(b3, k3, owned, s3)
    loads[0].wait()
    rise_two(gx, gy, near, near[1], s3, e2, s2)
    for move in loads[1:4]:
        move.wait()
    inside = within((12, 32, 128), gx * 8 - 8, gy * 16 - 8, 64, 128, 256)
    rise_one(x1[...], b1[...], k1[...], inside, s2, s1)

    spread_one(s1, 3, 9, e0)
    for move in loads[4:]:
        move.wait()
    low, high = HX - 4, HX + TX + 4
    x[low:HX, HY : HY + TY, :] = left[:, 16:48, :]
    x[HX : HX + TX, HY : HY + TY, :] = x0n[...]
    x[HX + TX : high, HY : HY + TY, :] = right[:, 16:48, :]
    x[low:high, HY - 8 : HY, :] = below[...]
    x[low:high, HY + TY : HY + TY + 8, :] = above[...]
    x[low:high, 0 : HY - 8, :] = jnp.zeros((high - low, HY - 8, 128), F32)
    x[low:high, RY - 4 : RY, :] = jnp.zeros((high - low, 4, 128), F32)
    inside_at = insider(RY, gx * TX - HX, gy * TY - HY)
    build_top(k0, wx, wy, wz, s, rd, low, high, inside_at, add_top(x, e0, x))
    sweep_top(x, wx, wy, wz, s, low, high, open_top(r, low, rd, d, x))
    for keep, gain in SMOOTH[1]:
        sweep_top(x, wx, wy, wz, s, 8, PX - 8, advance_top(keep, gain, r, low, rd, d, x))
    x[9 : PX - 9] = x[9 : PX - 9] + xbefore[...]

    def residual(p, at, v, av):
        d[at] = av

    xout[...] = x[HX : HX + TX, HY : HY + TY, :]
    keeps[0].start()
    sweep_top(x, wx, wy, wz, s, HX, HX + TX, residual)
    rout[...] = borig[...] - d[HX : HX + TX, HY : HY + TY, :]
    keeps[1].start()
    for move in keeps:
        move.wait()


def go_last(*args):
    top, wide, tile = (PX, RY, 128), (12, 32, 128), (TX, TY, 128)
    scratch = [(4, 64, 128), (4, 88, 128), (5, 48, 128), (5, 24, 128), wide, (16, RY, 128)] + [top] * 2
    scratch += [(3, 5, 24, 128)] + [wide] * 3 + [(4, 48, 128)] * 2 + [(24, 8, 128)] * 2
    scratch += [tile, top, (TX + 8, RY, 128), (TX + 2, RY, 128), tile] + [top] * 5 + [tile] * 2
    return call(last_kernel, [tile, tile], scratch, *args, far_in=13, far_out=2, copies=15)


def swap(low, high, axis):
    count = lax.axis_size(axis)
    odd = lax.axis_index(axis) % 2 == 1
    first = jnp.where(odd, low, high) if low is not high else low
    second = jnp.where(odd, high, low) if low is not high else low
    return (
        lax.ppermute(first, axis, [(i, i ^ 1) for i in range(count)]),
        lax.ppermute(second, axis, [(i, (i + 1 if i % 2 else i - 1) % count) for i in range(count)]),
    )


def apart(first, second, axis):
    odd = lax.axis_index(axis) % 2 == 1
    return jnp.where(odd, first, second), jnp.where(odd, second, first)


def gather(copies, axis):
    return lax.all_to_all(copies, axis, 0, 0, tiled=True)


def local(right_side, kappa, owners):
    pos = jnp.stack([lax.axis_index("gx"), lax.axis_index("gy")]).astype(jnp.int32)
    owned = jnp.repeat(jnp.repeat(owners.T, 2, 0), 8, 1).astype(F32)
    mid = jnp.stack([right_side, kappa])
    left, right = apart(*swap(mid[:, :HX], mid[:, TX - HX :], "gx"), "gx")
    wide = jnp.concatenate([left, mid, right], axis=1)
    low, high = (part.reshape(-1, 128) for part in (wide[:, :, :HX], wide[:, :, TY - HX :]))
    one, two, b0, k0, x0 = go_down(pos, wide, *swap(low, high, "gy"))
    by_x = swap(one, one, "gx")
    two = gather(two, "gx")
    left, right = apart(*by_x, "gx")
    rows = jnp.swapaxes(two, 0, 1).reshape(-1, 8, 128)
    wide = jnp.concatenate([left, one, right], axis=1)
    low, high = (
        jnp.concatenate([rows, part.reshape(-1, 8, 128)]) for part in (wide[:, :, :8], wide[:, :, 8:])
    )
    by_y = swap(low, high, "gy")
    near, three, k2 = go_mid(True, pos, two, *by_y, None)
    three = gather(three, "gy")
    b1n, send, send2, xbefore, source, k3, k1, x0n = go_turn(
        pos, owned, three, near, one, *by_x, *by_y, b0, k0, x0
    )

    by_x = (
        lax.ppermute(send, "gx", [(i, i ^ 1) for i in range(16)]),
        lax.ppermute(send2, "gx", [(i, (i + 1 if i % 2 else i - 1) % 16) for i in range(16)]),
    )
    left, right = apart(*by_x, "gx")
    wide = jnp.concatenate([left[:, :16], b1n, right[:, :16]])
    b1, x1, two = go_one(pos, b1n, *by_x, *swap(wide[:, :8], wide[:, 8:], "gy"), k1)
    two = gather(two, "gx")
    wide = jnp.concatenate([left[:, 16:], x0n, right[:, 16:]])
    low, high = (jnp.concatenate([two[:, 0], part]) for part in (wide[:, :8], wide[:, 24:]))
    by_y = swap(low, high, "gy")
    near, three = go_mid(False, pos, two, *by_y, k2)
    three = gather(three, "gy")
    field, residual = go_last(
        pos, owned, three, k3, near, b1, x1, k1, *by_x, *by_y, x0n, k0, source, xbefore, right_side
    )
    return field, residual


def solution(mesh):
    spec = P("gx", "gy", None)
    return jax.shard_map(
        local, mesh=mesh, in_specs=(spec, spec, P()), out_specs=(spec, spec), check_vma=False
    )
```

```python
import functools

import jax
import jax.numpy as jnp
from jax import lax
from jax.experimental import pallas as pl
from jax.experimental.pallas import tpu as pltpu
from jax.sharding import PartitionSpec as P

SIGMA = 0.02
F32 = jnp.float32
BF16 = jnp.bfloat16
TX, TY = 16, 32
HX = 10
HY = 12
PX, RY = TX + 2 * HX, TY + 2 * HY
CHUNK = 4
PARTS = 2
VMEM_BYTES = 56 * 1024 * 1024


def cheb_steps(degree, lower):
    centre = 0.5 * (2.0 + lower)
    half = 0.5 * (2.0 - lower)
    sharp = centre / half
    ratio = 1.0 / sharp
    steps = []
    for _ in range(degree - 1):
        nxt = 1.0 / (2.0 * sharp - ratio)
        steps.append((nxt * ratio, 2.0 * nxt / half))
        ratio = nxt
    return 1.0 / centre, steps


SMOOTH = cheb_steps(3, 0.3)
COARSE = cheb_steps(24, 0.05)


def lane_match(z, q, source, target):
    bits = z.bit_length() - 1
    cell = (lax.shift_right_logical(source, bits) + (128 // z) * q) & -2
    inner = lax.shift_right_logical(source & (z - 1), 1)
    return jnp.where(cell * (z // 4) + inner == target, 1.0, 0.0).astype(BF16)


def restrict_map(z, planes=(0, 4)):
    shape = ((planes[1] - planes[0]) * 128, 128)
    row = lax.broadcasted_iota(jnp.int32, shape, 0)
    return lane_match(z, planes[0] + lax.shift_right_logical(row, 7), row & 127, lanes(shape))


def prolong_map(z, planes=(0, 4)):
    shape = (128, (planes[1] - planes[0]) * 128)
    column = lanes(shape)
    target = lax.broadcasted_iota(jnp.int32, shape, 0)
    return lane_match(z, planes[0] + lax.shift_right_logical(column, 7), column & 127, target)


def prolong_one(z, q):
    shape = (128, 128)
    return lane_match(z, q, lanes(shape), lax.broadcasted_iota(jnp.int32, shape, 0))


def pair_dot(value, matrix):
    rows = value.shape[0]
    high = value.astype(BF16).astype(F32)
    rest = value - high
    mid = rest.astype(BF16).astype(F32)
    parts = jnp.concatenate([high, mid, rest - mid], axis=0).astype(BF16)
    out = jnp.dot(parts, matrix, preferred_element_type=F32)
    return out[:rows] + (out[rows : 2 * rows] + out[2 * rows :])


def lanes(shape):
    return lax.broadcasted_iota(jnp.int32, shape, len(shape) - 1)


def turn(value, shift, axis):
    return pltpu.roll(value, shift % value.shape[axis], axis)


def next_x(v, z):
    if z == 128:
        return jnp.concatenate([v[1:], v[:1]], axis=0)
    a = turn(v, -z, 2)
    b = jnp.concatenate([a[1:], a[:1]], axis=0)
    return jnp.where(lanes(v.shape) < 128 - z, a, b)


def prev_x(v, z):
    if z == 128:
        return jnp.concatenate([v[-1:], v[:-1]], axis=0)
    a = turn(v, z, 2)
    b = jnp.concatenate([a[-1:], a[:-1]], axis=0)
    return jnp.where(lanes(v.shape) >= z, a, b)


def faces_of(k, step, scale, low, high):
    own = (0.5 * scale) * k
    both = own + (0.5 * scale) * step
    if low is None:
        return both, None
    edge = jnp.where(low | high, own, 0.0)
    return jnp.where(high, 0.0, both), edge


def build(k, scale, z, inside=None, edge_x=(None, None), edge_y=(None, None)):
    shape = k.shape
    cell = lanes(shape) & (z - 1)
    wx, ex = faces_of(k, next_x(k, z), scale, *edge_x)
    wy, ey = faces_of(k, turn(k, -1, 1), scale, *edge_y)
    wz, ez = faces_of(k, turn(k, -1, 2), scale, cell == 0, cell == z - 1)
    s = ez + SIGMA * scale
    if ex is not None:
        s = s + ex
    if ey is not None:
        s = s + ey
    diagonal = s + wx + prev_x(wx, z) + wy + turn(wy, 1, 1) + wz + turn(wz, 1, 2)
    rd = 1.0 / diagonal
    if inside is not None:
        rd = jnp.where(inside, rd, 0.0)
    return wx, wy, wz, s, rd


def remain(v, b, level, z):
    wx, wy, wz, s, _ = level
    fx = wx * (next_x(v, z) - v)
    fy = wy * (turn(v, -1, 1) - v)
    fz = wz * (turn(v, -1, 2) - v)
    total = (fx - prev_x(fx, z)) + (fy - turn(fy, 1, 1)) + (fz - turn(fz, 1, 2))
    return (b - s * v) + total


def smooth(x, b, level, z):
    first, steps = SMOOTH
    rd = level[4]
    if x is None:
        d = (b * rd) * first
        x = d
    else:
        d = (remain(x, b, level, z) * rd) * first
        x = x + d
    for keep, gain in steps:
        d = keep * d + gain * (remain(x, b, level, z) * rd)
        x = x + d
    return x


def within(shape, first_x, first_y, z, size_x, size_y):
    plane = lax.broadcasted_iota(jnp.int32, shape, 0)
    cx = first_x + plane * (128 // z) + lax.shift_right_logical(lanes(shape), z.bit_length() - 1)
    cy = first_y + lax.broadcasted_iota(jnp.int32, shape, 1)
    return (cx >= 0) & (cx < size_x) & (cy >= 0) & (cy < size_y)


def pair_rows(ref, plane, start, count):
    return ref[plane, pl.ds(start, count, stride=2), :] + ref[plane, pl.ds(start + 1, count, stride=2), :]


def spread_rows(ref, plane, start, value):
    count = value.shape[0]
    ref[plane, pl.ds(start, count, stride=2), :] = value
    ref[plane, pl.ds(start + 1, count, stride=2), :] = value


def insider(rows, first_x, first_y):
    row = lax.broadcasted_iota(jnp.int32, (CHUNK, rows, 128), 1) + first_y
    row_in = (row >= 0) & (row < 512)
    plane = lax.broadcasted_iota(jnp.int32, (CHUNK, rows, 128), 0) + first_x
    return lambda p: row_in & (plane >= -p) & (plane < 256 - p)


def build_top(k_ref, wx, wy, wz, s, rd, low, high, inside_at, body):
    rows = k_ref.shape[1]
    shape = (CHUNK, rows, 128)
    lane = lanes(shape)

    def step(i, wxp):
        p = low + i * CHUNK
        k = k_ref[pl.ds(p, CHUNK)]
        kn = jnp.concatenate([k[1:], k_ref[pl.ds(jnp.minimum(p + CHUNK, k_ref.shape[0] - 1), 1)]], axis=0)
        own = 0.5 * k
        fx = 0.5 * kn + own
        fy = turn(own, -1, 1) + own
        fz = jnp.where(lane == 127, 0.0, turn(own, -1, 2) + own)
        sv = SIGMA + jnp.where((lane == 0) | (lane == 127), own, 0.0)
        fxp = jnp.concatenate([wxp, fx[:-1]], axis=0)
        diagonal = sv + (fx + fxp) + (fy + turn(fy, 1, 1)) + (fz + turn(fz, 1, 2))
        rdv = jnp.where(inside_at(p), 1.0 / diagonal, 0.0)
        at = pl.ds(p, CHUNK)
        wx[at], wy[at], wz[at], s[at], rd[at] = fx, fy, fz, sv, rdv
        body(p, rdv)
        return fx[-1:]

    assert (high - low) % CHUNK == 0
    lax.fori_loop(0, (high - low) // CHUNK, step, jnp.zeros((1, rows, 128), F32), unroll=True)


def sweep_top(x, wx, wy, wz, s, low, high, body):
    size = (high - low) // PARTS
    fx0 = wx[low - 1 : low] * (x[low : low + 1] - x[low - 1 : low])

    def step(i, fxp):
        p = low + i * size
        at = pl.ds(p, size)
        v = x[at]
        vn = jnp.concatenate([v[1:], x[pl.ds(p + size, 1)]], axis=0)
        fx = wx[at] * (vn - v)
        fy = wy[at] * (turn(v, -1, 1) - v)
        fz = wz[at] * (turn(v, -1, 2) - v)
        fxp = jnp.concatenate([fxp, fx[:-1]], axis=0)
        total = (fx - fxp) + (fy - turn(fy, 1, 1)) + (fz - turn(fz, 1, 2))
        body(p, at, v, s[at] * v - total)
        return fx[-1:]

    assert (high - low) % PARTS == 0
    lax.fori_loop(0, PARTS, step, fx0, unroll=True)


class Pick:
    def __init__(self, take_first, first, second):
        self.take_first, self.first, self.second = take_first, first, second

    def __getitem__(self, index):
        return jnp.where(self.take_first, self.first[index], self.second[index])


def sides(at, first, second):
    odd = (at & 1) == 1
    return Pick(odd, first, second), Pick(odd, second, first)


def fill_top(dst, number, wide, below, above):
    dst[:, 0:2, :] = jnp.zeros((PX, 2, 128), F32)
    dst[:, RY - 2 : RY, :] = jnp.zeros((PX, 2, 128), F32)
    dst[:, HY : HY + TY, :] = wide[number]
    for p in range(PX):
        part = slice(HX * (PX * number + p), HX * (PX * number + p + 1))
        dst[p, 2:HY, :] = below[part]
        dst[p, HY + TY : RY - 2, :] = above[part]


def down_kernel(pos, wide, by_y, by_y2, one, two, *refs):
    given, (bx, kx, x, wx, wy, wz, s, rd, d, rs, b1s, x1s, k1s, sems) = refs[:3], refs[3:]
    keeping = moves((bx, kx, x), given, sems)
    gx, gy = pos[0], pos[1]
    inside_at = insider(RY, gx * TX - HX, gy * TY - HY)
    below, above = sides(gy, by_y, by_y2)
    fill_top(bx, 0, wide, below, above)
    fill_top(kx, 1, wide, below, above)

    def clear(i, _):
        at = pl.ds(i * CHUNK, CHUNK)
        kx[at] = jnp.where(inside_at(i * CHUNK), kx[at], 0.0)
        return 0

    lax.fori_loop(0, PX // CHUNK, clear, 0, unroll=True)
    for move in keeping[:2]:
        move.start()
    start, steps = SMOOTH

    def begin(p, rdv):
        at = pl.ds(p, CHUNK)
        v = (bx[at] * rdv) * start
        d[at] = v
        x[at] = v

    build_top(kx, wx, wy, wz, s, rd, 0, PX, inside_at, begin)
    for keep, gain in steps:
        sweep_top(x, wx, wy, wz, s, 2, PX - 2, advance_top(keep, gain, bx, 0, rd, d, x))

    def residual(p, at, v, av):
        d[at] = bx[at] - av

    keeping[2].start()
    sweep_top(x, wx, wy, wz, s, 4, PX - 4, residual)

    def coarse(src):
        for c in range(16):
            rs[c] = src[2 + 2 * c] + src[3 + 2 * c]
        return pair_planes(rs, 8, 4, 24)

    for p in (2, 3, PX - 4, PX - 3):
        d[p] = jnp.zeros((RY, 128), F32)
    b1 = coarse(d)
    k1 = coarse(kx)
    level = build(k1, 0.25, 64, within(k1.shape, gx * 8 - 4, gy * 16 - 4, 64, 128, 256))
    x1 = smooth(None, b1, level, 64)
    b1s[...] = b1
    x1s[...] = x1
    k1s[...] = k1
    for number, src in enumerate((b1s, x1s, k1s)):
        one[number] = src[2:6, 4:20, :]
    b1s[...] = remain(x1, b1, level, 64)
    send_all(two, coarse_tile((b1s, k1s), 2, 4))
    for move in keeping:
        move.wait()


def moves(sources, targets, sems):
    return [pltpu.make_async_copy(a, b, sems.at[i]) for i, (a, b) in enumerate(zip(sources, targets))]


def pair_planes(rs, planes, start, rows):
    flat = [
        jnp.concatenate([pair_rows(rs, 2 * c, start, rows), pair_rows(rs, 2 * c + 1, start, rows)], axis=1)
        for c in range(planes)
    ]
    out = 0.125 * pair_dot(jnp.concatenate(flat, axis=0), restrict_map(128, (1, 3)))
    return out.reshape(planes, rows, 128)


def coarse_tile(sources, plane, row):
    flat = [
        jnp.concatenate([pair_rows(src, plane + q, row, 8) for q in range(4)], axis=1) for src in sources
    ]
    out = 0.125 * pair_dot(jnp.concatenate(flat, axis=0), restrict_map(64))
    return out.reshape(len(sources), 8, 128)


def send_all(out, value):
    for g in range(16):
        out[g] = value


def advance_top(keep, gain, b, shift_b, rd, d, x):
    def advance(p, at, v, av):
        dv = keep * d[at] + gain * ((b[pl.ds(p - shift_b, v.shape[0])] - av) * rd[at])
        d[at] = dv
        x[at] = v + dv

    return advance


def open_top(b, shift_b, rd, d, x):
    def advance(p, at, v, av):
        dv = ((b[pl.ds(p - shift_b, v.shape[0])] - av) * rd[at]) * SMOOTH[0]
        d[at] = dv
        x[at] = v + dv

    return advance


def call(kernel, outs, scratch, *args, far_in=0, far_out=0, copies=0, grant=VMEM_BYTES):
    near, far = pl.BlockSpec(memory_space=pltpu.VMEM), pl.BlockSpec(memory_space=pl.ANY)
    specs = [pl.BlockSpec(memory_space=pltpu.SMEM)] + [near] * (len(args) - 1 - far_in) + [far] * far_in
    return pl.pallas_call(
        kernel,
        out_shape=[jax.ShapeDtypeStruct(o, F32) for o in outs],
        in_specs=specs,
        out_specs=[near] * (len(outs) - far_out) + [far] * far_out,
        scratch_shapes=[pltpu.VMEM(o, F32) for o in scratch]
        + ([pltpu.SemaphoreType.DMA((copies,))] if copies else []),
        compiler_params=pltpu.CompilerParams(vmem_limit_bytes=grant),
        cost_estimate=pl.CostEstimate(flops=10**7, bytes_accessed=8 << 20, transcendentals=0),
    )(*args)


def go_down(*args):
    top = (PX, RY, 128)
    outs = [(3, 4, 16, 128), (16, 2, 8, 128)] + [top] * 3
    scratch = [top] * 9 + [(16, RY, 128)] + [(8, 24, 128)] * 3
    return call(down_kernel, outs, scratch, *args, far_out=3, copies=3)


def one_kernel(pos, mid, by_x, by_x2, by_y, by_y2, k1, bout, xout, two, res):
    gx, gy = pos[0], pos[1]
    left, right = sides(gx, by_x, by_x2)
    below, above = sides(gy, by_y, by_y2)
    head = (slice(None), slice(0, 16))
    fill_one(bout, left[head], mid[...], right[head], below[...], above[...])
    b = bout[...]
    inside = within(b.shape, gx * 8 - 8, gy * 16 - 8, 64, 128, 256)
    level = build(k1[...], 0.25, 64, inside)
    x = smooth(None, b, level, 64)
    xout[...] = x
    res[...] = remain(x, b, level, 64)
    send_all(two, coarse_tile((res,), 4, 8))


def fill_one(dst, left, tile, right, below, above):
    dst[0:4, 8:24, :] = left
    dst[4:8, 8:24, :] = tile
    dst[8:12, 8:24, :] = right
    dst[:, 0:8, :] = below
    dst[:, 24:32, :] = above


def go_one(*args):
    wide = (12, 32, 128)
    return call(one_kernel, [wide, wide, (16, 1, 8, 128)], [wide], *args)


def mid_kernel(first, pos, mid, by_y, by_y2, *refs):
    if first:
        near, three, k2 = refs[:3]
        scratch = refs[3:]
    else:
        k2, near, three = refs[:3]
        scratch = refs[3:]
    hold, rs, cs, edge = scratch
    gx, gy = pos[0], pos[1]
    below, above = sides(gy, by_y, by_y2)
    shape = (16, 24, 128)
    inside = within(shape, 0, gy * 8 - 8, 32, 64, 128)

    def rows(dst, number):
        part = slice(16 * number, 16 * number + 16)
        dst[:, 0:8, :] = below[part]
        dst[:, 8:16, :] = mid[:, number]
        dst[:, 16:24, :] = above[part]

    rows(rs, 0)
    b = rs[...]
    if first:
        rows(k2, 1)
        k2[...] = jnp.where(inside, k2[...], 0.0)
    k = k2[...]
    plane = lax.broadcasted_iota(jnp.int32, shape, 0)
    lane = lanes(shape)
    edge_x = ((plane == 0) & (lane < 32), (plane == 15) & (lane >= 96))
    level = build(k, 0.25**2, 32, inside, edge_x)
    x = smooth(None, b, level, 32)
    rs[...] = remain(x, b, level, 32)
    for number, value in enumerate((b, x, k)):
        hold[number] = value
    for i in range(5):
        at = gx - 2 + i
        ok = (at >= 0) & (at < 16)
        from_plane = jnp.clip(at, 0, 15)
        for number in range(3):
            near[number, i] = jnp.where(ok, hold[number, from_plane], 0.0)

    if first:
        for i in range(5):
            edge[0, i : i + 1, :] = near[1, i, 9:10, :]
            edge[1, i : i + 1, :] = near[1, i, 14:15, :]
        upper = lax.rem(gy + 1, 16)
        for g in range(16):
            three[g, 4] = jnp.where(upper == g, edge[0], edge[1])

    def coarse(src, out):
        flat = [
            jnp.concatenate([pair_rows(src, 4 * c + q, 4, 8) for q in range(4)], axis=1) for c in range(4)
        ]
        cs[...] = (0.125 * pair_dot(jnp.concatenate(flat, axis=0), restrict_map(32))).reshape(4, 8, 128)
        for c in range(4):
            part = cs[c, 2:6, :]
            for g in range(16):
                three[g, out + c // 2, 4 * (c % 2) : 4 * (c % 2) + 4, :] = part

    coarse(rs, 0)
    if first:
        coarse(k2, 2)


def go_mid(first, pos, mid, below, above, k2):
    outs = [(3, 5, 24, 128), (16, 5 if first else 2, 8, 128)]
    outs += [(16, 24, 128)] if first else []
    scratch = [(3, 16, 24, 128), (16, 24, 128), (4, 8, 128), (2, 8, 128)]
    args = (mid, below, above) + (() if first else (k2,))
    grant = VMEM_BYTES if first else VMEM_BYTES // 4
    return call(functools.partial(mid_kernel, first), outs, scratch, pos, *args, grant=grant)


def solve_last(b, k, owned):
    shape = k.shape
    scale = 0.25**4
    lane = lanes(shape)
    row = lax.broadcasted_iota(jnp.int32, shape, 0)
    moves = (
        (8, 1, lane < 8, True),
        (-8, 1, lane >= 120, True),
        (1, 0, row == 0, True),
        (-1, 0, row == 31, True),
        (1, 1, (lane & 7) == 0, False),
        (-1, 1, (lane & 7) == 7, False),
    )
    diagonal = jnp.full(shape, SIGMA * scale, F32)
    pulls = []
    for shift, axis, edge, masked in moves:
        weight = (0.5 * scale) * (k + jnp.where(edge, 0.0, turn(k, shift, axis)))
        diagonal = diagonal + weight
        keep = jnp.where(edge, 0.0, weight)
        if masked:
            keep = jnp.where(owned == turn(owned, shift, axis), keep, 0.0)
        pulls.append(keep)
    rd = 1.0 / diagonal
    pulls = [keep * rd for keep in pulls]
    g = b * rd
    first, steps = COARSE
    d = g * first
    x = d
    for keep, gain in steps:
        total = [pull * turn(x, move[0], move[1]) for pull, move in zip(pulls, moves)]
        near = (total[0] + total[1]) + (total[2] + total[3]) + (total[4] + total[5])
        d = keep * d + gain * ((g - x) + near)
        x = x + d
    return x


def fill_three(dst, gathered, first):
    for g in range(16):
        for c in range(4):
            part = gathered[g, first + c // 2, 4 * (c % 2) : 4 * (c % 2) + 4, :]
            dst[c, 4 * g : 4 * g + 4, :] = part


def solve_three(b_ref, k_ref, owned, s3):
    shape = (4, 64, 128)
    plane = lax.broadcasted_iota(jnp.int32, shape, 0)
    row = lax.broadcasted_iota(jnp.int32, shape, 1)
    lane = lanes(shape)
    edge_x = ((plane == 0) & (lane < 16), (plane == 3) & (lane >= 112))
    level = build(k_ref[...], 0.25**3, 16, None, edge_x, (row == 0, row == 63))
    b = b_ref[...]
    x = smooth(None, b, level, 16)
    s3[:, 8:72, :] = remain(x, b, level, 16)
    flat = [
        jnp.concatenate([pair_rows(src, q, row0, 32) for q in range(4)], axis=1) for src, row0 in ((s3, 8), (k_ref, 0))
    ]
    fine = 0.125 * pair_dot(jnp.concatenate(flat, axis=0), restrict_map(16))
    last = solve_last(fine[:32], fine[32:], owned[...])
    back = pair_dot(last, prolong_map(16))
    for q in range(4):
        spread_rows(s3, q, 8, back[:, 128 * q : 128 * q + 128])
    s3[:, 8:72, :] = smooth(x + s3[:, 8:72, :], b, level, 16)


def rise_two(gx, gy, near, x2, s3, e2, s2):
    pair = lax.shift_right_logical(gy + 1, 1)
    rows = pl.ds(pl.multiple_of(pair * 8, 8), 24)
    for i in range(5):
        at = jnp.clip(gx - 2 + i, 0, 15)
        spread_rows(e2, i, 0, pair_dot(s3[at // 4, rows, :], prolong_one(32, at % 4)))
    e = e2[:, pl.ds(pl.multiple_of((gy + 1 - 2 * pair) * 8, 8), 24), :]
    shape = (5, 24, 128)
    inside = within(shape, gx * 4 - 8, gy * 8 - 8, 32, 64, 128)
    level = build(near[2], 0.25**2, 32, inside)
    s2[...] = smooth(jnp.where(inside, x2 + e, 0.0), near[0], level, 32)


def rise_one(x1, b1, k1, inside, s2, s1):
    flat = jnp.concatenate([s2[i, 4:20, :] for i in range(1, 4)], axis=0)
    back = pair_dot(flat, prolong_map(64))
    for i in range(3):
        for q in range(4):
            spread_rows(s1, 4 * i + q, 0, back[16 * i : 16 * i + 16, 128 * q : 128 * q + 128])
    level = build(k1, 0.25, 64, inside)
    s1[...] = smooth(jnp.where(inside, x1 + s1[...], 0.0), b1, level, 64)


def spread_one(s1, low, high, e0):
    flat = jnp.concatenate([s1[i, 4:28, :] for i in range(low, high)], axis=0)
    back = pair_dot(flat, prolong_map(128, (1, 3)))
    for i in range(high - low):
        for q in range(2):
            part = back[24 * i : 24 * i + 24, 128 * q : 128 * q + 128]
            spread_rows(e0, 2 * (low - 2 + i) + q, 4, part)
    e0[:, 0:4, :] = jnp.zeros((16, 4, 128), F32)
    e0[:, RY - 4 : RY, :] = jnp.zeros((16, 4, 128), F32)


def add_top(x0, e0, x):
    def begin(p, rdv):
        c = (p - 2) // 2
        pair = (e0[pl.ds(c, 1)], e0[pl.ds(c + 1, 1)])
        correction = jnp.concatenate([pair[0], pair[0], pair[1], pair[1]], axis=0)
        at = pl.ds(p, CHUNK)
        x[at] = jnp.where(rdv > 0.0, x0[at] + correction, 0.0)

    return begin


def turn_kernel(
    pos, owned, three, *refs
):
    gx, gy = pos[0], pos[1]
    fars, (b1n, send, send2, *far_outs) = refs[:9], refs[9:17]
    b3, s3, e2, s2, x2s, b1s, s1, e0, d, x, rs, xout, rout, k3, k1, x0n = refs[17:33]
    tops, (wx, wy, wz, s, rd), sems = refs[33:42], refs[42:47], refs[47]
    near, one, by_x, by_x2, by_y, by_y2, b0, k0, x0 = tops
    left, right = sides(gx, by_x, by_x2)
    below, above = sides(gy, by_y, by_y2)
    part = pl.ds(32, 36)
    loads = moves(fars[:4] + (fars[4].at[part], fars[5].at[part]) + fars[6:], tops, sems)
    for move in loads:
        move.start()
    keeps = xkeep, rkeep, kkeep, k1keep, x0keep = [
        pltpu.make_async_copy(a, b, sems.at[9 + i])
        for i, (a, b) in enumerate(zip((xout, rout, k3, k1, x0n), far_outs))
    ]
    fill_three(b3, three, 0)
    fill_three(k3, three, 2)
    kkeep.start()
    solve_three(b3, k3, owned, s3)
    loads[0].wait()
    x2s[...] = near[1]
    lower, upper = lax.rem(gy + 15, 16), lax.rem(gy + 1, 16)
    for i in range(5):
        x2s[i, 1:2, :] = three[lower, 4, i : i + 1, :]
        x2s[i, 22:23, :] = three[upper, 4, i : i + 1, :]
    rise_two(gx, gy, near, x2s[...], s3, e2, s2)

    for move in loads[1:6]:
        move.wait()
    inside = within((12, 32, 128), gx * 8 - 8, gy * 16 - 8, 64, 128, 256)
    for number, dst in enumerate((b1s, s1, k1)):
        part = slice(12 * number, 12 * number + 12)
        fill_one(dst, left[number], one[number], right[number], below[part], above[part])
    k1[...] = jnp.where(inside, k1[...], 0.0)
    k1keep.start()
    rise_one(s1[...], b1s[...], k1[...], inside, s2, s1)

    spread_one(s1, 2, 10, e0)
    for move in loads[6:]:
        move.wait()
    inside_at = insider(RY, gx * TX - HX, gy * TY - HY)
    build_top(k0, wx, wy, wz, s, rd, 2, PX - 2, inside_at, add_top(x0, e0, x))
    start, steps = SMOOTH
    sweep_top(x, wx, wy, wz, s, 4, PX - 4, open_top(b0, 0, rd, d, x))
    for (keep, gain), edge in zip(steps, (4, 6)):
        sweep_top(x, wx, wy, wz, s, edge, PX - edge, advance_top(keep, gain, b0, 0, rd, d, x))

    def residual(p, at, v, av):
        rout[pl.ds(p - 6, v.shape[0])] = b0[at] - av

    sweep_top(x, wx, wy, wz, s, 6, PX - 6, residual)
    xout[...] = x[9 : PX - 9]
    xkeep.start()
    rkeep.start()

    def begin(i, _):
        at = pl.ds(6 + i * CHUNK, CHUNK)
        v = (rout[pl.ds(i * CHUNK, CHUNK)] * rd[at]) * start
        d[at] = v
        x[at] = v
        return 0

    lax.fori_loop(0, (PX - 12) // CHUNK, begin, 0, unroll=True)
    for keep, gain in steps:
        sweep_top(x, wx, wy, wz, s, 8, PX - 8, advance_top(keep, gain, rout, 6, rd, d, x))

    def again(p, at, v, av):
        d[at] = rout[pl.ds(p - 6, v.shape[0])] - av

    x0n[...] = x[HX : HX + TX, HY : HY + TY, :]
    x0keep.start()
    sweep_top(x, wx, wy, wz, s, HX, HX + TX, again)
    for c in range(8):
        rs[c] = d[HX + 2 * c] + d[HX + 1 + 2 * c]
    b1 = pair_planes(rs, 4, HY, 16)
    b1n[...] = b1
    odd = (gx & 1) == 1
    for side, of_odd, of_even in ((send, HX, HX + TX - 4), (send2, HX + TX - 4, HX)):
        side[:, 0:16, :] = b1
        side[:, 16:48, :] = x[pl.ds(jnp.where(odd, of_odd, of_even), 4), HY : HY + TY, :]
    for move in keeps:
        move.wait()


def go_turn(*args):
    top, wide, three, one = (PX, RY, 128), (12, 32, 128), (4, 64, 128), (3, 4, 16, 128)
    kept = [(TX + 2, RY, 128), (TX + 8, RY, 128), three, wide, (TX, TY, 128)]
    outs = [(4, 16, 128), (4, 48, 128), (4, 48, 128)] + kept
    scratch = [three, (4, 88, 128), (5, 48, 128), (5, 24, 128), (5, 24, 128), wide, wide, (16, RY, 128)]
    scratch += [top] * 2 + [(8, RY, 128)] + kept + [(3, 5, 24, 128)] + [one] * 3 + [(36, 8, 128)] * 2 + [top] * 8
    return call(turn_kernel, outs, scratch, *args, far_in=9, far_out=5, copies=14)


def last_kernel(
    pos, owned, three, k3, *refs
):
    gx, gy = pos[0], pos[1]
    fars, far_outs, (b3, s3, e2, s2, s1, e0, d, x) = refs[:13], refs[13:15], refs[15:23]
    tops, (wx, wy, wz, s, rd, xout, rout), sems = refs[23:36], refs[36:43], refs[43]
    near, b1, x1, k1, by_x, by_x2, by_y, by_y2, x0n, k0, r, xbefore, borig = tops
    left, right = sides(gx, by_x, by_x2)
    below, above = sides(gy, by_y, by_y2)
    part = pl.ds(16, 24)
    loads = moves(fars[:6] + (fars[6].at[part], fars[7].at[part]) + fars[8:], tops, sems)
    for move in loads:
        move.start()
    keeps = [
        pltpu.make_async_copy(a, b, sems.at[13 + i]) for i, (a, b) in enumerate(zip((xout, rout), far_outs))
    ]
    fill_three(b3, three, 0)
    solve_three(b3, k3, owned, s3)
    loads[0].wait()
    rise_two(gx, gy, near, near[1], s3, e2, s2)
    for move in loads[1:4]:
        move.wait()
    inside = within((12, 32, 128), gx * 8 - 8, gy * 16 - 8, 64, 128, 256)
    rise_one(x1[...], b1[...], k1[...], inside, s2, s1)

    spread_one(s1, 3, 9, e0)
    for move in loads[4:]:
        move.wait()
    low, high = HX - 4, HX + TX + 4
    x[low:HX, HY : HY + TY, :] = left[:, 16:48, :]
    x[HX : HX + TX, HY : HY + TY, :] = x0n[...]
    x[HX + TX : high, HY : HY + TY, :] = right[:, 16:48, :]
    x[low:high, HY - 8 : HY, :] = below[...]
    x[low:high, HY + TY : HY + TY + 8, :] = above[...]
    x[low:high, 0 : HY - 8, :] = jnp.zeros((high - low, HY - 8, 128), F32)
    x[low:high, RY - 4 : RY, :] = jnp.zeros((high - low, 4, 128), F32)
    inside_at = insider(RY, gx * TX - HX, gy * TY - HY)
    build_top(k0, wx, wy, wz, s, rd, low, high, inside_at, add_top(x, e0, x))
    sweep_top(x, wx, wy, wz, s, low, high, open_top(r, low, rd, d, x))
    for keep, gain in SMOOTH[1]:
        sweep_top(x, wx, wy, wz, s, 8, PX - 8, advance_top(keep, gain, r, low, rd, d, x))
    x[9 : PX - 9] = x[9 : PX - 9] + xbefore[...]

    def residual(p, at, v, av):
        d[at] = av

    xout[...] = x[HX : HX + TX, HY : HY + TY, :]
    keeps[0].start()
    sweep_top(x, wx, wy, wz, s, HX, HX + TX, residual)
    rout[...] = borig[...] - d[HX : HX + TX, HY : HY + TY, :]
    keeps[1].start()
    for move in keeps:
        move.wait()


def go_last(*args):
    top, wide, tile = (PX, RY, 128), (12, 32, 128), (TX, TY, 128)
    scratch = [(4, 64, 128), (4, 88, 128), (5, 48, 128), (5, 24, 128), wide, (16, RY, 128)] + [top] * 2
    scratch += [(3, 5, 24, 128)] + [wide] * 3 + [(4, 48, 128)] * 2 + [(24, 8, 128)] * 2
    scratch += [tile, top, (TX + 8, RY, 128), (TX + 2, RY, 128), tile] + [top] * 5 + [tile] * 2
    return call(last_kernel, [tile, tile], scratch, *args, far_in=13, far_out=2, copies=15)


def swap(low, high, axis):
    count = lax.axis_size(axis)
    odd = lax.axis_index(axis) % 2 == 1
    first = jnp.where(odd, low, high) if low is not high else low
    second = jnp.where(odd, high, low) if low is not high else low
    return (
        lax.ppermute(first, axis, [(i, i ^ 1) for i in range(count)]),
        lax.ppermute(second, axis, [(i, (i + 1 if i % 2 else i - 1) % count) for i in range(count)]),
    )


def apart(first, second, axis):
    odd = lax.axis_index(axis) % 2 == 1
    return jnp.where(odd, first, second), jnp.where(odd, second, first)


def gather(copies, axis):
    return lax.all_to_all(copies, axis, 0, 0, tiled=True)


def local(right_side, kappa, owners):
    pos = jnp.stack([lax.axis_index("gx"), lax.axis_index("gy")]).astype(jnp.int32)
    owned = jnp.repeat(jnp.repeat(owners.T, 2, 0), 8, 1).astype(F32)
    mid = jnp.stack([right_side, kappa])
    left, right = apart(*swap(mid[:, :HX], mid[:, TX - HX :], "gx"), "gx")
    wide = jnp.concatenate([left, mid, right], axis=1)
    low, high = (part.reshape(-1, 128) for part in (wide[:, :, :HX], wide[:, :, TY - HX :]))
    one, two, b0, k0, x0 = go_down(pos, wide, *swap(low, high, "gy"))
    by_x = swap(one, one, "gx")
    two = gather(two, "gx")
    left, right = apart(*by_x, "gx")
    rows = jnp.swapaxes(two, 0, 1).reshape(-1, 8, 128)
    wide = jnp.concatenate([left, one, right], axis=1)
    low, high = (
        jnp.concatenate([rows, part.reshape(-1, 8, 128)]) for part in (wide[:, :, :8], wide[:, :, 8:])
    )
    by_y = swap(low, high, "gy")
    near, three, k2 = go_mid(True, pos, two, *by_y, None)
    three = gather(three, "gy")
    b1n, send, send2, xbefore, source, k3, k1, x0n = go_turn(
        pos, owned, three, near, one, *by_x, *by_y, b0, k0, x0
    )

    by_x = (
        lax.ppermute(send, "gx", [(i, i ^ 1) for i in range(16)]),
        lax.ppermute(send2, "gx", [(i, (i + 1 if i % 2 else i - 1) % 16) for i in range(16)]),
    )
    left, right = apart(*by_x, "gx")
    wide = jnp.concatenate([left[:, :16], b1n, right[:, :16]])
    b1, x1, two = go_one(pos, b1n, *by_x, *swap(wide[:, :8], wide[:, 8:], "gy"), k1)
    two = gather(two, "gx")
    wide = jnp.concatenate([left[:, 16:], x0n, right[:, 16:]])
    low, high = (jnp.concatenate([two[:, 0], part]) for part in (wide[:, :8], wide[:, 24:]))
    by_y = swap(low, high, "gy")
    near, three = go_mid(False, pos, two, *by_y, k2)
    three = gather(three, "gy")
    field, residual = go_last(
        pos, owned, three, k3, near, b1, x1, k1, *by_x, *by_y, x0n, k0, source, xbefore, right_side
    )
    return field, residual


def solution(mesh):
    spec = P("gx", "gy", None)
    return jax.shard_map(
        local, mesh=mesh, in_specs=(spec, spec, P()), out_specs=(spec, spec), check_vma=False
    )
```

```python
import functools

import jax
import jax.numpy as jnp
from jax import lax
from jax.experimental import pallas as pl
from jax.experimental.pallas import tpu as pltpu
from jax.sharding import PartitionSpec as P

SIGMA = 0.02
F32 = jnp.float32
BF16 = jnp.bfloat16
TX, TY = 16, 32
HX = 10
HY = 12
PX, RY = TX + 2 * HX, TY + 2 * HY
CHUNK = 4
PARTS = 2
VMEM_BYTES = 56 * 1024 * 1024


def cheb_steps(degree, lower):
    centre = 0.5 * (2.0 + lower)
    half = 0.5 * (2.0 - lower)
    sharp = centre / half
    ratio = 1.0 / sharp
    steps = []
    for _ in range(degree - 1):
        nxt = 1.0 / (2.0 * sharp - ratio)
        steps.append((nxt * ratio, 2.0 * nxt / half))
        ratio = nxt
    return 1.0 / centre, steps


SMOOTH = cheb_steps(3, 0.3)
COARSE = cheb_steps(24, 0.05)


def lane_match(z, q, source, target):
    bits = z.bit_length() - 1
    cell = (lax.shift_right_logical(source, bits) + (128 // z) * q) & -2
    inner = lax.shift_right_logical(source & (z - 1), 1)
    return jnp.where(cell * (z // 4) + inner == target, 1.0, 0.0).astype(BF16)


def restrict_map(z, planes=(0, 4)):
    shape = ((planes[1] - planes[0]) * 128, 128)
    row = lax.broadcasted_iota(jnp.int32, shape, 0)
    return lane_match(z, planes[0] + lax.shift_right_logical(row, 7), row & 127, lanes(shape))


def prolong_map(z, planes=(0, 4)):
    shape = (128, (planes[1] - planes[0]) * 128)
    column = lanes(shape)
    target = lax.broadcasted_iota(jnp.int32, shape, 0)
    return lane_match(z, planes[0] + lax.shift_right_logical(column, 7), column & 127, target)


def prolong_one(z, q):
    shape = (128, 128)
    return lane_match(z, q, lanes(shape), lax.broadcasted_iota(jnp.int32, shape, 0))


def pair_dot(value, matrix):
    rows = value.shape[0]
    high = value.astype(BF16).astype(F32)
    rest = value - high
    mid = rest.astype(BF16).astype(F32)
    parts = jnp.concatenate([high, mid, rest - mid], axis=0).astype(BF16)
    out = jnp.dot(parts, matrix, preferred_element_type=F32)
    return out[:rows] + (out[rows : 2 * rows] + out[2 * rows :])


def lanes(shape):
    return lax.broadcasted_iota(jnp.int32, shape, len(shape) - 1)


def turn(value, shift, axis):
    return pltpu.roll(value, shift % value.shape[axis], axis)


def next_x(v, z):
    if z == 128:
        return jnp.concatenate([v[1:], v[:1]], axis=0)
    a = turn(v, -z, 2)
    b = jnp.concatenate([a[1:], a[:1]], axis=0)
    return jnp.where(lanes(v.shape) < 128 - z, a, b)


def prev_x(v, z):
    if z == 128:
        return jnp.concatenate([v[-1:], v[:-1]], axis=0)
    a = turn(v, z, 2)
    b = jnp.concatenate([a[-1:], a[:-1]], axis=0)
    return jnp.where(lanes(v.shape) >= z, a, b)


def faces_of(k, step, scale, low, high):
    own = (0.5 * scale) * k
    both = own + (0.5 * scale) * step
    if low is None:
        return both, None
    edge = jnp.where(low | high, own, 0.0)
    return jnp.where(high, 0.0, both), edge


def build(k, scale, z, inside=None, edge_x=(None, None), edge_y=(None, None)):
    shape = k.shape
    cell = lanes(shape) & (z - 1)
    wx, ex = faces_of(k, next_x(k, z), scale, *edge_x)
    wy, ey = faces_of(k, turn(k, -1, 1), scale, *edge_y)
    wz, ez = faces_of(k, turn(k, -1, 2), scale, cell == 0, cell == z - 1)
    s = ez + SIGMA * scale
    if ex is not None:
        s = s + ex
    if ey is not None:
        s = s + ey
    diagonal = s + wx + prev_x(wx, z) + wy + turn(wy, 1, 1) + wz + turn(wz, 1, 2)
    rd = 1.0 / diagonal
    if inside is not None:
        rd = jnp.where(inside, rd, 0.0)
    return wx, wy, wz, s, rd


def remain(v, b, level, z):
    wx, wy, wz, s, _ = level
    fx = wx * (next_x(v, z) - v)
    fy = wy * (turn(v, -1, 1) - v)
    fz = wz * (turn(v, -1, 2) - v)
    total = (fx - prev_x(fx, z)) + (fy - turn(fy, 1, 1)) + (fz - turn(fz, 1, 2))
    return (b - s * v) + total


def smooth(x, b, level, z):
    first, steps = SMOOTH
    rd = level[4]
    if x is None:
        d = (b * rd) * first
        x = d
    else:
        d = (remain(x, b, level, z) * rd) * first
        x = x + d
    for keep, gain in steps:
        d = keep * d + gain * (remain(x, b, level, z) * rd)
        x = x + d
    return x


def within(shape, first_x, first_y, z, size_x, size_y):
    plane = lax.broadcasted_iota(jnp.int32, shape, 0)
    cx = first_x + plane * (128 // z) + lax.shift_right_logical(lanes(shape), z.bit_length() - 1)
    cy = first_y + lax.broadcasted_iota(jnp.int32, shape, 1)
    return (cx >= 0) & (cx < size_x) & (cy >= 0) & (cy < size_y)


def pair_rows(ref, plane, start, count):
    return ref[plane, pl.ds(start, count, stride=2), :] + ref[plane, pl.ds(start + 1, count, stride=2), :]


def spread_rows(ref, plane, start, value):
    count = value.shape[0]
    ref[plane, pl.ds(start, count, stride=2), :] = value
    ref[plane, pl.ds(start + 1, count, stride=2), :] = value


def insider(rows, first_x, first_y):
    row = lax.broadcasted_iota(jnp.int32, (CHUNK, rows, 128), 1) + first_y
    row_in = (row >= 0) & (row < 512)
    plane = lax.broadcasted_iota(jnp.int32, (CHUNK, rows, 128), 0) + first_x
    return lambda p: row_in & (plane >= -p) & (plane < 256 - p)


def build_top(k_ref, wx, wy, wz, s, rd, low, high, inside_at, body):
    rows = k_ref.shape[1]
    shape = (CHUNK, rows, 128)
    lane = lanes(shape)

    def step(i, wxp):
        p = low + i * CHUNK
        k = k_ref[pl.ds(p, CHUNK)]
        kn = jnp.concatenate([k[1:], k_ref[pl.ds(jnp.minimum(p + CHUNK, k_ref.shape[0] - 1), 1)]], axis=0)
        own = 0.5 * k
        fx = 0.5 * kn + own
        fy = turn(own, -1, 1) + own
        fz = jnp.where(lane == 127, 0.0, turn(own, -1, 2) + own)
        sv = SIGMA + jnp.where((lane == 0) | (lane == 127), own, 0.0)
        fxp = jnp.concatenate([wxp, fx[:-1]], axis=0)
        diagonal = sv + (fx + fxp) + (fy + turn(fy, 1, 1)) + (fz + turn(fz, 1, 2))
        rdv = jnp.where(inside_at(p), 1.0 / diagonal, 0.0)
        at = pl.ds(p, CHUNK)
        wx[at], wy[at], wz[at], s[at], rd[at] = fx, fy, fz, sv, rdv
        body(p, rdv)
        return fx[-1:]

    assert (high - low) % CHUNK == 0
    lax.fori_loop(0, (high - low) // CHUNK, step, jnp.zeros((1, rows, 128), F32), unroll=True)


def sweep_top(x, wx, wy, wz, s, low, high, body):
    size = (high - low) // PARTS
    fx0 = wx[low - 1 : low] * (x[low : low + 1] - x[low - 1 : low])

    def step(i, fxp):
        p = low + i * size
        at = pl.ds(p, size)
        v = x[at]
        vn = jnp.concatenate([v[1:], x[pl.ds(p + size, 1)]], axis=0)
        fx = wx[at] * (vn - v)
        fy = wy[at] * (turn(v, -1, 1) - v)
        fz = wz[at] * (turn(v, -1, 2) - v)
        fxp = jnp.concatenate([fxp, fx[:-1]], axis=0)
        total = (fx - fxp) + (fy - turn(fy, 1, 1)) + (fz - turn(fz, 1, 2))
        body(p, at, v, s[at] * v - total)
        return fx[-1:]

    assert (high - low) % PARTS == 0
    lax.fori_loop(0, PARTS, step, fx0, unroll=True)


class Pick:
    def __init__(self, take_first, first, second):
        self.take_first, self.first, self.second = take_first, first, second

    def __getitem__(self, index):
        return jnp.where(self.take_first, self.first[index], self.second[index])


def sides(at, first, second):
    odd = (at & 1) == 1
    return Pick(odd, first, second), Pick(odd, second, first)


def fill_top(dst, number, wide, below, above):
    dst[:, 0:2, :] = jnp.zeros((PX, 2, 128), F32)
    dst[:, RY - 2 : RY, :] = jnp.zeros((PX, 2, 128), F32)
    dst[:, HY : HY + TY, :] = wide[number]
    for p in range(PX):
        part = slice(HX * (PX * number + p), HX * (PX * number + p + 1))
        dst[p, 2:HY, :] = below[part]
        dst[p, HY + TY : RY - 2, :] = above[part]


def down_kernel(pos, wide, by_y, by_y2, one, two, *refs):
    given, (bx, kx, x, wx, wy, wz, s, rd, d, rs, b1s, x1s, k1s, sems) = refs[:3], refs[3:]
    keeping = moves((bx, kx, x), given, sems)
    gx, gy = pos[0], pos[1]
    inside_at = insider(RY, gx * TX - HX, gy * TY - HY)
    below, above = sides(gy, by_y, by_y2)
    fill_top(bx, 0, wide, below, above)
    fill_top(kx, 1, wide, below, above)

    def clear(i, _):
        at = pl.ds(i * CHUNK, CHUNK)
        kx[at] = jnp.where(inside_at(i * CHUNK), kx[at], 0.0)
        return 0

    lax.fori_loop(0, PX // CHUNK, clear, 0, unroll=True)
    for move in keeping[:2]:
        move.start()
    start, steps = SMOOTH

    def begin(p, rdv):
        at = pl.ds(p, CHUNK)
        v = (bx[at] * rdv) * start
        d[at] = v
        x[at] = v

    build_top(kx, wx, wy, wz, s, rd, 0, PX, inside_at, begin)
    for keep, gain in steps:
        sweep_top(x, wx, wy, wz, s, 2, PX - 2, advance_top(keep, gain, bx, 0, rd, d, x))

    def residual(p, at, v, av):
        d[at] = bx[at] - av

    keeping[2].start()
    sweep_top(x, wx, wy, wz, s, 4, PX - 4, residual)

    def coarse(src):
        for c in range(16):
            rs[c] = src[2 + 2 * c] + src[3 + 2 * c]
        return pair_planes(rs, 8, 4, 24)

    for p in (2, 3, PX - 4, PX - 3):
        d[p] = jnp.zeros((RY, 128), F32)
    b1 = coarse(d)
    k1 = coarse(kx)
    level = build(k1, 0.25, 64, within(k1.shape, gx * 8 - 4, gy * 16 - 4, 64, 128, 256))
    x1 = smooth(None, b1, level, 64)
    b1s[...] = b1
    x1s[...] = x1
    k1s[...] = k1
    for number, src in enumerate((b1s, x1s, k1s)):
        one[number] = src[2:6, 4:20, :]
    b1s[...] = remain(x1, b1, level, 64)
    send_all(two, coarse_tile((b1s, k1s), 2, 4))
    for move in keeping:
        move.wait()


def moves(sources, targets, sems):
    return [pltpu.make_async_copy(a, b, sems.at[i]) for i, (a, b) in enumerate(zip(sources, targets))]


def pair_planes(rs, planes, start, rows):
    flat = [
        jnp.concatenate([pair_rows(rs, 2 * c, start, rows), pair_rows(rs, 2 * c + 1, start, rows)], axis=1)
        for c in range(planes)
    ]
    out = 0.125 * pair_dot(jnp.concatenate(flat, axis=0), restrict_map(128, (1, 3)))
    return out.reshape(planes, rows, 128)


def coarse_tile(sources, plane, row):
    flat = [
        jnp.concatenate([pair_rows(src, plane + q, row, 8) for q in range(4)], axis=1) for src in sources
    ]
    out = 0.125 * pair_dot(jnp.concatenate(flat, axis=0), restrict_map(64))
    return out.reshape(len(sources), 8, 128)


def send_all(out, value):
    for g in range(16):
        out[g] = value


def advance_top(keep, gain, b, shift_b, rd, d, x):
    def advance(p, at, v, av):
        dv = keep * d[at] + gain * ((b[pl.ds(p - shift_b, v.shape[0])] - av) * rd[at])
        d[at] = dv
        x[at] = v + dv

    return advance


def open_top(b, shift_b, rd, d, x):
    def advance(p, at, v, av):
        dv = ((b[pl.ds(p - shift_b, v.shape[0])] - av) * rd[at]) * SMOOTH[0]
        d[at] = dv
        x[at] = v + dv

    return advance


def call(kernel, outs, scratch, *args, far_in=0, far_out=0, copies=0, grant=VMEM_BYTES):
    near, far = pl.BlockSpec(memory_space=pltpu.VMEM), pl.BlockSpec(memory_space=pl.ANY)
    specs = [pl.BlockSpec(memory_space=pltpu.SMEM)] + [near] * (len(args) - 1 - far_in) + [far] * far_in
    return pl.pallas_call(
        kernel,
        out_shape=[jax.ShapeDtypeStruct(o, F32) for o in outs],
        in_specs=specs,
        out_specs=[near] * (len(outs) - far_out) + [far] * far_out,
        scratch_shapes=[pltpu.VMEM(o, F32) for o in scratch]
        + ([pltpu.SemaphoreType.DMA((copies,))] if copies else []),
        compiler_params=pltpu.CompilerParams(vmem_limit_bytes=grant),
        cost_estimate=pl.CostEstimate(flops=10**7, bytes_accessed=8 << 20, transcendentals=0),
    )(*args)


def go_down(*args):
    top = (PX, RY, 128)
    outs = [(3, 4, 16, 128), (16, 2, 8, 128)] + [top] * 3
    scratch = [top] * 9 + [(16, RY, 128)] + [(8, 24, 128)] * 3
    return call(down_kernel, outs, scratch, *args, far_out=3, copies=3)


def one_kernel(pos, mid, by_x, by_x2, by_y, by_y2, k1, bout, xout, two, res):
    gx, gy = pos[0], pos[1]
    left, right = sides(gx, by_x, by_x2)
    below, above = sides(gy, by_y, by_y2)
    head = (slice(None), slice(0, 16))
    fill_one(bout, left[head], mid[...], right[head], below[...], above[...])
    b = bout[...]
    inside = within(b.shape, gx * 8 - 8, gy * 16 - 8, 64, 128, 256)
    level = build(k1[...], 0.25, 64, inside)
    x = smooth(None, b, level, 64)
    xout[...] = x
    res[...] = remain(x, b, level, 64)
    send_all(two, coarse_tile((res,), 4, 8))


def fill_one(dst, left, tile, right, below, above):
    dst[0:4, 8:24, :] = left
    dst[4:8, 8:24, :] = tile
    dst[8:12, 8:24, :] = right
    dst[:, 0:8, :] = below
    dst[:, 24:32, :] = above


def go_one(*args):
    wide = (12, 32, 128)
    return call(one_kernel, [wide, wide, (16, 1, 8, 128)], [wide], *args)


def mid_kernel(first, pos, mid, by_y, by_y2, *refs):
    if first:
        near, three, k2 = refs[:3]
        scratch = refs[3:]
    else:
        k2, near, three = refs[:3]
        scratch = refs[3:]
    hold, rs, cs, edge = scratch
    gx, gy = pos[0], pos[1]
    below, above = sides(gy, by_y, by_y2)
    shape = (16, 24, 128)
    inside = within(shape, 0, gy * 8 - 8, 32, 64, 128)

    def rows(dst, number):
        part = slice(16 * number, 16 * number + 16)
        dst[:, 0:8, :] = below[part]
        dst[:, 8:16, :] = mid[:, number]
        dst[:, 16:24, :] = above[part]

    rows(rs, 0)
    b = rs[...]
    if first:
        rows(k2, 1)
        k2[...] = jnp.where(inside, k2[...], 0.0)
    k = k2[...]
    plane = lax.broadcasted_iota(jnp.int32, shape, 0)
    lane = lanes(shape)
    edge_x = ((plane == 0) & (lane < 32), (plane == 15) & (lane >= 96))
    level = build(k, 0.25**2, 32, inside, edge_x)
    x = smooth(None, b, level, 32)
    rs[...] = remain(x, b, level, 32)
    for number, value in enumerate((b, x, k)):
        hold[number] = value
    for i in range(5):
        at = gx - 2 + i
        ok = (at >= 0) & (at < 16)
        from_plane = jnp.clip(at, 0, 15)
        for number in range(3):
            near[number, i] = jnp.where(ok, hold[number, from_plane], 0.0)

    if first:
        for i in range(5):
            edge[0, i : i + 1, :] = near[1, i, 9:10, :]
            edge[1, i : i + 1, :] = near[1, i, 14:15, :]
        upper = lax.rem(gy + 1, 16)
        for g in range(16):
            three[g, 4] = jnp.where(upper == g, edge[0], edge[1])

    def coarse(src, out):
        flat = [
            jnp.concatenate([pair_rows(src, 4 * c + q, 4, 8) for q in range(4)], axis=1) for c in range(4)
        ]
        cs[...] = (0.125 * pair_dot(jnp.concatenate(flat, axis=0), restrict_map(32))).reshape(4, 8, 128)
        for c in range(4):
            part = cs[c, 2:6, :]
            for g in range(16):
                three[g, out + c // 2, 4 * (c % 2) : 4 * (c % 2) + 4, :] = part

    coarse(rs, 0)
    if first:
        coarse(k2, 2)


def go_mid(first, pos, mid, below, above, k2):
    outs = [(3, 5, 24, 128), (16, 5 if first else 2, 8, 128)]
    outs += [(16, 24, 128)] if first else []
    scratch = [(3, 16, 24, 128), (16, 24, 128), (4, 8, 128), (2, 8, 128)]
    args = (mid, below, above) + (() if first else (k2,))
    grant = VMEM_BYTES // 4
    return call(functools.partial(mid_kernel, first), outs, scratch, pos, *args, grant=grant)


def solve_last(b, k, owned):
    shape = k.shape
    scale = 0.25**4
    lane = lanes(shape)
    row = lax.broadcasted_iota(jnp.int32, shape, 0)
    moves = (
        (8, 1, lane < 8, True),
        (-8, 1, lane >= 120, True),
        (1, 0, row == 0, True),
        (-1, 0, row == 31, True),
        (1, 1, (lane & 7) == 0, False),
        (-1, 1, (lane & 7) == 7, False),
    )
    diagonal = jnp.full(shape, SIGMA * scale, F32)
    pulls = []
    for shift, axis, edge, masked in moves:
        weight = (0.5 * scale) * (k + jnp.where(edge, 0.0, turn(k, shift, axis)))
        diagonal = diagonal + weight
        keep = jnp.where(edge, 0.0, weight)
        if masked:
            keep = jnp.where(owned == turn(owned, shift, axis), keep, 0.0)
        pulls.append(keep)
    rd = 1.0 / diagonal
    pulls = [keep * rd for keep in pulls]
    g = b * rd
    first, steps = COARSE
    d = g * first
    x = d
    for keep, gain in steps:
        total = [pull * turn(x, move[0], move[1]) for pull, move in zip(pulls, moves)]
        near = (total[0] + total[1]) + (total[2] + total[3]) + (total[4] + total[5])
        d = keep * d + gain * ((g - x) + near)
        x = x + d
    return x


def fill_three(dst, gathered, first):
    for g in range(16):
        for c in range(4):
            part = gathered[g, first + c // 2, 4 * (c % 2) : 4 * (c % 2) + 4, :]
            dst[c, 4 * g : 4 * g + 4, :] = part


def solve_three(b_ref, k_ref, owned, s3):
    shape = (4, 64, 128)
    plane = lax.broadcasted_iota(jnp.int32, shape, 0)
    row = lax.broadcasted_iota(jnp.int32, shape, 1)
    lane = lanes(shape)
    edge_x = ((plane == 0) & (lane < 16), (plane == 3) & (lane >= 112))
    level = build(k_ref[...], 0.25**3, 16, None, edge_x, (row == 0, row == 63))
    b = b_ref[...]
    x = smooth(None, b, level, 16)
    s3[:, 8:72, :] = remain(x, b, level, 16)
    flat = [
        jnp.concatenate([pair_rows(src, q, row0, 32) for q in range(4)], axis=1) for src, row0 in ((s3, 8), (k_ref, 0))
    ]
    fine = 0.125 * pair_dot(jnp.concatenate(flat, axis=0), restrict_map(16))
    last = solve_last(fine[:32], fine[32:], owned[...])
    back = pair_dot(last, prolong_map(16))
    for q in range(4):
        spread_rows(s3, q, 8, back[:, 128 * q : 128 * q + 128])
    s3[:, 8:72, :] = smooth(x + s3[:, 8:72, :], b, level, 16)


def rise_two(gx, gy, near, x2, s3, e2, s2):
    pair = lax.shift_right_logical(gy + 1, 1)
    rows = pl.ds(pl.multiple_of(pair * 8, 8), 24)
    for i in range(5):
        at = jnp.clip(gx - 2 + i, 0, 15)
        spread_rows(e2, i, 0, pair_dot(s3[at // 4, rows, :], prolong_one(32, at % 4)))
    e = e2[:, pl.ds(pl.multiple_of((gy + 1 - 2 * pair) * 8, 8), 24), :]
    shape = (5, 24, 128)
    inside = within(shape, gx * 4 - 8, gy * 8 - 8, 32, 64, 128)
    level = build(near[2], 0.25**2, 32, inside)
    s2[...] = smooth(jnp.where(inside, x2 + e, 0.0), near[0], level, 32)


def rise_one(x1, b1, k1, inside, s2, s1):
    flat = jnp.concatenate([s2[i, 4:20, :] for i in range(1, 4)], axis=0)
    back = pair_dot(flat, prolong_map(64))
    for i in range(3):
        for q in range(4):
            spread_rows(s1, 4 * i + q, 0, back[16 * i : 16 * i + 16, 128 * q : 128 * q + 128])
    level = build(k1, 0.25, 64, inside)
    s1[...] = smooth(jnp.where(inside, x1 + s1[...], 0.0), b1, level, 64)


def spread_one(s1, low, high, e0):
    flat = jnp.concatenate([s1[i, 4:28, :] for i in range(low, high)], axis=0)
    back = pair_dot(flat, prolong_map(128, (1, 3)))
    for i in range(high - low):
        for q in range(2):
            part = back[24 * i : 24 * i + 24, 128 * q : 128 * q + 128]
            spread_rows(e0, 2 * (low - 2 + i) + q, 4, part)
    e0[:, 0:4, :] = jnp.zeros((16, 4, 128), F32)
    e0[:, RY - 4 : RY, :] = jnp.zeros((16, 4, 128), F32)


def add_top(x0, e0, x):
    def begin(p, rdv):
        c = (p - 2) // 2
        pair = (e0[pl.ds(c, 1)], e0[pl.ds(c + 1, 1)])
        correction = jnp.concatenate([pair[0], pair[0], pair[1], pair[1]], axis=0)
        at = pl.ds(p, CHUNK)
        x[at] = jnp.where(rdv > 0.0, x0[at] + correction, 0.0)

    return begin


def turn_kernel(
    pos, owned, three, *refs
):
    gx, gy = pos[0], pos[1]
    fars, (b1n, send, send2, *far_outs) = refs[:9], refs[9:17]
    b3, s3, e2, s2, x2s, b1s, s1, e0, d, x, rs, xout, rout, k3, k1, x0n = refs[17:33]
    tops, (wx, wy, wz, s, rd), sems = refs[33:42], refs[42:47], refs[47]
    near, one, by_x, by_x2, by_y, by_y2, b0, k0, x0 = tops
    left, right = sides(gx, by_x, by_x2)
    below, above = sides(gy, by_y, by_y2)
    part = pl.ds(32, 36)
    loads = moves(fars[:4] + (fars[4].at[part], fars[5].at[part]) + fars[6:], tops, sems)
    for move in loads:
        move.start()
    keeps = xkeep, rkeep, kkeep, k1keep, x0keep = [
        pltpu.make_async_copy(a, b, sems.at[9 + i])
        for i, (a, b) in enumerate(zip((xout, rout, k3, k1, x0n), far_outs))
    ]
    fill_three(b3, three, 0)
    fill_three(k3, three, 2)
    kkeep.start()
    solve_three(b3, k3, owned, s3)
    loads[0].wait()
    x2s[...] = near[1]
    lower, upper = lax.rem(gy + 15, 16), lax.rem(gy + 1, 16)
    for i in range(5):
        x2s[i, 1:2, :] = three[lower, 4, i : i + 1, :]
        x2s[i, 22:23, :] = three[upper, 4, i : i + 1, :]
    rise_two(gx, gy, near, x2s[...], s3, e2, s2)

    for move in loads[1:6]:
        move.wait()
    inside = within((12, 32, 128), gx * 8 - 8, gy * 16 - 8, 64, 128, 256)
    for number, dst in enumerate((b1s, s1, k1)):
        part = slice(12 * number, 12 * number + 12)
        fill_one(dst, left[number], one[number], right[number], below[part], above[part])
    k1[...] = jnp.where(inside, k1[...], 0.0)
    k1keep.start()
    rise_one(s1[...], b1s[...], k1[...], inside, s2, s1)

    spread_one(s1, 2, 10, e0)
    for move in loads[6:]:
        move.wait()
    inside_at = insider(RY, gx * TX - HX, gy * TY - HY)
    build_top(k0, wx, wy, wz, s, rd, 2, PX - 2, inside_at, add_top(x0, e0, x))
    start, steps = SMOOTH
    sweep_top(x, wx, wy, wz, s, 4, PX - 4, open_top(b0, 0, rd, d, x))
    for (keep, gain), edge in zip(steps, (4, 6)):
        sweep_top(x, wx, wy, wz, s, edge, PX - edge, advance_top(keep, gain, b0, 0, rd, d, x))

    def residual(p, at, v, av):
        rout[pl.ds(p - 6, v.shape[0])] = b0[at] - av

    sweep_top(x, wx, wy, wz, s, 6, PX - 6, residual)
    xout[...] = x[9 : PX - 9]
    xkeep.start()
    rkeep.start()

    def begin(i, _):
        at = pl.ds(6 + i * CHUNK, CHUNK)
        v = (rout[pl.ds(i * CHUNK, CHUNK)] * rd[at]) * start
        d[at] = v
        x[at] = v
        return 0

    lax.fori_loop(0, (PX - 12) // CHUNK, begin, 0, unroll=True)
    for keep, gain in steps:
        sweep_top(x, wx, wy, wz, s, 8, PX - 8, advance_top(keep, gain, rout, 6, rd, d, x))

    def again(p, at, v, av):
        d[at] = rout[pl.ds(p - 6, v.shape[0])] - av

    x0n[...] = x[HX : HX + TX, HY : HY + TY, :]
    x0keep.start()
    sweep_top(x, wx, wy, wz, s, HX, HX + TX, again)
    for c in range(8):
        rs[c] = d[HX + 2 * c] + d[HX + 1 + 2 * c]
    b1 = pair_planes(rs, 4, HY, 16)
    b1n[...] = b1
    odd = (gx & 1) == 1
    for side, of_odd, of_even in ((send, HX, HX + TX - 4), (send2, HX + TX - 4, HX)):
        side[:, 0:16, :] = b1
        side[:, 16:48, :] = x[pl.ds(jnp.where(odd, of_odd, of_even), 4), HY : HY + TY, :]
    for move in keeps:
        move.wait()


def go_turn(*args):
    top, wide, three, one = (PX, RY, 128), (12, 32, 128), (4, 64, 128), (3, 4, 16, 128)
    kept = [(TX + 2, RY, 128), (TX + 8, RY, 128), three, wide, (TX, TY, 128)]
    outs = [(4, 16, 128), (4, 48, 128), (4, 48, 128)] + kept
    scratch = [three, (4, 88, 128), (5, 48, 128), (5, 24, 128), (5, 24, 128), wide, wide, (16, RY, 128)]
    scratch += [top] * 2 + [(8, RY, 128)] + kept + [(3, 5, 24, 128)] + [one] * 3 + [(36, 8, 128)] * 2 + [top] * 8
    return call(turn_kernel, outs, scratch, *args, far_in=9, far_out=5, copies=14)


def last_kernel(
    pos, owned, three, k3, *refs
):
    gx, gy = pos[0], pos[1]
    fars, far_outs, (b3, s3, e2, s2, s1, e0, d, x) = refs[:13], refs[13:15], refs[15:23]
    tops, (wx, wy, wz, s, rd, xout, rout), sems = refs[23:36], refs[36:43], refs[43]
    near, b1, x1, k1, by_x, by_x2, by_y, by_y2, x0n, k0, r, xbefore, borig = tops
    left, right = sides(gx, by_x, by_x2)
    below, above = sides(gy, by_y, by_y2)
    part = pl.ds(16, 24)
    loads = moves(fars[:6] + (fars[6].at[part], fars[7].at[part]) + fars[8:], tops, sems)
    for move in loads:
        move.start()
    keeps = [
        pltpu.make_async_copy(a, b, sems.at[13 + i]) for i, (a, b) in enumerate(zip((xout, rout), far_outs))
    ]
    fill_three(b3, three, 0)
    solve_three(b3, k3, owned, s3)
    loads[0].wait()
    rise_two(gx, gy, near, near[1], s3, e2, s2)
    for move in loads[1:4]:
        move.wait()
    inside = within((12, 32, 128), gx * 8 - 8, gy * 16 - 8, 64, 128, 256)
    rise_one(x1[...], b1[...], k1[...], inside, s2, s1)

    spread_one(s1, 3, 9, e0)
    for move in loads[4:]:
        move.wait()
    low, high = HX - 4, HX + TX + 4
    x[low:HX, HY : HY + TY, :] = left[:, 16:48, :]
    x[HX : HX + TX, HY : HY + TY, :] = x0n[...]
    x[HX + TX : high, HY : HY + TY, :] = right[:, 16:48, :]
    x[low:high, HY - 8 : HY, :] = below[...]
    x[low:high, HY + TY : HY + TY + 8, :] = above[...]
    x[low:high, 0 : HY - 8, :] = jnp.zeros((high - low, HY - 8, 128), F32)
    x[low:high, RY - 4 : RY, :] = jnp.zeros((high - low, 4, 128), F32)
    inside_at = insider(RY, gx * TX - HX, gy * TY - HY)
    build_top(k0, wx, wy, wz, s, rd, low, high, inside_at, add_top(x, e0, x))
    sweep_top(x, wx, wy, wz, s, low, high, open_top(r, low, rd, d, x))
    for keep, gain in SMOOTH[1]:
        sweep_top(x, wx, wy, wz, s, 8, PX - 8, advance_top(keep, gain, r, low, rd, d, x))
    x[9 : PX - 9] = x[9 : PX - 9] + xbefore[...]

    def residual(p, at, v, av):
        d[at] = av

    xout[...] = x[HX : HX + TX, HY : HY + TY, :]
    keeps[0].start()
    sweep_top(x, wx, wy, wz, s, HX, HX + TX, residual)
    rout[...] = borig[...] - d[HX : HX + TX, HY : HY + TY, :]
    keeps[1].start()
    for move in keeps:
        move.wait()


def go_last(*args):
    top, wide, tile = (PX, RY, 128), (12, 32, 128), (TX, TY, 128)
    scratch = [(4, 64, 128), (4, 88, 128), (5, 48, 128), (5, 24, 128), wide, (16, RY, 128)] + [top] * 2
    scratch += [(3, 5, 24, 128)] + [wide] * 3 + [(4, 48, 128)] * 2 + [(24, 8, 128)] * 2
    scratch += [tile, top, (TX + 8, RY, 128), (TX + 2, RY, 128), tile] + [top] * 5 + [tile] * 2
    return call(last_kernel, [tile, tile], scratch, *args, far_in=13, far_out=2, copies=15)


def swap(low, high, axis):
    count = lax.axis_size(axis)
    odd = lax.axis_index(axis) % 2 == 1
    first = jnp.where(odd, low, high) if low is not high else low
    second = jnp.where(odd, high, low) if low is not high else low
    return (
        lax.ppermute(first, axis, [(i, i ^ 1) for i in range(count)]),
        lax.ppermute(second, axis, [(i, (i + 1 if i % 2 else i - 1) % count) for i in range(count)]),
    )


def apart(first, second, axis):
    odd = lax.axis_index(axis) % 2 == 1
    return jnp.where(odd, first, second), jnp.where(odd, second, first)


def gather(copies, axis):
    return lax.all_to_all(copies, axis, 0, 0, tiled=True)


def local(right_side, kappa, owners):
    pos = jnp.stack([lax.axis_index("gx"), lax.axis_index("gy")]).astype(jnp.int32)
    owned = jnp.repeat(jnp.repeat(owners.T, 2, 0), 8, 1).astype(F32)
    mid = jnp.stack([right_side, kappa])
    left, right = apart(*swap(mid[:, :HX], mid[:, TX - HX :], "gx"), "gx")
    wide = jnp.concatenate([left, mid, right], axis=1)
    low, high = (part.reshape(-1, 128) for part in (wide[:, :, :HX], wide[:, :, TY - HX :]))
    one, two, b0, k0, x0 = go_down(pos, wide, *swap(low, high, "gy"))
    by_x = swap(one, one, "gx")
    two = gather(two, "gx")
    left, right = apart(*by_x, "gx")
    rows = jnp.swapaxes(two, 0, 1).reshape(-1, 8, 128)
    wide = jnp.concatenate([left, one, right], axis=1)
    low, high = (
        jnp.concatenate([rows, part.reshape(-1, 8, 128)]) for part in (wide[:, :, :8], wide[:, :, 8:])
    )
    by_y = swap(low, high, "gy")
    near, three, k2 = go_mid(True, pos, two, *by_y, None)
    three = gather(three, "gy")
    b1n, send, send2, xbefore, source, k3, k1, x0n = go_turn(
        pos, owned, three, near, one, *by_x, *by_y, b0, k0, x0
    )

    by_x = (
        lax.ppermute(send, "gx", [(i, i ^ 1) for i in range(16)]),
        lax.ppermute(send2, "gx", [(i, (i + 1 if i % 2 else i - 1) % 16) for i in range(16)]),
    )
    left, right = apart(*by_x, "gx")
    wide = jnp.concatenate([left[:, :16], b1n, right[:, :16]])
    b1, x1, two = go_one(pos, b1n, *by_x, *swap(wide[:, :8], wide[:, 8:], "gy"), k1)
    two = gather(two, "gx")
    wide = jnp.concatenate([left[:, 16:], x0n, right[:, 16:]])
    low, high = (jnp.concatenate([two[:, 0], part]) for part in (wide[:, :8], wide[:, 24:]))
    by_y = swap(low, high, "gy")
    near, three = go_mid(False, pos, two, *by_y, k2)
    three = gather(three, "gy")
    field, residual = go_last(
        pos, owned, three, k3, near, b1, x1, k1, *by_x, *by_y, x0n, k0, source, xbefore, right_side
    )
    return field, residual


def solution(mesh):
    spec = P("gx", "gy", None)
    return jax.shard_map(
        local, mesh=mesh, in_specs=(spec, spec, P()), out_specs=(spec, spec), check_vma=False
    )
```
